32 devices in a mesh: seq: 4 (over y, x), wide: 8 (over z, core).
Axes of the slice: x: 2, y: 2, z: 4, core: 2. Of those that a mesh axis runs over, the one named last changes fastest.
Arguments:
- inputs: bfloat16 [8, 1024, 2048], P('seq', 'wide'), may hold values from -9 to 9
- lengths: int32 [8], P('seq'), may hold values from 256 to 1024, as said below
- norm_gain: bfloat16 [2048], P('wide'), may hold values from 0.5 to 1.5
- gelu_weight: bfloat16 [2048, 2560], P('wide'), may hold values from -0.125 to 0.125
- branch_weight: bfloat16 [2048, 2560], P('wide'), may hold values from -0.125 to 0.125
- forget_gates: bfloat16 [2560, 256], P('wide'), may hold values from -0.375 to 0.375
- admit_gates: bfloat16 [2560, 256], P('wide'), may hold values from -0.375 to 0.375
- forget_bias: bfloat16 [2560], P('wide'), may hold values from -4 to 4
- admit_bias: bfloat16 [2560], P('wide'), may hold values from -4 to 4
- decay_rate: bfloat16 [2560], P('wide'), may hold values from 3.6478043e-05 to 0.019897461
- conv_weight: bfloat16 [4, 2560], P(None, 'wide'), may hold values from -3 to 3
- conv_bias: bfloat16 [2560], P('wide'), may hold values from -3 to 3
- out_weight: bfloat16 [2560, 2048], P('wide'), may hold values from -0.5 to 0.5
- mlp_gain: bfloat16 [2048], P('wide'), may hold values from 0.5 to 1.5
- gate_weight: bfloat16 [2048, 6144], P('wide', 'seq'), may hold values from -0.125 to 0.125
- up_weight: bfloat16 [2048, 6144], P('wide', 'seq'), may hold values from -0.125 to 0.125
- down_weight: bfloat16 [6144, 2048], P('seq', 'wide'), may hold values from -0.15625 to 0.15625
- cotangent: bfloat16 [8, 1024, 2048], P('seq', 'wide'), may hold values from -6 to 6
Outputs:
- output: bfloat16 [8, 1024, 2048], P('seq', 'wide')
- inputs_grad: float32 [8, 1024, 2048], P('seq', 'wide')
- norm_gain_grad: float32 [2048], P('wide')
- gelu_weight_grad: float32 [2048, 2560], P('wide')
- branch_weight_grad: float32 [2048, 2560], P('wide')
- forget_gates_grad: float32 [2560, 256], P('wide')
- admit_gates_grad: float32 [2560, 256], P('wide')
- forget_bias_grad: float32 [2560], P('wide')
- admit_bias_grad: float32 [2560], P('wide')
- decay_rate_grad: float32 [2560], P('wide')
- conv_weight_grad: float32 [4, 2560], P(None, 'wide')
- conv_bias_grad: float32 [2560], P('wide')
- out_weight_grad: float32 [2560, 2048], P('wide')
- mlp_gain_grad: float32 [2048], P('wide')
- gate_weight_grad: float32 [2048, 6144], P('wide', 'seq')
- up_weight_grad: float32 [2048, 6144], P('wide', 'seq')
- down_weight_grad: float32 [6144, 2048], P('seq', 'wide')
- statistics: float32 [3], replicated
The draws below stay inside these ranges and needn't reach their ends.
Inputs may be any that keep to these rules, and one draw needn't show every extreme that they name: `lengths`: in each group of 2 consecutive sequences one, drawn from the seed, has all 1024 tokens valid.
All inputs are finite; a program needn't handle non-finite values.
Results may differ from the reference program's by a relative error of at most 0.011.
Values may be sent and summed in bfloat16 or wider, within the bound.
A program may use at most 320 MiB of HBM per device.

```python
import math
import jax
import jax.numpy as jnp
from jax import lax

D = 2048
R = 2560
NBLK = 10
BW = 256
CONV = 4
FF = 6144
SEQS = 2
B = 8
SEQ_LEN = 1024
N_SEQ = 4


def draw_inputs(key, part):
    key = jax.random.fold_in(key, 5)
    position = jnp.arange(SEQ_LEN, dtype=jnp.float32) / SEQ_LEN
    scale = 0.5 + position
    values = jax.random.truncated_normal(key, -6.0, 6.0, (B, SEQ_LEN, D), jnp.float32)
    return (values * scale[None, :, None]).astype(jnp.bfloat16)


def draw_lengths(key, part):
    key = jax.random.fold_in(key, 11)
    first, second = jax.random.split(key)
    values = jax.random.randint(first, (SEQS * N_SEQ,), SEQ_LEN // 4, SEQ_LEN + 1)
    chosen = jax.random.randint(second, (N_SEQ, 1), 0, SEQS)
    within = jnp.arange(SEQS)[None, :]
    full = (within == chosen).reshape(SEQS * N_SEQ)
    return jnp.where(full, SEQ_LEN, values).astype(jnp.int32)


def levels(stream_key, dims, cuts, low, largest):
    level, own = 1.0, jax.random.fold_in(stream_key, 6)
    for axis_at, shards_of in cuts:
        steps = jnp.exp(jax.random.uniform(jax.random.fold_in(own, axis_at), (shards_of,), jnp.float32, low / len(cuts), largest / len(cuts)))
        level = level * jnp.repeat(steps, dims[axis_at] // shards_of).reshape([-1 if axis == axis_at else 1 for axis in range(len(dims))])
    return level


def centred(rng, dims, deviation, most, pieces=(), kind=jnp.bfloat16):
    array = jax.random.normal(rng, dims, jnp.float32) * deviation
    if len(pieces) > 0:
        array = levels(rng, dims, pieces, -0.22, 0.18) * array
    return jnp.clip(array, min=-most, max=most).astype(kind)


def setup_inputs(seed: int = 0) -> dict:
    keys = jax.random.split(jax.random.key(seed), 19)
    inputs = draw_inputs(jax.random.fold_in(keys[18], 71), 0)
    lengths = draw_lengths(jax.random.fold_in(keys[18], 71), 0)
    norm_gain = jnp.clip(1.0 + 0.1 * jax.random.normal(keys[2], (D,), jnp.float32), 0.5, 1.5).astype(jnp.bfloat16)
    gelu_weight = centred(keys[3], (D, R), D ** -0.5, 0.125, ((0, 8),))
    branch_weight = centred(keys[4], (D, R), D ** -0.5, 0.125, ((0, 8),))
    forget_gates = centred(keys[5], (R, BW), BW ** -0.5, 0.375, ((0, 8),))
    admit_gates = centred(keys[6], (R, BW), BW ** -0.5, 0.375, ((0, 8),))
    forget_bias = centred(keys[7], (R,), 1.0, 4.0, ((0, 8),))
    admit_bias = centred(keys[8], (R,), 1.0, 4.0, ((0, 8),))
    decay_rate = jnp.clip(jnp.exp(math.log(0.019897461) - 6.3016369 * jax.random.uniform(keys[9], (R,), jnp.float32) ** levels(keys[9], (R,), ((0, 8),), -0.2, 0.2)), 3.647804260253906e-05, 0.019897461).astype(jnp.bfloat16)
    conv_weight = centred(keys[10], (CONV, R), CONV ** -0.5, 3.0, ((1, 8),))
    conv_bias = centred(keys[11], (R,), 0.5, 3.0, ((0, 8),))
    out_weight = centred(keys[12], (R, D), (R // 16) ** -0.5, 0.5, ((0, 8),))
    mlp_gain = jnp.clip(1.0 + 0.1 * jax.random.normal(keys[13], (D,), jnp.float32), 0.5, 1.5).astype(jnp.bfloat16)
    gate_weight = centred(keys[14], (D, FF), D ** -0.5, 0.125, ((0, 8), (1, 4)))
    up_weight = centred(keys[15], (D, FF), D ** -0.5, 0.125, ((0, 8), (1, 4)))
    down_weight = centred(keys[16], (FF, D), (FF // 4) ** -0.5, 0.15625, ((0, 4), (1, 8)))
    cotangent = centred(keys[17], (B, SEQ_LEN, D), 1.0, 6.0, ((0, 4), (1, 8)))
    return {"inputs": inputs, "lengths": lengths, "norm_gain": norm_gain, "gelu_weight": gelu_weight, "branch_weight": branch_weight, "forget_gates": forget_gates, "admit_gates": admit_gates, "forget_bias": forget_bias, "admit_bias": admit_bias, "decay_rate": decay_rate, "conv_weight": conv_weight, "conv_bias": conv_bias, "out_weight": out_weight, "mlp_gain": mlp_gain, "gate_weight": gate_weight, "up_weight": up_weight, "down_weight": down_weight, "cotangent": cotangent}


@jax.custom_vjp
def low(v):
    return lax.optimization_barrier(v.astype(jnp.bfloat16)).astype(jnp.float32)

@jax.custom_vjp
def low_back(v):
    return v

def low_keep(v):
    return (low(v), None)

def low_pass(kept, grad):
    return (grad,)

def back_keep(v):
    return (v, None)

def back_low(kept, grad):
    return (low(grad),)
low.defvjp(low_keep, low_pass)
low_back.defvjp(back_keep, back_low)

def rms_norm(values, gain):
    return values * lax.rsqrt(lax.optimization_barrier(jnp.mean(values * values, axis=-1, keepdims=True)) + 1e-06) * gain

def product(left, right):
    return jnp.dot(left, right, precision=lax.Precision.HIGHEST, preferred_element_type=jnp.float32)

def block_gates(values, weight, bias):
    steps = values.shape[0]
    blocks = values.reshape(steps, NBLK, BW)
    mixed = jnp.einsum('tki,kij->tkj', blocks, weight.reshape(NBLK, BW, BW), precision=lax.Precision.HIGHEST)
    return mixed.reshape(steps, R) + bias

def combine_pairs(earlier, later):
    return (earlier[0] * later[0], later[0] * earlier[1] + later[1])

def sequence_block(sequence, length, params):
    norm_gain, gelu_weight, branch_weight, forget_gates, admit_gates, forget_bias, admit_bias, decay_rate, conv_weight, conv_bias, out_weight, mlp_gain, gate_weight, up_weight, down_weight = params
    steps = sequence.shape[0]
    normed = low(rms_norm(sequence, norm_gain))
    branch_y = low_back(product(normed, gelu_weight))
    branch_x = low(low_back(product(normed, branch_weight)))
    conv_in = low_back(branch_x)
    forget_logits = low_back(low(block_gates(branch_x, forget_gates, forget_bias)))
    admit_logits = low_back(low(block_gates(branch_x, admit_gates, admit_bias)))
    padded = jnp.concatenate([jnp.zeros((CONV - 1, R), jnp.float32), conv_in], axis=0)
    conv_out = conv_bias
    for offset in range(CONV):
        conv_out = conv_out + conv_weight[offset] * padded[CONV - 1 - offset:CONV - 1 - offset + steps]
    log_rate = -8.0 * decay_rate * (0.1 + 0.9 * jax.nn.sigmoid(forget_logits))
    drive = jnp.sqrt(-jnp.expm1(2.0 * log_rate)) * jax.nn.sigmoid(admit_logits) * conv_out
    unused_products, carried = lax.associative_scan(combine_pairs, (jnp.exp(log_rate), drive), axis=0)
    state = low_back(low(carried))
    mixed = low(state * jax.nn.gelu(branch_y))
    temporal = low_back(product(mixed, out_weight))
    stream = sequence + temporal
    normed_two = low(rms_norm(stream, mlp_gain))
    gate = low_back(product(normed_two, gate_weight))
    up_values = low_back(product(normed_two, up_weight))
    hidden = low(jax.nn.gelu(gate) * up_values)
    feed = low_back(product(hidden, down_weight))
    result = stream + feed
    valid = (jnp.arange(steps) < length).astype(jnp.float32)[:, None]
    sums = jnp.stack([jnp.sum(valid * result * result), jnp.sum(valid * temporal * temporal), jnp.sum(valid * feed * feed)])
    return (result, sums)

def reference(inputs, lengths, norm_gain, gelu_weight, branch_weight, forget_gates, admit_gates, forget_bias, admit_bias, decay_rate, conv_weight, conv_bias, out_weight, mlp_gain, gate_weight, up_weight, down_weight, cotangent):
    params = tuple((p.astype(jnp.float32) for p in (norm_gain, gelu_weight, branch_weight, forget_gates, admit_gates, forget_bias, admit_bias, decay_rate, conv_weight, conv_bias, out_weight, mlp_gain, gate_weight, up_weight, down_weight)))

    def forward(values, weights):

        def single(item):
            sequence, length = item
            return jax.checkpoint(sequence_block)(sequence, length, weights)
        return lax.map(single, (values, lengths))
    result, pullback, sums = jax.vjp(forward, inputs.astype(jnp.float32), params, has_aux=True)
    inputs_grad, grads = pullback(cotangent.astype(jnp.float32))
    totals = lax.optimization_barrier(jnp.sum(sums, axis=0))
    count = jnp.sum(lengths.astype(jnp.float32))
    statistics = jnp.sqrt(totals / (count * D))
    return (result.astype(jnp.bfloat16), inputs_grad, grads[0], grads[1], grads[2], grads[3], grads[4], grads[5], grads[6], grads[7], grads[8], grads[9], grads[10], grads[11], grads[12], grads[13], grads[14], statistics)
```

```python
import jax
import jax.numpy as jnp
from jax import lax
from jax.sharding import PartitionSpec as P

BW = 256
CONV = 4
HALO = 8
BF = jnp.bfloat16
F32 = jnp.float32


def dot(left, right):
    return jnp.dot(left, right, preferred_element_type=F32)


def contract_last(left, right):
    return lax.dot_general(left, right, (((1,), (1,)), ((), ())), preferred_element_type=F32)


def contract_rows(left, right):
    return lax.dot_general(left, right, (((0,), (0,)), ((), ())), preferred_element_type=F32)


def swap(values, mask):
    return lax.ppermute(values, "seq", [(i, i ^ mask) for i in range(lax.axis_size("seq"))])


def gather_seq(values):
    half = values.shape[0] // 2
    near = swap(values, 1)
    side = swap(values, 2)
    first = swap(near[:half], 2)
    second = swap(side[half:], 1)
    return [values, near, side, jnp.concatenate([first, second], axis=0)]


def reduce_seq(block_of):
    far = block_of(3).astype(BF)
    half = far.shape[0] // 2
    to_side = swap(far[:half], 1)
    to_near = swap(far[half:], 2)
    near = block_of(1)
    near = jnp.concatenate([near[:half], near[half:] + to_near.astype(F32)], axis=0).astype(BF)
    near = swap(near, 1)
    side = block_of(2)
    side = jnp.concatenate([side[:half] + to_side.astype(F32), side[half:]], axis=0).astype(BF)
    side = swap(side, 2)
    return block_of(0) + near.astype(F32) + side.astype(F32)


def inverse_rms(values):
    return lax.rsqrt(jnp.mean(values * values, axis=-1, keepdims=True) + 1e-06)


def rms_norm(values, gain):
    return values * inverse_rms(values) * gain


def rms_back(values, gain, grad):
    inv = inverse_rms(values)
    inner = jnp.mean(values * gain * grad, axis=-1, keepdims=True)
    return inv * gain * grad - values * (inv * inv * inv) * inner


def gelu_grad_of(values):
    c = 0.7978845608028654
    sq = values * values
    t = jnp.tanh(c * values * (1.0 + 0.044715 * sq))
    return 0.5 * (1.0 + t) + 0.5 * values * (1.0 - t * t) * c * (1.0 + 3.0 * 0.044715 * sq)


def body(
    inputs,
    lengths,
    norm_gain,
    gelu_weight,
    branch_weight,
    forget_gates,
    admit_gates,
    forget_bias,
    admit_bias,
    decay_rate,
    conv_weight,
    conv_bias,
    out_weight,
    mlp_gain,
    gate_weight,
    up_weight,
    down_weight,
    cotangent,
):
    groups = lax.axis_size("seq")
    wide = lax.axis_size("wide")
    s = lax.axis_index("seq")
    w = lax.axis_index("wide")
    seqs, tokens, width = inputs.shape
    rows = seqs * tokens
    total = groups * rows
    all_seqs = groups * seqs
    channels = gelu_weight.shape[1]
    share = channels // groups
    window = (share + BW - 1) // BW * BW
    blocks = window // BW

    def base_of(index):
        return jnp.minimum(index * share // BW * BW, channels - window)

    base = base_of(s)
    off = s * share - base
    quarter = width // groups
    gate_cols = 2 * BW // groups

    small = jnp.concatenate(
        [norm_gain, mlp_gain, forget_bias, admit_bias, decay_rate, conv_bias, conv_weight.reshape(-1)]
    )
    small = lax.all_gather(small, "wide").astype(F32)
    dw, rw = width // wide, channels // wide
    gain_one = small[:, :dw].reshape(1, width)
    gain_two = small[:, dw : 2 * dw].reshape(1, width)
    per_channel = small[:, 2 * dw :].reshape(wide, 8, rw).transpose(1, 0, 2).reshape(8, channels)
    per_channel = lax.dynamic_slice_in_dim(per_channel, s * share, share, 1)
    forget_shift, admit_shift, decay, taps_bias = (per_channel[i : i + 1] for i in range(4))
    taps = per_channel[4:8]

    branch_cols = lax.all_gather(
        lax.dynamic_slice_in_dim(branch_weight, base, window, 1), "wide", axis=0, tiled=True
    )
    gate_quarter = lax.all_gather(
        lax.dynamic_slice_in_dim(
            jnp.concatenate([forget_gates, admit_gates], axis=1), s * gate_cols, gate_cols, 1
        ),
        "wide",
        axis=0,
        tiled=True,
    )
    gelu_cols = lax.all_gather(
        lax.dynamic_slice_in_dim(gelu_weight, s * share, share, 1), "wide", axis=0, tiled=True
    )
    out_quarter = lax.all_gather(
        lax.dynamic_slice_in_dim(out_weight, s * quarter, quarter, 1), "wide", axis=0, tiled=True
    )
    mlp_full = lax.all_gather(
        jnp.concatenate([gate_weight, up_weight], axis=1), "wide", axis=0, tiled=True
    )
    down_full = lax.all_gather(down_weight, "wide", axis=1, tiled=True)
    hidden_units = gate_weight.shape[1]

    gates = jnp.zeros((window, groups * gate_cols), BF)
    out_rows = jnp.zeros((share, width), BF)
    for k in range(groups):
        other = s ^ k
        part = lax.dynamic_slice_in_dim(gate_quarter, base_of(other), window, 0)
        part = swap(part, k) if k else part
        gates = lax.dynamic_update_slice_in_dim(gates, part, other * gate_cols, 1)
    for k in range(groups):
        other = s ^ k
        part = lax.dynamic_slice_in_dim(out_quarter, other * share, share, 0)
        part = swap(part, k) if k else part
        out_rows = lax.dynamic_update_slice_in_dim(out_rows, part, other * quarter, 1)
    forget_blocks = gates[:, :BW].reshape(blocks, BW, BW)
    admit_blocks = gates[:, BW:].reshape(blocks, BW, BW)

    flat_low = inputs.reshape(rows, width)
    upstream = cotangent.reshape(rows, width)
    edge = lax.ppermute(
        inputs[:, tokens - HALO :, :].reshape(seqs * HALO, width),
        "wide",
        [(i, i + 1) for i in range(wide - 1)],
    )
    token_blocks = gather_seq(jnp.concatenate([flat_low, edge], axis=0))
    all_low = jnp.concatenate(
        [b[:rows] for b in token_blocks] + [b[rows:] for b in token_blocks], axis=0
    )
    upstream_all = jnp.concatenate(gather_seq(upstream), axis=0)
    normed_ext = rms_norm(all_low.astype(F32), gain_one).astype(BF)
    normed_all = normed_ext[:total]

    x_ext = dot(normed_ext, branch_cols).astype(BF)
    x_win = x_ext[:total]
    x_blocks = x_win.reshape(total, blocks, BW)

    def logits_of(weight, shift):
        mixed = jnp.einsum("tki,kij->tkj", x_blocks, weight, preferred_element_type=F32)
        mixed = lax.dynamic_slice_in_dim(mixed.reshape(total, window), off, share, 1)
        return (mixed + shift).astype(BF).reshape(all_seqs, tokens, share)

    forget_sig = jax.nn.sigmoid(logits_of(forget_blocks, forget_shift).astype(F32))
    admit_sig = jax.nn.sigmoid(logits_of(admit_blocks, admit_shift).astype(F32))
    x_own = lax.dynamic_slice_in_dim(x_ext, off, share, 1)
    before = x_own[total:].reshape(all_seqs, HALO, share)[:, HALO - (CONV - 1) :]
    padded = jnp.concatenate([before, x_own[:total].reshape(all_seqs, tokens, share)], axis=1)

    def shifted(k):
        return padded[:, CONV - 1 - k : CONV - 1 - k + tokens, :].astype(F32)

    conv_out = taps_bias
    for k in range(CONV):
        conv_out = conv_out + taps[k] * shifted(k)
    span = 0.1 + 0.9 * forget_sig
    log_rate = -8.0 * decay * span
    rate = jnp.exp(log_rate)
    scale = jnp.sqrt(-jnp.expm1(2.0 * log_rate))
    drive = scale * admit_sig * conv_out
    within = jnp.cumsum(log_rate, axis=1)
    grow = jnp.exp(within)
    inner = grow * jnp.cumsum(jnp.exp(-within) * drive, axis=1)
    ends = lax.all_gather(jnp.stack([grow[:, -1], inner[:, -1]]), "wide")
    carry = jnp.zeros((all_seqs, share), F32)
    for j in range(wide - 1):
        carry = jnp.where(j < w, ends[j, 0] * carry + ends[j, 1], carry)
    carried = inner + grow * carry[:, None, :]
    carried_before = jnp.concatenate([carry[:, None, :], carried[:, :-1]], axis=1)
    state = carried.astype(BF).astype(F32).reshape(total, share)

    branch_y = dot(normed_all, gelu_cols)
    gelu_y = jax.nn.gelu(branch_y)
    mixed_low = (state * gelu_y).astype(BF)
    temporal = reduce_seq(lambda k: dot(mixed_low[k * rows : (k + 1) * rows], out_rows))
    flat = flat_low.astype(F32)
    stream = flat + temporal
    normed_two = rms_norm(stream, gain_two).astype(BF)
    normed_two_all = jnp.concatenate(gather_seq(normed_two), axis=0)

    gate_up = dot(normed_two_all, mlp_full)
    gate, up_values = gate_up[:, :hidden_units], gate_up[:, hidden_units:]
    gelu_gate = jax.nn.gelu(gate)
    hidden_low = (gelu_gate * up_values).astype(BF)
    hidden_grad = contract_last(upstream_all, down_full)
    gate_rows = (hidden_grad * up_values * gelu_grad_of(gate)).astype(BF)
    up_rows = (hidden_grad * gelu_gate).astype(BF)
    mlp_rows = jnp.concatenate([gate_rows, up_rows], axis=1)
    normed_two_grad = reduce_seq(
        lambda k: contract_last(mlp_rows[k * rows : (k + 1) * rows], mlp_full)
    )
    mlp_grad = lax.psum_scatter(
        contract_rows(normed_two_all, mlp_rows).astype(BF), "wide", scatter_dimension=0, tiled=True
    ).astype(F32)
    down_grad = lax.psum_scatter(
        contract_rows(hidden_low, upstream_all).astype(BF), "wide", scatter_dimension=1, tiled=True
    ).astype(F32)
    feed = reduce_seq(lambda k: dot(hidden_low[k * rows : (k + 1) * rows], down_full))
    result = stream + feed
    output = result.astype(BF).reshape(seqs, tokens, width)
    position = w * tokens + jnp.arange(tokens, dtype=jnp.int32)
    valid = (position[None, :] < lengths[:, None]).astype(F32).reshape(rows, 1)
    partial_sums = jnp.stack(
        [
            jnp.sum(valid * result * result),
            jnp.sum(valid * temporal * temporal),
            jnp.sum(valid * feed * feed),
            jnp.sum(valid),
        ]
    )

    gain_two_grad = jnp.sum(normed_two_grad * stream * inverse_rms(stream), axis=0)
    stream_grad = upstream.astype(F32) + rms_back(stream, gain_two, normed_two_grad)
    stream_low_all = jnp.concatenate(gather_seq(stream_grad.astype(BF)), axis=0)

    mixed_grad = contract_last(stream_low_all, out_rows)
    state_grad = (mixed_grad * gelu_y).astype(BF).astype(F32).reshape(all_seqs, tokens, share)
    y_rows = (mixed_grad * state * gelu_grad_of(branch_y)).astype(BF)
    gathered_back = lax.cumsum(grow * state_grad, axis=1, reverse=True)
    adjoint_local = jnp.exp(-within) * gathered_back
    gelu_part = lax.psum_scatter(
        contract_rows(normed_all, y_rows).astype(BF), "wide", scatter_dimension=0, tiled=True
    )
    heads = lax.all_gather(gathered_back[:, 0], "wide")
    reach = jnp.exp(within[:, -1:] - within)
    later = jnp.zeros((all_seqs, share), F32)
    for j in range(wide - 1, 0, -1):
        later = jnp.where(j > w, ends[j, 0] * later + heads[j], later)
    adjoint = adjoint_local + reach * later[:, None, :]
    drive_part = scale * admit_sig
    conv_out_grad = adjoint * drive_part
    after = lax.ppermute(
        conv_out_grad[:, : CONV - 1], "wide", [(i + 1, i) for i in range(wide - 1)]
    )
    grad_padded = jnp.concatenate([conv_out_grad, after], axis=1)
    conv_rows = sum(taps[k] * grad_padded[:, k : k + tokens] for k in range(CONV)).astype(BF)
    log_rate_grad = adjoint * (
        rate * carried_before - rate * rate / scale * admit_sig * conv_out
    )
    forget_rows = (
        log_rate_grad * (-7.2) * decay * forget_sig * (1.0 - forget_sig)
    ).astype(BF)
    admit_rows = (adjoint * scale * conv_out * admit_sig * (1.0 - admit_sig)).astype(BF)
    channel_grads = jnp.stack(
        [
            jnp.sum(forget_rows.astype(F32), axis=(0, 1)),
            jnp.sum(admit_rows.astype(F32), axis=(0, 1)),
            jnp.sum(log_rate_grad * (-8.0) * span, axis=(0, 1)),
            jnp.sum(conv_out_grad, axis=(0, 1)),
        ]
        + [jnp.sum(conv_out_grad * shifted(k), axis=(0, 1)) for k in range(CONV)]
    )

    def in_window(values):
        return lax.dynamic_update_slice_in_dim(
            jnp.zeros((total, window), BF), values.reshape(total, share), off, 1
        )

    forget_win = in_window(forget_rows).reshape(total, blocks, BW)
    admit_win = in_window(admit_rows).reshape(total, blocks, BW)
    branch_back = jnp.einsum(
        "tkj,kij->tki", forget_win, forget_blocks, preferred_element_type=F32
    ) + jnp.einsum("tkj,kij->tki", admit_win, admit_blocks, preferred_element_type=F32)
    branch_rows = (
        branch_back.reshape(total, window) + in_window(conv_rows).astype(F32)
    ).astype(BF)
    normed_grad = reduce_seq(
        lambda k: contract_last(branch_rows[k * rows : (k + 1) * rows], branch_cols)
        + contract_last(y_rows[k * rows : (k + 1) * rows], gelu_cols)
    )
    branch_part = lax.psum_scatter(
        contract_rows(normed_all, branch_rows).astype(BF), "wide", scatter_dimension=0, tiled=True
    )
    gate_grads = jnp.concatenate(
        [
            jnp.einsum("tki,tkj->kij", x_blocks, rows_win, preferred_element_type=F32).reshape(
                window, BW
            )
            for rows_win in (forget_win, admit_win)
        ],
        axis=1,
    )
    out_grad = contract_rows(mixed_low, stream_low_all).astype(BF)

    gate_cols_grad = jnp.zeros((channels, gate_cols), F32)
    out_cols_grad = jnp.zeros((channels, quarter), BF)
    for k in range(groups):
        other = s ^ k
        part = lax.dynamic_slice_in_dim(gate_grads, other * gate_cols, gate_cols, 1)
        part = swap(part.astype(BF), k).astype(F32) if k else part
        start = base_of(other)
        part = part + lax.dynamic_slice_in_dim(gate_cols_grad, start, window, 0)
        gate_cols_grad = lax.dynamic_update_slice_in_dim(gate_cols_grad, part, start, 0)
        part = lax.dynamic_slice_in_dim(out_grad, other * quarter, quarter, 1)
        part = swap(part, k) if k else part
        out_cols_grad = lax.dynamic_update_slice_in_dim(out_cols_grad, part, other * share, 0)
    late_part = lax.psum_scatter(
        jnp.concatenate([out_cols_grad, gate_cols_grad.astype(BF)], axis=1),
        "wide",
        scatter_dimension=0,
        tiled=True,
    )
    out_whole = jnp.zeros((channels // wide, width), F32)
    gates_whole = jnp.zeros((channels // wide, 2 * BW), F32)
    gelu_whole = jnp.zeros((width // wide, channels), F32)
    branch_whole = jnp.zeros((width // wide, channels), F32)
    for k in range(groups):
        other = s ^ k
        part = swap(late_part, k) if k else late_part
        out_whole = lax.dynamic_update_slice_in_dim(
            out_whole, part[:, :quarter].astype(F32), other * quarter, 1
        )
        gates_whole = lax.dynamic_update_slice_in_dim(
            gates_whole, part[:, quarter:].astype(F32), other * gate_cols, 1
        )
        part = swap(gelu_part, k) if k else gelu_part
        gelu_whole = lax.dynamic_update_slice_in_dim(
            gelu_whole, part.astype(F32), other * share, 1
        )
        part = (swap(branch_part, k) if k else branch_part).astype(F32)
        start = base_of(other)
        part = part + lax.dynamic_slice_in_dim(branch_whole, start, window, 1)
        branch_whole = lax.dynamic_update_slice_in_dim(branch_whole, part, start, 1)

    gain_one_grad = jnp.sum(normed_grad * flat * inverse_rms(flat), axis=0)
    inputs_grad = (stream_grad + rms_back(flat, gain_one, normed_grad)).reshape(
        seqs, tokens, width
    )
    channel_all = lax.dynamic_update_slice_in_dim(
        jnp.zeros((8, channels), F32), channel_grads, s * share, 1
    )
    sums = lax.psum(
        jnp.concatenate(
            [channel_all.reshape(-1), gain_one_grad, gain_two_grad, partial_sums]
        ),
        ("seq", "wide"),
    )
    channel_sums = lax.dynamic_slice_in_dim(
        sums[: 8 * channels].reshape(8, channels), w * rw, rw, 1
    )
    gain_sums = lax.dynamic_slice_in_dim(
        sums[8 * channels : 8 * channels + 2 * width].reshape(2, width), w * dw, dw, 1
    )
    totals = sums[8 * channels + 2 * width :]
    statistics = jnp.sqrt(totals[0:3] / (totals[3] * width))
    return (
        output,
        inputs_grad,
        gain_sums[0],
        gelu_whole,
        branch_whole,
        gates_whole[:, :BW],
        gates_whole[:, BW:],
        channel_sums[0],
        channel_sums[1],
        channel_sums[2],
        channel_sums[4:8],
        channel_sums[3],
        out_whole,
        gain_sums[1],
        mlp_grad[:, :hidden_units],
        mlp_grad[:, hidden_units:],
        down_grad,
        statistics,
    )


def solution(mesh):
    in_specs = (
        P("seq", "wide", None),
        P("seq"),
        P("wide"),
        P("wide", None),
        P("wide", None),
        P("wide", None),
        P("wide", None),
        P("wide"),
        P("wide"),
        P("wide"),
        P(None, "wide"),
        P("wide"),
        P("wide", None),
        P("wide"),
        P("wide", "seq"),
        P("wide", "seq"),
        P("seq", "wide"),
        P("seq", "wide", None),
    )
    out_specs = (
        P("seq", "wide", None),
        P("seq", "wide", None),
        P("wide"),
        P("wide", None),
        P("wide", None),
        P("wide", None),
        P("wide", None),
        P("wide"),
        P("wide"),
        P("wide"),
        P(None, "wide"),
        P("wide"),
        P("wide", None),
        P("wide"),
        P("wide", "seq"),
        P("wide", "seq"),
        P("seq", "wide"),
        P(),
    )
    return jax.shard_map(body, mesh=mesh, in_specs=in_specs, out_specs=out_specs, check_vma=False)
```

```python
import jax
import jax.numpy as jnp
from jax import lax
from jax.experimental import pallas as pl
from jax.experimental.pallas import tpu as pltpu
from jax.sharding import PartitionSpec as P

BW = 256
CONV = 4
HALO = 8
BF = jnp.bfloat16
F32 = jnp.float32
LANES = 128
ROWS16 = 16
MESH = pl.DeviceIdType.MESH


def dot(left, right):
    return jnp.dot(left, right, preferred_element_type=F32)


def contract_last(left, right):
    return lax.dot_general(left, right, (((1,), (1,)), ((), ())), preferred_element_type=F32)


def contract_rows(left, right):
    return lax.dot_general(left, right, (((0,), (0,)), ((), ())), preferred_element_type=F32)


def swap(values, mask):
    return lax.ppermute(values, "seq", [(i, i ^ mask) for i in range(lax.axis_size("seq"))])


def gather_seq(values):
    half = values.shape[0] // 2
    near = swap(values, 1)
    side = swap(values, 2)
    first = swap(near[:half], 2)
    second = swap(side[half:], 1)
    return [values, near, side, jnp.concatenate([first, second], axis=0)]


def inverse_rms(values):
    return lax.rsqrt(jnp.mean(values * values, axis=-1, keepdims=True) + 1e-06)


def rms_norm(values, gain):
    return values * inverse_rms(values) * gain


def sigmoid(values):
    return 0.5 * jnp.tanh(0.5 * values) + 0.5


def gelu_parts(values):
    c = 0.7978845608028654
    sq = values * values
    t = jnp.tanh(c * values * (1.0 + 0.044715 * sq))
    half = 0.5 * (1.0 + t)
    return values * half, half + 0.5 * values * (1.0 - t * t) * (c * (1.0 + 3.0 * 0.044715 * sq))


def drop_of(rate_log):
    u = 2.0 * rate_log
    series = 1.0 + u * (1.0 / 8.0)
    for n in (7, 6, 5, 4, 3, 2):
        series = 1.0 + u * series * (1.0 / n)
    return jnp.where(u > -0.4, -u * series, 1.0 - jnp.exp(u))


def scan_rows(rate, drive, reverse):
    rows, lanes = rate.shape
    count = rows // 8
    rate = rate.reshape(count, 8, lanes)
    drive = drive.reshape(count, 8, lanes)
    row = lax.broadcasted_iota(jnp.int32, (count, 8, lanes), 1)
    for step in (1, 2, 4):
        shift = 8 - step if reverse else step
        keep = row < 8 - step if reverse else row >= step
        drive = drive + rate * jnp.where(keep, pltpu.roll(drive, shift, 1), 0.0)
        rate = rate * jnp.where(keep, pltpu.roll(rate, shift, 1), 1.0)
    state, reach = jnp.zeros((1, lanes), F32), jnp.ones((1, lanes), F32)
    states, reaches = [None] * count, [None] * count
    last = 0 if reverse else 7
    for i in reversed(range(count)) if reverse else range(count):
        states[i] = drive[i] + rate[i] * state
        reaches[i] = rate[i] * reach
        state = states[i][last : last + 1]
        reach = reaches[i][last : last + 1]
    return jnp.concatenate(states, axis=0), jnp.concatenate(reaches, axis=0)


def forward_kernel(
    off_ref, x_ref, edge_ref, gates_ref, chan_ref,
    forget_out, admit_out, conv_out_ref, rate_out, local_out, reach_out, ends_out,
    logits,
):
    q = pl.program_id(0)
    tokens = x_ref.shape[0]
    share = chan_ref.shape[1]
    blocks = x_ref.shape[1] // BW
    off = pl.multiple_of(off_ref[0], LANES)
    for b in range(blocks):
        cols = slice(b * BW, (b + 1) * BW)
        mixed = jnp.dot(x_ref[:, cols], gates_ref[cols, :], preferred_element_type=F32)
        logits[0, :, cols] = mixed[:, :BW]
        logits[1, :, cols] = mixed[:, BW:]
    for j in range(share // LANES):
        lanes = slice(j * LANES, (j + 1) * LANES)
        here = pl.ds(pl.multiple_of(off + j * LANES, LANES), LANES)
        chan = [chan_ref[i : i + 1, lanes] for i in range(8)]
        forget = (logits[0, :, here] + chan[0]).astype(BF)
        admit = (logits[1, :, here] + chan[1]).astype(BF)
        forget_out[:, lanes] = forget
        admit_out[:, lanes] = admit
        edge = edge_ref[pl.ds(pl.multiple_of(q * HALO, HALO), HALO), here]
        padded = jnp.concatenate([edge, x_ref[:, here].astype(F32)], axis=0)
        conv = chan[3] + chan[4] * padded[HALO:]
        for k in range(1, CONV):
            conv = conv + chan[4 + k] * pltpu.roll(padded, k, 0)[HALO:]
        conv_out_ref[:, lanes] = conv
        rate_log = -8.0 * chan[2] * (0.1 + 0.9 * sigmoid(forget.astype(F32)))
        rate = jnp.exp(rate_log)
        drive = jnp.sqrt(drop_of(rate_log)) * sigmoid(admit.astype(F32)) * conv
        state, reach = scan_rows(rate, drive, False)
        rate_out[:, lanes] = rate
        local_out[:, lanes] = state
        reach_out[:, lanes] = reach
        ends_out[0, 0, :, lanes] = reach[tokens - 1 :]
        ends_out[0, 1, :, lanes] = state[tokens - 1 :]


def whole(shape):
    return pl.BlockSpec(shape, lambda q: (0,) * len(shape))


def per_seq(width):
    return pl.BlockSpec((1, 1, width), lambda q: (q, 0, 0))


def temporal_forward(off, x_win, edge, gates, chan, tokens):
    total, window = x_win.shape
    share = chan.shape[1]
    seqs = total // tokens
    part = lambda width: pl.BlockSpec((tokens, width), lambda q: (q, 0))
    return pl.pallas_call(
        forward_kernel,
        grid=(seqs,),
        in_specs=[
            pl.BlockSpec(memory_space=pltpu.SMEM),
            part(window),
            whole(edge.shape),
            whole(gates.shape),
            whole(chan.shape),
        ],
        out_specs=[
            part(share), part(share), part(share), part(share), part(share), part(share),
            pl.BlockSpec((1, 2, 1, share), lambda q: (q, 0, 0, 0)),
        ],
        out_shape=[
            jax.ShapeDtypeStruct((total, share), BF),
            jax.ShapeDtypeStruct((total, share), BF),
            jax.ShapeDtypeStruct((total, share), F32),
            jax.ShapeDtypeStruct((total, share), F32),
            jax.ShapeDtypeStruct((total, share), F32),
            jax.ShapeDtypeStruct((total, share), F32),
            jax.ShapeDtypeStruct((seqs, 2, 1, share), F32),
        ],
        scratch_shapes=[
            pltpu.VMEM((2, tokens, window), F32),
        ],
        compiler_params=pltpu.CompilerParams(vmem_limit_bytes=48 * 1024 * 1024),
        cost_estimate=pl.CostEstimate(flops=1000, bytes_accessed=1000, transcendentals=0),
        name="temporal_forward",
    )(off, x_win, edge, gates, chan)


def backward_scan_kernel(
    grad_ref, y_ref, local_ref, reach_ref, carry_ref, rate_ref,
    y_rows_out, adjoint_out, later_out, heads_out,
):
    tokens, share = grad_ref.shape
    row = lax.broadcasted_iota(jnp.int32, (tokens, LANES), 0)
    for j in range(share // LANES):
        lanes = slice(j * LANES, (j + 1) * LANES)
        grad = grad_ref[:, lanes]
        value, slope = gelu_parts(y_ref[:, lanes])
        state = (local_ref[:, lanes] + reach_ref[:, lanes] * carry_ref[0, :, lanes]).astype(BF)
        y_rows_out[:, lanes] = (grad * state.astype(F32) * slope).astype(BF)
        state_grad = (grad * value).astype(BF).astype(F32)
        rate = rate_ref[:, lanes]
        ahead = jnp.where(row == tokens - 1, 1.0, pltpu.roll(rate, tokens - 1, 0))
        adjoint, later = scan_rows(ahead, state_grad, True)
        adjoint_out[:, lanes] = adjoint
        later_out[:, lanes] = later
        heads_out[0, :, lanes] = rate[:1] * adjoint[:1]


def backward_scan(grad, y, local, reach, carry, rate, tokens):
    total, share = grad.shape
    seqs = total // tokens
    part = pl.BlockSpec((tokens, share), lambda q: (q, 0))
    return pl.pallas_call(
        backward_scan_kernel,
        grid=(seqs,),
        in_specs=[part, part, part, part, per_seq(share), part],
        out_specs=[part, part, part, per_seq(share)],
        out_shape=[
            jax.ShapeDtypeStruct((total, share), BF),
            jax.ShapeDtypeStruct((total, share), F32),
            jax.ShapeDtypeStruct((total, share), F32),
            jax.ShapeDtypeStruct((seqs, 1, share), F32),
        ],
        compiler_params=pltpu.CompilerParams(vmem_limit_bytes=48 * 1024 * 1024),
        cost_estimate=pl.CostEstimate(flops=1000, bytes_accessed=1000, transcendentals=0),
        name="backward_scan",
    )(grad, y, local, reach, carry[:, None, :], rate)


def backward_rows_kernel(
    off_ref, adjoint_ref, later_ref, local_ref, reach_ref, rate_ref, conv_ref,
    forget_ref, admit_ref, x_ref, edge_ref, gates_ref, chan_ref, carry_ref, tail_ref, after_ref,
    branch_out, forget_out, admit_out, sums_out,
    conv_rows,
):
    q = pl.program_id(0)
    tokens = adjoint_ref.shape[0]
    share = chan_ref.shape[1]
    window = x_ref.shape[1]
    off = pl.multiple_of(off_ref[0], LANES)
    forget_out[...] = jnp.zeros_like(forget_out)
    admit_out[...] = jnp.zeros_like(admit_out)
    conv_rows[...] = jnp.zeros_like(conv_rows)

    @pl.when(q == 0)
    def _():
        sums_out[...] = jnp.zeros_like(sums_out)

    row = lax.broadcasted_iota(jnp.int32, (tokens, LANES), 0)
    for j in range(share // LANES):
        lanes = slice(j * LANES, (j + 1) * LANES)
        here = pl.ds(pl.multiple_of(off + j * LANES, LANES), LANES)
        chan = [chan_ref[i : i + 1, lanes] for i in range(8)]
        reach = reach_ref[:, lanes]
        carry = carry_ref[0, :, lanes]
        carried = local_ref[:, lanes] + reach * carry
        before = jnp.where(row == 0, carry, pltpu.roll(carried, 1, 0))
        adjoint = adjoint_ref[:, lanes] + later_ref[:, lanes] * tail_ref[0, :, lanes]
        forget_sig = sigmoid(forget_ref[:, lanes].astype(F32))
        admit_sig = sigmoid(admit_ref[:, lanes].astype(F32))
        span = 0.1 + 0.9 * forget_sig
        rate_log = -8.0 * chan[2] * span
        rate = rate_ref[:, lanes]
        scale = jnp.sqrt(drop_of(rate_log))
        conv = conv_ref[:, lanes]
        gated = admit_sig * conv
        log_grad = adjoint * (rate * before - rate * rate / scale * gated)
        conv_grad = adjoint * scale * admit_sig
        forget_rows = (
            log_grad * (-7.2) * chan[2] * forget_sig * (1.0 - forget_sig)
        ).astype(BF)
        admit_rows = (adjoint * scale * gated * (1.0 - admit_sig)).astype(BF)
        forget_out[:, here] = forget_rows
        admit_out[:, here] = admit_rows
        after = after_ref[pl.ds(pl.multiple_of(q * HALO, HALO), HALO), lanes]
        ahead = jnp.concatenate([conv_grad, after], axis=0)
        back = chan[4] * conv_grad
        for k in range(1, CONV):
            back = back + chan[4 + k] * pltpu.roll(ahead, tokens + HALO - k, 0)[:tokens]
        conv_rows[:, here] = back.astype(BF).astype(F32)
        edge = edge_ref[pl.ds(pl.multiple_of(q * HALO, HALO), HALO), here]
        padded = jnp.concatenate([edge, x_ref[:, here].astype(F32)], axis=0)
        sums = [
            forget_rows.astype(F32),
            admit_rows.astype(F32),
            log_grad * (-8.0) * span,
            conv_grad,
            conv_grad * padded[HALO:],
        ] + [conv_grad * pltpu.roll(padded, k, 0)[HALO:] for k in range(1, CONV)]
        sums_out[:, lanes] += jnp.concatenate(
            [jnp.sum(v, axis=0, keepdims=True) for v in sums], axis=0
        )
    for b in range(window // BW):
        cols = slice(b * BW, (b + 1) * BW)
        back = conv_rows[:, cols]
        for source, at in ((forget_out, 0), (admit_out, BW)):
            back = back + lax.dot_general(
                source[:, cols],
                gates_ref[cols, at : at + BW],
                (((1,), (1,)), ((), ())),
                preferred_element_type=F32,
            )
        branch_out[:, cols] = back.astype(BF)


def backward_rows(off, adjoint, later, local, reach, rate, conv, forget, admit, x_win, edge, gates, chan, carry, tail, after, tokens):
    total, window = x_win.shape
    share = chan.shape[1]
    seqs = total // tokens
    part = lambda width: pl.BlockSpec((tokens, width), lambda q: (q, 0))
    return pl.pallas_call(
        backward_rows_kernel,
        grid=(seqs,),
        in_specs=[pl.BlockSpec(memory_space=pltpu.SMEM)]
        + [part(share)] * 8
        + [part(window)]
        + [whole(v.shape) for v in (edge, gates, chan)]
        + [per_seq(share), per_seq(share), whole(after.shape)],
        out_specs=[part(window), part(window), part(window), whole((8, share))],
        out_shape=[jax.ShapeDtypeStruct((total, window), BF)] * 3
        + [jax.ShapeDtypeStruct((8, share), F32)],
        scratch_shapes=[pltpu.VMEM((tokens, window), F32)],
        compiler_params=pltpu.CompilerParams(vmem_limit_bytes=48 * 1024 * 1024),
        cost_estimate=pl.CostEstimate(flops=1000, bytes_accessed=1000, transcendentals=0),
        name="backward_rows",
    )(off, adjoint, later, local, reach, rate, conv, forget, admit, x_win, edge, gates, chan, carry[:, None, :], tail[:, None, :], after)


def partner(mask):
    s = lax.axis_index("seq")
    if mask == 1:
        other = s + 1 - 2 * (s % 2)
    else:
        other = (s + 2) % 4
    return {"seq": other}


def greet():
    barrier = pltpu.get_barrier_semaphore()
    for mask in (1, 2):
        pl.semaphore_signal(barrier, inc=1, device_id=partner(mask), device_id_type=MESH)
    pl.semaphore_wait(barrier, 2)


def sender(sends, recvs):
    def send(slot, source, target, mask):
        copy = pltpu.make_async_remote_copy(
            src_ref=source,
            dst_ref=target,
            send_sem=sends.at[slot],
            recv_sem=recvs.at[slot],
            device_id=partner(mask),
            device_id_type=MESH,
        )
        copy.start()
        return copy

    return send


def over_chunks(rows, run):
    def step(i, carry):
        run(pl.ds(pl.multiple_of(i * ROWS16, ROWS16), ROWS16))
        return carry

    lax.fori_loop(0, rows // ROWS16, step, 0)


def reduce_phase(product, send, first_slot, acc, sent, got):
    rows = acc.shape[1]
    half = rows // 2
    low, high = pl.ds(0, half), pl.ds(half, half)
    product(3, lambda cols, value: sent.__setitem__((0, slice(None), cols), value.astype(BF)))
    far_near = send(first_slot, sent.at[0, low], got.at[0, low], 1)
    far_side = send(first_slot + 1, sent.at[0, high], got.at[0, high], 2)
    product(1, lambda cols, value: acc.__setitem__((1, slice(None), cols), value))
    over_chunks(half, lambda r: sent.__setitem__((1, r), acc[1, r].astype(BF)))
    near_low = send(first_slot + 2, sent.at[1, low], got.at[1, low], 1)
    product(2, lambda cols, value: acc.__setitem__((2, slice(None), cols), value))

    def tail(k):
        def run(r):
            r = pl.ds(pl.multiple_of(r.start + half, ROWS16), ROWS16)
            sent[k, r] = acc[k, r].astype(BF)

        return run

    over_chunks(half, tail(2))
    side_high = send(first_slot + 3, sent.at[2, high], got.at[2, high], 2)
    far_side.wait_recv()

    def add_high(r):
        r = pl.ds(pl.multiple_of(r.start + half, ROWS16), ROWS16)
        sent[1, r] = (acc[1, r] + got[0, r].astype(F32)).astype(BF)

    over_chunks(half, add_high)
    near_high = send(first_slot + 4, sent.at[1, high], got.at[1, high], 1)
    far_near.wait_recv()

    def add_low(r):
        sent[2, r] = (acc[2, r] + got[0, r].astype(F32)).astype(BF)

    over_chunks(half, add_low)
    side_low = send(first_slot + 5, sent.at[2, low], got.at[2, low], 2)
    product(0, lambda cols, value: acc.__setitem__((0, slice(None), cols), value))
    arriving = [near_low, side_high, near_high, side_low]
    for copy in arriving:
        copy.wait_recv()
    return [far_near, far_side] + arriving


def gather_phase(send, first_slot, out):
    half = out.shape[1] // 2
    low, high = pl.ds(0, half), pl.ds(half, half)
    near_low = send(first_slot, out.at[0, low], out.at[1, low], 1)
    side_high = send(first_slot + 1, out.at[0, high], out.at[2, high], 2)
    near_high = send(first_slot + 2, out.at[0, high], out.at[1, high], 1)
    side_low = send(first_slot + 3, out.at[0, low], out.at[2, low], 2)
    near_low.wait_recv()
    far_low = send(first_slot + 4, out.at[1, low], out.at[3, low], 2)
    side_high.wait_recv()
    far_high = send(first_slot + 5, out.at[2, high], out.at[3, high], 1)
    for copy in (near_high, side_low, far_low, far_high):
        copy.wait_recv()
    return [near_low, side_high, near_high, side_low, far_low, far_high]


def product_of(left, right, contract, rows, tile):
    def product(k, store):
        def step(c, carry):
            cols = pl.ds(pl.multiple_of(c * tile, tile), tile)
            total = None
            for a, b in zip(left, right):
                part = b[cols, :] if contract else b[:, cols]
                value = lax.dot_general(
                    a[k * rows : (k + 1) * rows, :],
                    part,
                    (((1,), (1 if contract else 0,)), ((), ())),
                    preferred_element_type=F32,
                )
                total = value if total is None else total + value
            store(cols, total)
            return carry

        width = right[0].shape[0 if contract else 1]
        lax.fori_loop(0, width // tile, step, 0)

    return product


def rms_parts(values):
    return lax.rsqrt(jnp.mean(values * values, axis=-1, keepdims=True) + 1e-06)


def stream_kernel(
    mixed_ref, weight_ref, flat_ref, gain_ref,
    stream_out, temporal_out, normed_out,
    acc, sent, got, sends, recvs,
):
    rows = flat_ref.shape[0]
    greet()
    send = sender(sends, recvs)
    copies = reduce_phase(
        product_of([mixed_ref], [weight_ref], False, rows, 512), send, 0, acc, sent, got
    )

    def finish(r):
        temporal = acc[0, r] + got[1, r].astype(F32) + got[2, r].astype(F32)
        temporal_out[r] = temporal
        stream = flat_ref[r].astype(F32) + temporal
        stream_out[r] = stream
        normed_out[0, r] = (stream * rms_parts(stream) * gain_ref[...]).astype(BF)

    over_chunks(rows, finish)
    copies += gather_phase(send, 6, normed_out)
    for copy in copies:
        copy.wait_send()


def exchange_scratch(rows, width, copies):
    return [
        pltpu.VMEM((3, rows, width), F32),
        pltpu.VMEM((3, rows, width), BF),
        pltpu.VMEM((3, rows, width), BF),
        pltpu.SemaphoreType.DMA((copies,)),
        pltpu.SemaphoreType.DMA((copies,)),
    ]


def remote_call(kernel, name, ident, outs, operands, scratch):
    return pl.pallas_call(
        kernel,
        in_specs=[pl.BlockSpec(memory_space=pltpu.VMEM)] * len(operands),
        out_specs=[pl.BlockSpec(memory_space=pltpu.VMEM)] * len(outs),
        out_shape=[jax.ShapeDtypeStruct(shape, kind) for shape, kind in outs],
        scratch_shapes=scratch,
        compiler_params=pltpu.CompilerParams(
            collective_id=ident, has_side_effects=True, vmem_limit_bytes=60 * 1024 * 1024
        ),
        cost_estimate=pl.CostEstimate(flops=1000, bytes_accessed=1000, transcendentals=0),
        name=name,
    )(*operands)


def stream_and_norm(mixed, weight, flat, gain):
    rows, width = flat.shape
    groups = mixed.shape[0] // rows
    return remote_call(
        stream_kernel,
        "stream_and_norm",
        1,
        [((rows, width), F32), ((rows, width), F32), ((groups, rows, width), BF)],
        (mixed, weight, flat, gain),
        exchange_scratch(rows, width, 12),
    )


def stream_back_kernel(
    rows_ref, weight_ref, stream_ref, gain_ref, upstream_ref,
    grad_out, low_out, gain_out,
    acc, sent, got, sends, recvs,
):
    rows, width = stream_ref.shape
    greet()
    send = sender(sends, recvs)
    copies = reduce_phase(
        product_of([rows_ref], [weight_ref], True, rows, 512), send, 0, acc, sent, got
    )
    gain_out[...] = jnp.zeros_like(gain_out)

    def finish(r):
        grad = acc[0, r] + got[1, r].astype(F32) + got[2, r].astype(F32)
        stream = stream_ref[r]
        inv = rms_parts(stream)
        scaled = grad * gain_ref[...]
        inner = jnp.mean(stream * scaled, axis=-1, keepdims=True)
        total = upstream_ref[r].astype(F32) + inv * scaled - stream * (inv * inv * inv * inner)
        grad_out[r] = total
        low_out[0, r] = total.astype(BF)
        gained = grad * stream * inv
        gain_out[...] += gained[:8] + gained[8:]

    over_chunks(rows, finish)
    copies += gather_phase(send, 6, low_out)
    for copy in copies:
        copy.wait_send()


def stream_back(rows_all, weight, stream, gain, upstream):
    rows, width = stream.shape
    groups = rows_all.shape[0] // rows
    return remote_call(
        stream_back_kernel,
        "stream_back",
        2,
        [((rows, width), F32), ((groups, rows, width), BF), ((8, width), F32)],
        (rows_all, weight, stream, gain, upstream),
        exchange_scratch(rows, width, 12),
    )


def inputs_back_kernel(
    branch_ref, y_ref, weight_ref, flat_ref, gain_ref, stream_grad_ref,
    grad_out, gain_out,
    acc, sent, got, sends, recvs,
):
    rows, width = flat_ref.shape
    greet()
    send = sender(sends, recvs)
    window = branch_ref.shape[1]
    weights = [weight_ref.at[:, :window], weight_ref.at[:, window:]]
    copies = reduce_phase(
        product_of([branch_ref, y_ref], weights, True, rows, 512), send, 0, acc, sent, got
    )
    gain_out[...] = jnp.zeros_like(gain_out)

    def finish(r):
        grad = acc[0, r] + got[1, r].astype(F32) + got[2, r].astype(F32)
        values = flat_ref[r].astype(F32)
        inv = rms_parts(values)
        scaled = grad * gain_ref[...]
        inner = jnp.mean(values * scaled, axis=-1, keepdims=True)
        grad_out[r] = stream_grad_ref[r] + inv * scaled - values * (inv * inv * inv * inner)
        gained = grad * values * inv
        gain_out[...] += gained[:8] + gained[8:]

    over_chunks(rows, finish)
    for copy in copies:
        copy.wait_send()


def inputs_back(branch_rows, y_rows, weight, flat, gain, stream_grad):
    rows, width = flat.shape
    return remote_call(
        inputs_back_kernel,
        "inputs_back",
        3,
        [((rows, width), F32), ((8, width), F32)],
        (branch_rows, y_rows, weight, flat, gain, stream_grad),
        exchange_scratch(rows, width, 6),
    )


def result_kernel(
    hidden_ref, weight_ref, stream_ref, temporal_ref, valid_ref,
    result_out, sums_out,
    acc, sent, got, sends, recvs,
):
    rows = stream_ref.shape[0]
    greet()
    send = sender(sends, recvs)
    copies = reduce_phase(
        product_of([hidden_ref], [weight_ref], False, rows, 512), send, 0, acc, sent, got
    )
    sums_out[...] = jnp.zeros_like(sums_out)

    def finish(r):
        feed = acc[0, r] + got[1, r].astype(F32) + got[2, r].astype(F32)
        result = stream_ref[r] + feed
        result_out[r] = result.astype(BF)
        valid = valid_ref[r]
        for i, values in enumerate((result, temporal_ref[r], feed)):
            square = valid * values * values
            sums_out[i] += square[:8] + square[8:]

    over_chunks(rows, finish)
    for copy in copies:
        copy.wait_send()


def result_of(hidden, weight, stream, temporal, valid):
    rows, width = stream.shape
    return remote_call(
        result_kernel,
        "result_of",
        4,
        [((rows, width), BF), ((3, 8, width), F32)],
        (hidden, weight, stream, temporal, valid),
        exchange_scratch(rows, width, 6),
    )


def body(
    inputs,
    lengths,
    norm_gain,
    gelu_weight,
    branch_weight,
    forget_gates,
    admit_gates,
    forget_bias,
    admit_bias,
    decay_rate,
    conv_weight,
    conv_bias,
    out_weight,
    mlp_gain,
    gate_weight,
    up_weight,
    down_weight,
    cotangent,
):
    groups = lax.axis_size("seq")
    wide = lax.axis_size("wide")
    s = lax.axis_index("seq")
    w = lax.axis_index("wide")
    seqs, tokens, width = inputs.shape
    rows = seqs * tokens
    total = groups * rows
    all_seqs = groups * seqs
    channels = gelu_weight.shape[1]
    share = channels // groups
    window = (share + BW - 1) // BW * BW
    blocks = window // BW

    def base_of(index):
        return jnp.minimum(index * share // BW * BW, channels - window)

    base = base_of(s)
    off = s * share - base
    quarter = width // groups
    gate_cols = 2 * BW // groups

    flat_low = inputs.reshape(rows, width)
    upstream = cotangent.reshape(rows, width)
    edge = lax.ppermute(
        inputs[:, tokens - HALO :, :].reshape(seqs * HALO, width),
        "wide",
        [(i, i + 1) for i in range(wide - 1)],
    )
    token_blocks = gather_seq(flat_low)
    edge_blocks = [swap(edge, k) if k else edge for k in range(groups)]

    x_y_cols = lax.all_gather(
        jnp.concatenate(
            [
                lax.dynamic_slice_in_dim(branch_weight, base, window, 1),
                lax.dynamic_slice_in_dim(gelu_weight, s * share, share, 1),
            ],
            axis=1,
        ),
        "wide",
        axis=0,
        tiled=True,
    )
    dw, rw = width // wide, channels // wide
    small = jnp.concatenate(
        [norm_gain, mlp_gain, forget_bias, admit_bias, decay_rate, conv_bias, conv_weight.reshape(-1)]
    ).reshape(-1, gate_cols)
    gates_quarter = jnp.concatenate([forget_gates, admit_gates], axis=1)
    small = jnp.concatenate(
        [lax.dynamic_slice_in_dim(gates_quarter, s * gate_cols, gate_cols, 1), small], axis=0
    )
    small, token_blocks[1] = lax.optimization_barrier((small, token_blocks[1]))
    small = lax.all_gather(small, "wide")
    gates_quarter = small[:, :rw].reshape(channels, gate_cols)
    small = small[:, rw:].reshape(wide, -1).astype(F32)
    gain_one = small[:, :dw].reshape(1, width)
    gain_two = small[:, dw : 2 * dw].reshape(1, width)
    per_channel = small[:, 2 * dw :].reshape(wide, 8, rw).transpose(1, 0, 2).reshape(8, channels)
    per_channel = lax.dynamic_slice_in_dim(per_channel, s * share, share, 1)

    out_quarter = lax.all_gather(
        lax.dynamic_slice_in_dim(out_weight, s * quarter, quarter, 1), "wide", axis=0, tiled=True
    )
    mlp_full = lax.all_gather(
        jnp.concatenate([gate_weight, up_weight], axis=1), "wide", axis=0, tiled=True
    )
    down_full = lax.all_gather(down_weight, "wide", axis=1, tiled=True)
    hidden_units = gate_weight.shape[1]

    def in_order(parts):
        near = [jnp.where(s % 2 == 1, parts[k ^ 1], parts[k]) for k in range(groups)]
        return [jnp.where(s // 2 == 1, near[k ^ 2], near[k]) for k in range(groups)]

    gate_parts, out_parts = [], []
    for k in range(groups):
        other = s ^ k
        part = lax.dynamic_slice_in_dim(gates_quarter, base_of(other), window, 0)
        gate_parts.append(swap(part, k) if k else part)
        part = lax.dynamic_slice_in_dim(out_quarter, other * share, share, 0)
        out_parts.append(swap(part, k) if k else part)
    gates = jnp.concatenate(in_order(gate_parts), axis=1)
    out_rows = jnp.concatenate(in_order(out_parts), axis=1)

    all_low = jnp.concatenate(token_blocks + edge_blocks, axis=0)
    normed_ext = rms_norm(all_low.astype(F32), gain_one).astype(BF)
    normed_all = normed_ext[:total]

    x_y = dot(normed_all, x_y_cols)
    x_win = x_y[:, :window].astype(BF)
    branch_y = x_y[:, window:]
    edge_win = dot(normed_ext[total:], x_y_cols[:, :window]).astype(BF).astype(F32)
    offset = off.reshape(1)
    forget, admit, conv_out, rate, local, reach, ends = temporal_forward(
        offset, x_win, edge_win, gates, per_channel, tokens
    )
    ends, later_upstream = lax.optimization_barrier((ends, upstream))
    upstream_all = jnp.concatenate(gather_seq(later_upstream), axis=0)
    ends = lax.all_gather(ends, "wide")[:, :, :, 0]
    carry = jnp.zeros((all_seqs, share), F32)
    for j in range(wide - 1):
        carry = jnp.where(j < w, ends[j, :, 0] * carry + ends[j, :, 1], carry)
    carried = local.reshape(all_seqs, tokens, share) + reach.reshape(
        all_seqs, tokens, share
    ) * carry[:, None, :]
    state = carried.astype(BF).astype(F32).reshape(total, share)

    gelu_y = jax.nn.gelu(branch_y)
    mixed_low = (state * gelu_y).astype(BF)
    stream, temporal, normed_two_all = stream_and_norm(mixed_low, out_rows, flat_low, gain_two)
    normed_two_all = normed_two_all.reshape(total, width)

    gate_up = dot(normed_two_all, mlp_full)
    gate, up_values = gate_up[:, :hidden_units], gate_up[:, hidden_units:]
    gelu_gate = jax.nn.gelu(gate)
    hidden_low = (gelu_gate * up_values).astype(BF)
    down_part = contract_rows(hidden_low, upstream_all).astype(BF)
    hidden_low, down_part, upstream_low = lax.optimization_barrier(
        (hidden_low, down_part, upstream_all)
    )
    down_grad = lax.psum_scatter(down_part, "wide", scatter_dimension=1, tiled=True)
    hidden_grad = contract_last(upstream_low, down_full)
    gate_rows = (hidden_grad * up_values * gelu_parts(gate)[1]).astype(BF)
    up_rows = (hidden_grad * gelu_gate).astype(BF)
    mlp_rows = jnp.concatenate([gate_rows, up_rows], axis=1)
    mlp_part = contract_rows(normed_two_all, mlp_rows).astype(BF)
    mlp_rows, mlp_part = lax.optimization_barrier((mlp_rows, mlp_part))
    mlp_grad = lax.psum_scatter(mlp_part, "wide", scatter_dimension=0, tiled=True)
    stream_grad, stream_low_all, gain_two_grad = stream_back(
        mlp_rows, mlp_full, stream, gain_two, upstream
    )
    gain_two_grad = jnp.sum(gain_two_grad, axis=0)
    stream_low_all = stream_low_all.reshape(total, width)
    stream_low_all, down_grad = lax.optimization_barrier((stream_low_all, down_grad))
    position = w * tokens + jnp.arange(tokens, dtype=jnp.int32)
    valid = (position[None, :] < lengths[:, None]).astype(F32).reshape(rows, 1)
    mixed_grad = contract_last(stream_low_all, out_rows)
    y_rows, adjoint, later, heads = backward_scan(
        mixed_grad, branch_y, local, reach, carry, rate, tokens
    )
    heads = lax.all_gather(heads, "wide")[:, :, 0]

    def firsts(values):
        return values.reshape(all_seqs, tokens, share)[:, :HALO].astype(F32)

    first_rate = -8.0 * per_channel[2] * (0.1 + 0.9 * jax.nn.sigmoid(firsts(forget)))
    gain = jnp.sqrt(-jnp.expm1(2.0 * first_rate)) * jax.nn.sigmoid(firsts(admit))
    after = lax.ppermute(
        jnp.stack([firsts(adjoint) * gain, firsts(later) * gain]),
        "wide",
        [(i + 1, i) for i in range(wide - 1)],
    )
    tail = jnp.zeros((all_seqs, share), F32)
    next_tail = tail
    for j in range(wide - 1, 0, -1):
        stepped = ends[j, :, 0] * tail + heads[j]
        next_tail = jnp.where(j > w + 1, stepped, next_tail)
        tail = jnp.where(j > w, stepped, tail)
    after = (after[0] + after[1] * next_tail[:, None, :]).reshape(all_seqs * HALO, share)
    branch_rows, forget_win, admit_win, channel_grads = backward_rows(
        offset, adjoint, later, local, reach, rate, conv_out, forget, admit,
        x_win, edge_win, gates, per_channel, carry, tail, after, tokens,
    )
    bases = [min(j * share // BW * BW, channels - window) for j in range(groups)]

    def placed(parts, axis):
        rest = [
            tuple(
                (bases[j], channels - window - bases[j]) if d == axis else (0, 0) for d in range(2)
            )
            for j in range(groups)
        ]
        return sum(jnp.pad(p.astype(F32), r) for p, r in zip(parts, rest))

    def swapped(part_of):
        return [swap(part_of(s ^ k), k) if k else part_of(s) for k in range(groups)]

    def stack(values):
        values = values.reshape(wide, values.shape[0] // wide, values.shape[1])
        tiles = values.shape[2] // LANES
        return jnp.concatenate(
            [values[:, :, i * LANES : (i + 1) * LANES] for i in range(tiles)], axis=1
        )

    def unstack(values, count, columns):
        return jnp.concatenate(
            [values[i * count : (i + 1) * count] for i in range(columns // LANES)], axis=1
        )

    out_grad = contract_rows(mixed_low, stream_low_all).astype(BF)
    out_cols = jnp.concatenate(
        in_order(
            swapped(lambda j: lax.dynamic_slice_in_dim(out_grad, j * quarter, quarter, 1))
        ),
        axis=0,
    )
    gelu_part = contract_rows(normed_all, y_rows).astype(BF)

    gate_grads = jnp.concatenate(
        [
            jnp.einsum(
                "tki,tkj->kij",
                x_win.reshape(total, blocks, BW),
                rows_win.reshape(total, blocks, BW),
                preferred_element_type=F32,
            ).reshape(window, BW)
            for rows_win in (forget_win, admit_win)
        ],
        axis=1,
    ).astype(BF)
    gate_cols_grad = placed(
        in_order(
            swapped(lambda j: lax.dynamic_slice_in_dim(gate_grads, j * gate_cols, gate_cols, 1))
        ),
        0,
    ).astype(BF)
    branch_part = contract_rows(normed_all, branch_rows).astype(BF)
    first_pieces = [(gelu_part, share), (out_cols, quarter)]
    second_pieces = [(branch_part, window), (gate_cols_grad, gate_cols)]
    first = jnp.concatenate([stack(values) for values, _unused in first_pieces], axis=1)
    second = jnp.concatenate([stack(values) for values, _unused in second_pieces], axis=1)
    first, mlp_grad, branch_late = lax.optimization_barrier((first, mlp_grad, branch_rows))
    first = lax.psum_scatter(first, "wide", scatter_dimension=0, tiled=True)
    inputs_grad, gain_one_grad = inputs_back(
        branch_late, y_rows, x_y_cols, flat_low, gain_one, stream_grad
    )
    second = lax.psum_scatter(second, "wide", scatter_dimension=0, tiled=True)
    first, gain_one_grad, stream_late = lax.optimization_barrier((first, gain_one_grad, stream))
    output, square_sums = result_of(hidden_low, down_full, stream_late, temporal, valid)
    second, square_sums = lax.optimization_barrier((second, square_sums))

    def spread(summed, pieces):
        parts = in_order(swapped(lambda j: summed[0]))
        start, spread_pieces = 0, []
        for values, columns in pieces:
            count = values.shape[0] // wide
            size = count * columns // LANES
            spread_pieces.append([unstack(p[start : start + size], count, columns) for p in parts])
            start += size
        return spread_pieces

    gelu_parts_all, out_parts_all = spread(first, first_pieces)
    branch_parts_all, gate_parts_all = spread(second, second_pieces)
    gelu_whole = jnp.concatenate(gelu_parts_all, axis=1).astype(F32)
    out_whole = jnp.concatenate(out_parts_all, axis=1).astype(F32)
    branch_whole = placed(branch_parts_all, 1)
    gates_whole = jnp.concatenate(gate_parts_all, axis=1).astype(F32)
    partial_sums = jnp.concatenate([jnp.sum(square_sums, axis=(1, 2)), jnp.sum(valid).reshape(1)])
    inputs_grad = inputs_grad.reshape(seqs, tokens, width)
    output = output.reshape(seqs, tokens, width)
    channel_all = lax.dynamic_update_slice_in_dim(
        jnp.zeros((8, channels), F32), channel_grads, s * share, 1
    )
    sums = jnp.concatenate(
        [
            channel_all.reshape(8, wide, rw).transpose(1, 0, 2).reshape(wide, 8 * rw),
            jnp.sum(gain_one_grad, axis=0).reshape(wide, dw),
            gain_two_grad.reshape(wide, dw),
            jnp.tile(partial_sums[None, :], (wide, 1)),
        ],
        axis=1,
    )
    sums = jnp.sum(lax.all_to_all(sums, "wide", 0, 0), axis=0)
    sums = sums + swap(sums, 1)
    sums = sums + swap(sums, 2)
    channel_sums = sums[: 8 * rw].reshape(8, rw)
    gain_sums = sums[8 * rw : 8 * rw + 2 * dw].reshape(2, dw)
    totals = sums[8 * rw + 2 * dw :]
    statistics = jnp.sqrt(totals[0:3] / (totals[3] * width))
    return (
        output,
        inputs_grad,
        gain_sums[0],
        gelu_whole,
        branch_whole,
        gates_whole[:, :BW],
        gates_whole[:, BW:],
        channel_sums[0],
        channel_sums[1],
        channel_sums[2],
        channel_sums[4:8],
        channel_sums[3],
        out_whole,
        gain_sums[1],
        mlp_grad[:, :hidden_units].astype(F32),
        mlp_grad[:, hidden_units:].astype(F32),
        down_grad.astype(F32),
        statistics,
    )


def solution(mesh):
    in_specs = (
        P("seq", "wide", None),
        P("seq"),
        P("wide"),
        P("wide", None),
        P("wide", None),
        P("wide", None),
        P("wide", None),
        P("wide"),
        P("wide"),
        P("wide"),
        P(None, "wide"),
        P("wide"),
        P("wide", None),
        P("wide"),
        P("wide", "seq"),
        P("wide", "seq"),
        P("seq", "wide"),
        P("seq", "wide", None),
    )
    out_specs = (
        P("seq", "wide", None),
        P("seq", "wide", None),
        P("wide"),
        P("wide", None),
        P("wide", None),
        P("wide", None),
        P("wide", None),
        P("wide"),
        P("wide"),
        P("wide"),
        P(None, "wide"),
        P("wide"),
        P("wide", None),
        P("wide"),
        P("wide", "seq"),
        P("wide", "seq"),
        P("seq", "wide"),
        P(),
    )
    return jax.shard_map(body, mesh=mesh, in_specs=in_specs, out_specs=out_specs, check_vma=False)
```

```python
import functools

import jax
import jax.numpy as jnp
from jax import lax
from jax.experimental import pallas as pl
from jax.experimental.pallas import tpu as pltpu
from jax.sharding import PartitionSpec as P

BW = 256
CONV = 4
HALO = 8
BF = jnp.bfloat16
F32 = jnp.float32
LANES = 128
ROWS16 = 16
MESH = pl.DeviceIdType.MESH


def dot(left, right):
    return jnp.dot(left, right, preferred_element_type=F32)


def contract_last(left, right):
    return lax.dot_general(left, right, (((1,), (1,)), ((), ())), preferred_element_type=F32)


def contract_rows(left, right):
    return lax.dot_general(left, right, (((0,), (0,)), ((), ())), preferred_element_type=F32)


def swap(values, mask):
    return lax.ppermute(values, "seq", [(i, i ^ mask) for i in range(lax.axis_size("seq"))])


def inverse_rms(values):
    return lax.rsqrt(jnp.mean(values * values, axis=-1, keepdims=True) + 1e-06)


def rms_norm(values, gain):
    return values * inverse_rms(values) * gain


def sigmoid(values):
    return 0.5 * jnp.tanh(0.5 * values) + 0.5


def gelu_parts(values):
    c = 0.7978845608028654
    sq = values * values
    t = jnp.tanh(c * values * (1.0 + 0.044715 * sq))
    half = 0.5 * (1.0 + t)
    return values * half, half + 0.5 * values * (1.0 - t * t) * (c * (1.0 + 3.0 * 0.044715 * sq))


def drop_of(rate_log):
    u = 2.0 * rate_log
    series = 1.0 + u * (1.0 / 8.0)
    for n in (7, 6, 5, 4, 3, 2):
        series = 1.0 + u * series * (1.0 / n)
    return jnp.where(u > -0.4, -u * series, 1.0 - jnp.exp(u))


def scan_rows(rate, drive, reverse):
    rows, lanes = rate.shape
    count = rows // 8
    rate = rate.reshape(count, 8, lanes)
    drive = drive.reshape(count, 8, lanes)
    row = lax.broadcasted_iota(jnp.int32, (count, 8, lanes), 1)
    for step in (1, 2, 4):
        shift = 8 - step if reverse else step
        keep = row < 8 - step if reverse else row >= step
        drive = drive + rate * jnp.where(keep, pltpu.roll(drive, shift, 1), 0.0)
        rate = rate * jnp.where(keep, pltpu.roll(rate, shift, 1), 1.0)
    state, reach = jnp.zeros((1, lanes), F32), jnp.ones((1, lanes), F32)
    states, reaches = [None] * count, [None] * count
    last = 0 if reverse else 7
    for i in reversed(range(count)) if reverse else range(count):
        states[i] = drive[i] + rate[i] * state
        reaches[i] = rate[i] * reach
        state = states[i][last : last + 1]
        reach = reaches[i][last : last + 1]
    return jnp.concatenate(states, axis=0), jnp.concatenate(reaches, axis=0)


def forward_kernel(
    off_ref, x_ref, edge_ref, gates_ref, chan_ref,
    forget_out, admit_out, conv_out_ref, rate_out, local_out, reach_out, ends_out,
    logits,
):
    q = pl.program_id(0)
    tokens = x_ref.shape[0]
    share = chan_ref.shape[1]
    blocks = x_ref.shape[1] // BW
    off = pl.multiple_of(off_ref[0], LANES)
    for b in range(blocks):
        cols = slice(b * BW, (b + 1) * BW)
        mixed = jnp.dot(x_ref[:, cols], gates_ref[cols, :], preferred_element_type=F32)
        logits[0, :, cols] = mixed[:, :BW]
        logits[1, :, cols] = mixed[:, BW:]
    for j in range(share // LANES):
        lanes = slice(j * LANES, (j + 1) * LANES)
        here = pl.ds(pl.multiple_of(off + j * LANES, LANES), LANES)
        chan = [chan_ref[i : i + 1, lanes] for i in range(8)]
        forget = (logits[0, :, here] + chan[0]).astype(BF)
        admit = (logits[1, :, here] + chan[1]).astype(BF)
        forget_out[:, lanes] = forget
        admit_out[:, lanes] = admit
        edge = edge_ref[pl.ds(pl.multiple_of(q * HALO, HALO), HALO), here]
        padded = jnp.concatenate([edge, x_ref[:, here].astype(F32)], axis=0)
        conv = chan[3] + chan[4] * padded[HALO:]
        for k in range(1, CONV):
            conv = conv + chan[4 + k] * pltpu.roll(padded, k, 0)[HALO:]
        conv_out_ref[:, lanes] = conv
        rate_log = -8.0 * chan[2] * (0.1 + 0.9 * sigmoid(forget.astype(F32)))
        rate = jnp.exp(rate_log)
        drive = jnp.sqrt(drop_of(rate_log)) * sigmoid(admit.astype(F32)) * conv
        state, reach = scan_rows(rate, drive, False)
        rate_out[:, lanes] = rate
        local_out[:, lanes] = state
        reach_out[:, lanes] = reach
        ends_out[0, 0, :, lanes] = reach[tokens - 1 :]
        ends_out[0, 1, :, lanes] = state[tokens - 1 :]


def whole(shape):
    return pl.BlockSpec(shape, lambda q: (0,) * len(shape))


def per_seq(width):
    return pl.BlockSpec((1, 1, width), lambda q: (q, 0, 0))


def temporal_forward(off, x_win, edge, gates, chan, tokens):
    total, window = x_win.shape
    share = chan.shape[1]
    seqs = total // tokens
    part = lambda width: pl.BlockSpec((tokens, width), lambda q: (q, 0))
    return pl.pallas_call(
        forward_kernel,
        grid=(seqs,),
        in_specs=[
            pl.BlockSpec(memory_space=pltpu.SMEM),
            part(window),
            whole(edge.shape),
            whole(gates.shape),
            whole(chan.shape),
        ],
        out_specs=[
            part(share), part(share), part(share), part(share), part(share), part(share),
            pl.BlockSpec((1, 2, 1, share), lambda q: (q, 0, 0, 0)),
        ],
        out_shape=[
            jax.ShapeDtypeStruct((total, share), BF),
            jax.ShapeDtypeStruct((total, share), BF),
            jax.ShapeDtypeStruct((total, share), F32),
            jax.ShapeDtypeStruct((total, share), F32),
            jax.ShapeDtypeStruct((total, share), F32),
            jax.ShapeDtypeStruct((total, share), F32),
            jax.ShapeDtypeStruct((seqs, 2, 1, share), F32),
        ],
        scratch_shapes=[
            pltpu.VMEM((2, tokens, window), F32),
        ],
        compiler_params=pltpu.CompilerParams(vmem_limit_bytes=48 * 1024 * 1024),
        cost_estimate=pl.CostEstimate(flops=1000, bytes_accessed=1000, transcendentals=0),
        name="temporal_forward",
    )(off, x_win, edge, gates, chan)


def partner(mask):
    s = lax.axis_index("seq")
    if mask == 1:
        other = s + 1 - 2 * (s % 2)
    else:
        other = (s + 2) % 4
    return {"seq": other}


def greet():
    barrier = pltpu.get_barrier_semaphore()
    for mask in (1, 2):
        pl.semaphore_signal(barrier, inc=1, device_id=partner(mask), device_id_type=MESH)
    pl.semaphore_wait(barrier, 2)


def sender(sends, recvs):
    def send(slot, source, target, mask):
        copy = pltpu.make_async_remote_copy(
            src_ref=source,
            dst_ref=target,
            send_sem=sends.at[slot],
            recv_sem=recvs.at[slot],
            device_id=partner(mask),
            device_id_type=MESH,
        )
        copy.start()
        return copy

    return send


def over_chunks(rows, run):
    def step(i, carry):
        run(pl.ds(pl.multiple_of(i * ROWS16, ROWS16), ROWS16))
        return carry

    lax.fori_loop(0, rows // ROWS16, step, 0)


def reduce_phase(product, send, first_slot, acc, sent, got):
    rows = acc.shape[1]
    half = rows // 2
    low, high = pl.ds(0, half), pl.ds(half, half)
    product(3, lambda cols, value: sent.__setitem__((0, slice(None), cols), value.astype(BF)))
    far_near = send(first_slot, sent.at[0, low], got.at[0, low], 1)
    far_side = send(first_slot + 1, sent.at[0, high], got.at[0, high], 2)
    product(1, lambda cols, value: acc.__setitem__((1, slice(None), cols), value))
    over_chunks(half, lambda r: sent.__setitem__((1, r), acc[1, r].astype(BF)))
    near_low = send(first_slot + 2, sent.at[1, low], got.at[1, low], 1)
    product(2, lambda cols, value: acc.__setitem__((2, slice(None), cols), value))

    def tail(k):
        def run(r):
            r = pl.ds(pl.multiple_of(r.start + half, ROWS16), ROWS16)
            sent[k, r] = acc[k, r].astype(BF)

        return run

    over_chunks(half, tail(2))
    side_high = send(first_slot + 3, sent.at[2, high], got.at[2, high], 2)
    far_side.wait_recv()

    def add_high(r):
        r = pl.ds(pl.multiple_of(r.start + half, ROWS16), ROWS16)
        sent[1, r] = (acc[1, r] + got[0, r].astype(F32)).astype(BF)

    over_chunks(half, add_high)
    near_high = send(first_slot + 4, sent.at[1, high], got.at[1, high], 1)
    far_near.wait_recv()

    def add_low(r):
        sent[2, r] = (acc[2, r] + got[0, r].astype(F32)).astype(BF)

    over_chunks(half, add_low)
    side_low = send(first_slot + 5, sent.at[2, low], got.at[2, low], 2)
    product(0, lambda cols, value: acc.__setitem__((0, slice(None), cols), value))
    arriving = [near_low, side_high, near_high, side_low]
    for copy in arriving:
        copy.wait_recv()
    return [far_near, far_side] + arriving


def both_ways(send, slot, source, out):
    half = source.shape[0] // 2
    low, high = pl.ds(0, half), pl.ds(half, half)
    return [
        send(slot, source.at[low], out.at[1, low], 1),
        send(slot + 1, source.at[high], out.at[2, high], 2),
        send(slot + 2, source.at[high], out.at[1, high], 1),
        send(slot + 3, source.at[low], out.at[2, low], 2),
    ]


def pass_on(send, slot, out, copies):
    half = out.shape[1] // 2
    low, high = pl.ds(0, half), pl.ds(half, half)
    copies[0].wait_recv()
    far_low = send(slot + 4, out.at[1, low], out.at[3, low], 2)
    copies[1].wait_recv()
    far_high = send(slot + 5, out.at[2, high], out.at[3, high], 1)
    return copies + [far_low, far_high]


def settle(copies):
    for copy in copies[2:]:
        copy.wait_recv()
    for copy in copies:
        copy.wait_send()


def at_seq(k):
    s = lax.axis_index("seq")
    return s if k == 0 else 3 - s if k == 3 else partner(k)["seq"]


def product_of(left, right, contract, rows, tile, ready=None):
    def product(k, store):
        def step(c, carry):
            cols = pl.ds(pl.multiple_of(c * tile, tile), tile)
            if ready is not None and k == 3:
                ready(c)
            total = None
            for a, b in zip(left, right):
                part = b[cols, :] if contract else b[:, cols]
                value = lax.dot_general(
                    a[k * rows : (k + 1) * rows, :],
                    part,
                    (((1,), (1 if contract else 0,)), ((), ())),
                    preferred_element_type=F32,
                )
                total = value if total is None else total + value
            store(cols, total)
            return carry

        width = right[0].shape[0 if contract else 1]
        lax.fori_loop(0, width // tile, step, 0)

    return product


def rms_parts(values):
    return lax.rsqrt(jnp.mean(values * values, axis=-1, keepdims=True) + 1e-06)


def stream_kernel(
    mixed_ref, weight_ref, flat_ref, gain_ref,
    stream_out, temporal_out, normed_out,
    acc, sent, got, sends, recvs,
):
    rows = flat_ref.shape[0]
    greet()
    send = sender(sends, recvs)
    copies = reduce_phase(
        product_of([mixed_ref], [weight_ref], False, rows, 512), send, 0, acc, sent, got
    )

    def finish(r):
        temporal = acc[0, r] + got[1, r].astype(F32) + got[2, r].astype(F32)
        temporal_out[r] = temporal
        stream = flat_ref[r].astype(F32) + temporal
        stream_out[r] = stream
        normed_out[0, r] = (stream * rms_parts(stream) * gain_ref[...]).astype(BF)

    over_chunks(rows, finish)
    gathered = pass_on(send, 6, normed_out, both_ways(send, 6, normed_out.at[0], normed_out))
    settle(gathered)
    for copy in copies:
        copy.wait_send()


def exchange_scratch(rows, width, copies):
    return [
        pltpu.VMEM((3, rows, width), F32),
        pltpu.VMEM((3, rows, width), BF),
        pltpu.VMEM((3, rows, width), BF),
        pltpu.SemaphoreType.DMA((copies,)),
        pltpu.SemaphoreType.DMA((copies,)),
    ]


def remote_call(kernel, name, ident, outs, operands, scratch, far=0):
    return pl.pallas_call(
        kernel,
        in_specs=[pl.BlockSpec(memory_space=pltpu.VMEM)] * (len(operands) - far)
        + [pl.BlockSpec(memory_space=pl.ANY)] * far,
        out_specs=[pl.BlockSpec(memory_space=pltpu.VMEM)] * len(outs),
        out_shape=[jax.ShapeDtypeStruct(shape, kind) for shape, kind in outs],
        scratch_shapes=scratch,
        compiler_params=pltpu.CompilerParams(
            collective_id=ident, has_side_effects=True, vmem_limit_bytes=60 * 1024 * 1024
        ),
        cost_estimate=pl.CostEstimate(flops=1000, bytes_accessed=1000, transcendentals=0),
        name=name,
    )(*operands)


def stream_and_norm(mixed, weight, flat, gain):
    rows, width = flat.shape
    groups = mixed.shape[0] // rows
    return remote_call(
        stream_kernel,
        "stream_and_norm",
        1,
        [((rows, width), F32), ((rows, width), F32), ((groups, rows, width), BF)],
        (mixed, weight, flat, gain),
        exchange_scratch(rows, width, 12),
    )


def stream_back_kernel(
    rows_ref, stream_ref, gain_ref, upstream_ref, weight_far, hidden_far, down_far,
    grad_out, low_out, gain_out, feed_out,
    weight_ref, hidden_ref, down_ref, fetches,
    acc, sent, got, sends, recvs,
):
    rows, width = stream_ref.shape
    tile = 512

    def fetch(c):
        part = pl.ds(pl.multiple_of(c * tile, tile), tile)
        return pltpu.make_async_copy(weight_far.at[part], weight_ref.at[part], fetches.at[c])

    count = width // tile
    for c in range(count):
        fetch(c).start()
    late = [
        pltpu.make_async_copy(hidden_far, hidden_ref, fetches.at[count]),
        pltpu.make_async_copy(down_far, down_ref, fetches.at[count + 1]),
    ]
    for copy in late:
        copy.start()
    greet()
    send = sender(sends, recvs)
    product = product_of(
        [rows_ref], [weight_ref], True, rows, tile, ready=lambda c: fetch(c).wait()
    )
    copies = reduce_phase(product, send, 0, acc, sent, got)
    gain_out[...] = jnp.zeros_like(gain_out)

    def finish(r):
        grad = acc[0, r] + got[1, r].astype(F32) + got[2, r].astype(F32)
        stream = stream_ref[r]
        inv = rms_parts(stream)
        scaled = grad * gain_ref[...]
        inner = jnp.mean(stream * scaled, axis=-1, keepdims=True)
        total = upstream_ref[r].astype(F32) + inv * scaled - stream * (inv * inv * inv * inner)
        grad_out[r] = total
        low_out[0, r] = total.astype(BF)
        gained = grad * stream * inv
        gain_out[...] += gained[:8] + gained[8:]

    over_chunks(rows, finish)
    gathered = both_ways(send, 6, low_out.at[0], low_out)
    for copy in late:
        copy.wait()
    feed = product_of([hidden_ref], [down_ref], False, rows, tile)

    def feed_block(k):
        feed(k, lambda cols, value: feed_out.__setitem__((k, slice(None), cols), value.astype(BF)))

    feed_block(3)
    gathered = pass_on(send, 6, low_out, gathered)
    for k in range(3):
        feed_block(k)
    settle(gathered)
    for copy in copies:
        copy.wait_send()


def stream_back(rows_all, weight, stream, gain, upstream, hidden, down):
    rows, width = stream.shape
    groups = rows_all.shape[0] // rows
    return remote_call(
        stream_back_kernel,
        "stream_back",
        2,
        [
            ((rows, width), F32),
            ((groups, rows, width), BF),
            ((8, width), F32),
            ((groups, rows, width), BF),
        ],
        (rows_all, stream, gain, upstream, weight, hidden, down),
        [
            pltpu.VMEM(weight.shape, BF),
            pltpu.VMEM(hidden.shape, BF),
            pltpu.VMEM(down.shape, BF),
            pltpu.SemaphoreType.DMA((width // 512 + 2,)),
        ]
        + exchange_scratch(rows, width, 12),
        far=3,
    )


def inputs_back_kernel(
    branch_ref, y_ref, weight_ref, flat_ref, gain_ref,
    grad_out, gain_out,
    acc, sent, got, sends, recvs,
):
    rows, width = flat_ref.shape
    greet()
    send = sender(sends, recvs)
    window = branch_ref.shape[1]
    weights = [weight_ref.at[:, :window], weight_ref.at[:, window:]]
    copies = reduce_phase(
        product_of([branch_ref, y_ref], weights, True, rows, 512), send, 0, acc, sent, got
    )
    gain_out[...] = jnp.zeros_like(gain_out)

    def finish(r):
        grad = acc[0, r] + got[1, r].astype(F32) + got[2, r].astype(F32)
        values = flat_ref[r].astype(F32)
        inv = rms_parts(values)
        scaled = grad * gain_ref[...]
        inner = jnp.mean(values * scaled, axis=-1, keepdims=True)
        grad_out[r] = inv * scaled - values * (inv * inv * inv * inner)
        gained = grad * values * inv
        gain_out[...] += gained[:8] + gained[8:]

    over_chunks(rows, finish)
    for copy in copies:
        copy.wait_send()


def inputs_back(branch_rows, y_rows, weight, flat, gain):
    rows, width = flat.shape
    return remote_call(
        inputs_back_kernel,
        "inputs_back",
        3,
        [((rows, width), F32), ((8, width), F32)],
        (branch_rows, y_rows, weight, flat, gain),
        exchange_scratch(rows, width, 6),
    )


def start_kernel(inputs_ref, inputs_out, edge_out, sends, recvs):
    seqs = edge_out.shape[1] // ROWS16
    tokens = inputs_ref.shape[0] // seqs
    w = lax.axis_index("wide")
    wide = lax.axis_size("wide")
    after, before = lax.rem(w + 1, wide), lax.rem(w + wide - 1, wide)
    barrier = pltpu.get_barrier_semaphore()
    for mask in (1, 2):
        pl.semaphore_signal(barrier, inc=1, device_id=partner(mask), device_id_type=MESH)
    pl.semaphore_signal(barrier, inc=1, device_id={"wide": before}, device_id_type=MESH)
    pl.semaphore_wait(barrier, 3)
    send = sender(sends, recvs)
    edges = []
    for q in range(seqs):
        copy = pltpu.make_async_remote_copy(
            src_ref=inputs_ref.at[pl.ds((q + 1) * tokens - ROWS16, ROWS16)],
            dst_ref=edge_out.at[0, pl.ds(q * ROWS16, ROWS16)],
            send_sem=sends.at[12 + q],
            recv_sem=recvs.at[12 + q],
            device_id={"wide": after},
            device_id_type=MESH,
        )
        copy.start()
        edges.append(copy)
    blocks = both_ways(send, 0, inputs_ref, inputs_out)
    inputs_out[0] = inputs_ref[...]
    for copy in edges:
        copy.wait_recv()
        copy.wait_send()
    edges = both_ways(send, 6, edge_out.at[0], edge_out)
    blocks = pass_on(send, 0, inputs_out, blocks)
    edges = pass_on(send, 6, edge_out, edges)
    settle(blocks)
    settle(edges)


def start(inputs, groups, seqs):
    rows, width = inputs.shape
    copies = 12 + seqs
    return remote_call(
        start_kernel,
        "start",
        6,
        [((groups, rows, width), BF), ((groups, seqs * ROWS16, width), BF)],
        (inputs,),
        [pltpu.SemaphoreType.DMA((copies,)), pltpu.SemaphoreType.DMA((copies,))],
    )


def middle_kernel(
    grad_ref, y_ref, local_ref, reach_ref, carry_ref, rate_ref, chan_ref, ends_ref,
    edge_ref, gates_ref, valid_ref, feed_ref,
    conv_far, forget_far, admit_far, x_far, stream_far, temporal_far,
    y_rows_out, branch_out, forget_out, admit_out, sums_out, result_out, squares_out,
    adjoint, later, heads, packet, packet_in, tails, after, conv_rows,
    conv_ref, forget_ref, admit_ref, x_ref, stream_ref, temporal_ref,
    sent, got, fetches, sends, recvs, head_sends, head_recvs,
):
    wide, seqs, share = ends_ref.shape
    tokens = grad_ref.shape[0] // seqs
    window = x_ref.shape[1]
    rows, width = stream_ref.shape
    half = rows // 2
    low, high = pl.ds(0, half), pl.ds(half, half)
    w = lax.axis_index("wide")
    first_channel = lax.axis_index("seq") * share
    base = jnp.minimum(first_channel // BW * BW, lax.axis_size("seq") * share - window)
    off = pl.multiple_of(first_channel - base, LANES)
    fetched = []
    for i, (far, near) in enumerate(
        (
            (conv_far, conv_ref),
            (forget_far, forget_ref),
            (admit_far, admit_ref),
            (x_far, x_ref),
            (stream_far, stream_ref),
            (temporal_far, temporal_ref),
        )
    ):
        copy = pltpu.make_async_copy(far, near, fetches.at[i])
        copy.start()
        fetched.append(copy)

    barrier = pltpu.get_barrier_semaphore()
    for mask in (1, 2):
        pl.semaphore_signal(barrier, inc=1, device_id=partner(mask), device_id_type=MESH)

    def tell(i, carry):
        other = lax.rem(w + i, wide)
        pl.semaphore_signal(barrier, inc=1, device_id={"wide": other}, device_id_type=MESH)
        return carry

    lax.fori_loop(1, wide, tell, 0)
    pl.semaphore_wait(barrier, wide + 1)
    send = sender(sends, recvs)
    far_near = send(0, feed_ref.at[3, low], got.at[0, low], 1)
    far_side = send(1, feed_ref.at[3, high], got.at[0, high], 2)
    near_low = send(2, feed_ref.at[1, low], got.at[1, low], 1)
    side_high = send(3, feed_ref.at[2, high], got.at[2, high], 2)

    row = lax.broadcasted_iota(jnp.int32, (tokens, LANES), 0)
    fetched[1].wait()
    fetched[2].wait()

    def scan_step(q, carry):
        r = pl.ds(pl.multiple_of(q * tokens, tokens), tokens)
        head_rows = pl.ds(pl.multiple_of(q * tokens, tokens), ROWS16)
        for j in range(share // LANES):
            lanes = slice(j * LANES, (j + 1) * LANES)
            grad = grad_ref[r, lanes]
            value, slope = gelu_parts(y_ref[r, lanes])
            state = (local_ref[r, lanes] + reach_ref[r, lanes] * carry_ref[q, :, lanes]).astype(BF)
            y_rows_out[r, lanes] = (grad * state.astype(F32) * slope).astype(BF)
            state_grad = (grad * value).astype(BF).astype(F32)
            rate = rate_ref[r, lanes]
            ahead = jnp.where(row == tokens - 1, 1.0, pltpu.roll(rate, tokens - 1, 0))
            adjoints, laters = scan_rows(ahead, state_grad, True)
            adjoint[r, lanes] = adjoints
            later[r, lanes] = laters
            tails[q, :, lanes] = rate[:1] * adjoints[:1]
            forget_sig = sigmoid(forget_ref[head_rows, lanes].astype(F32)[:HALO])
            admit_sig = sigmoid(admit_ref[head_rows, lanes].astype(F32)[:HALO])
            rate_log = -8.0 * chan_ref[2:3, lanes] * (0.1 + 0.9 * forget_sig)
            gain = jnp.sqrt(drop_of(rate_log)) * admit_sig
            for i, values in enumerate((adjoints[:HALO] * gain, laters[:HALO] * gain)):
                for t in range(CONV - 1):
                    packet[i, t, q, :, lanes] = values[t : t + 1]
        return carry

    lax.fori_loop(0, seqs, scan_step, 0)
    for q in range(seqs):
        heads[0, q : q + 1, :] = tails[q]

    def head_copy(i):
        return pltpu.make_async_remote_copy(
            src_ref=heads.at[0],
            dst_ref=heads.at[i],
            send_sem=head_sends.at[i],
            recv_sem=head_recvs.at[i],
            device_id={"wide": lax.rem(w + i, wide)},
            device_id_type=MESH,
        )

    def head_start(i, carry):
        head_copy(i).start()
        return carry

    def head_wait(i, carry):
        copy = head_copy(i)
        copy.wait_recv()
        copy.wait_send()
        return carry

    lax.fori_loop(1, wide, head_start, 0)
    packets = pltpu.make_async_remote_copy(
        src_ref=packet,
        dst_ref=packet_in,
        send_sem=sends.at[6],
        recv_sem=recvs.at[6],
        device_id={"wide": lax.rem(w + wide - 1, wide)},
        device_id_type=MESH,
    )
    packets.start()

    far_side.wait_recv()
    sent[0] = (feed_ref[1, high].astype(F32) + got[0, high].astype(F32)).astype(BF)
    near_high = send(4, sent.at[0], got.at[1, high], 1)
    far_near.wait_recv()
    sent[1] = (feed_ref[2, low].astype(F32) + got[0, low].astype(F32)).astype(BF)
    side_low = send(5, sent.at[1], got.at[2, low], 2)

    lax.fori_loop(1, wide, head_wait, 0)
    packets.wait_recv()
    packets.wait_send()

    def tail_step(i, carry):
        tail, next_tail = carry
        j = wide - i
        stepped = ends_ref[j] * tail + heads[lax.rem(w + i, wide)]
        return jnp.where(j > w, stepped, tail), jnp.where(j > w + 1, stepped, next_tail)

    zero = jnp.zeros((seqs, share), F32)
    tail, next_tail = lax.fori_loop(1, wide, tail_step, (zero, zero))
    next_tail = jnp.where(w == wide - 1, 0.0, next_tail)
    inside = jnp.where(w == wide - 1, 0.0, 1.0)
    after[...] = jnp.zeros_like(after)
    for q in range(seqs):
        tails[q] = tail[q : q + 1]
        for t in range(CONV - 1):
            after[q * HALO + t : q * HALO + t + 1, :] = (
                inside * packet_in[0, t, q] + packet_in[1, t, q] * next_tail[q : q + 1]
            )

    forget_out[...] = jnp.zeros_like(forget_out)
    admit_out[...] = jnp.zeros_like(admit_out)
    conv_rows[...] = jnp.zeros_like(conv_rows)
    sums_out[...] = jnp.zeros_like(sums_out)
    fetched[0].wait()
    fetched[3].wait()

    def rows_step(q, carry):
        r = pl.ds(pl.multiple_of(q * tokens, tokens), tokens)
        pack = pl.ds(pl.multiple_of(q * HALO, HALO), HALO)
        for j in range(share // LANES):
            lanes = slice(j * LANES, (j + 1) * LANES)
            here = pl.ds(pl.multiple_of(off + j * LANES, LANES), LANES)
            chan = [chan_ref[i : i + 1, lanes] for i in range(8)]
            start = carry_ref[q, :, lanes]
            carried = local_ref[r, lanes] + reach_ref[r, lanes] * start
            before = jnp.where(row == 0, start, pltpu.roll(carried, 1, 0))
            full = adjoint[r, lanes] + later[r, lanes] * tails[q, :, lanes]
            forget_sig = sigmoid(forget_ref[r, lanes].astype(F32))
            admit_sig = sigmoid(admit_ref[r, lanes].astype(F32))
            span = 0.1 + 0.9 * forget_sig
            rate = rate_ref[r, lanes]
            scale = jnp.sqrt(drop_of(-8.0 * chan[2] * span))
            gated = admit_sig * conv_ref[r, lanes]
            log_grad = full * (rate * before - rate * rate / scale * gated)
            conv_grad = full * scale * admit_sig
            forget_rows = (
                log_grad * (-7.2) * chan[2] * forget_sig * (1.0 - forget_sig)
            ).astype(BF)
            admit_rows = (full * scale * gated * (1.0 - admit_sig)).astype(BF)
            forget_out[r, here] = forget_rows
            admit_out[r, here] = admit_rows
            ahead = jnp.concatenate([conv_grad, after[pack, lanes]], axis=0)
            back = chan[4] * conv_grad
            for k in range(1, CONV):
                back = back + chan[4 + k] * pltpu.roll(ahead, tokens + HALO - k, 0)[:tokens]
            conv_rows[:, here] = back.astype(BF).astype(F32)
            padded = jnp.concatenate(
                [edge_ref[pack, here], x_ref[r, here].astype(F32)], axis=0
            )
            sums = [
                forget_rows.astype(F32),
                admit_rows.astype(F32),
                log_grad * (-8.0) * span,
                conv_grad,
                conv_grad * padded[HALO:],
            ] + [conv_grad * pltpu.roll(padded, k, 0)[HALO:] for k in range(1, CONV)]
            sums_out[:, lanes] += jnp.concatenate(
                [jnp.sum(v, axis=0, keepdims=True) for v in sums], axis=0
            )
        for b in range(window // BW):
            cols = slice(b * BW, (b + 1) * BW)
            back = conv_rows[:, cols]
            for source, at in ((forget_out, 0), (admit_out, BW)):
                back = back + lax.dot_general(
                    source[r, cols],
                    gates_ref[cols, at : at + BW],
                    (((1,), (1,)), ((), ())),
                    preferred_element_type=F32,
                )
            branch_out[r, cols] = back.astype(BF)
        return carry

    lax.fori_loop(0, seqs, rows_step, 0)
    fetched[4].wait()
    fetched[5].wait()
    for copy in (near_low, side_high, near_high, side_low):
        copy.wait_recv()
    squares_out[...] = jnp.zeros_like(squares_out)

    def finish(r):
        feed = feed_ref[0, r].astype(F32) + got[1, r].astype(F32) + got[2, r].astype(F32)
        result = stream_ref[r] + feed
        result_out[r] = result
        valid = valid_ref[r]
        for i, values in enumerate((result, temporal_ref[r], feed)):
            square = valid * values * values
            squares_out[i] += square[:8] + square[8:]

    over_chunks(rows, finish)
    for copy in (far_near, far_side, near_low, side_high, near_high, side_low):
        copy.wait_send()


def middle(
    grad, y, local, reach, carry, rate, chan, ends, edge, gates, valid, feed,
    conv, forget, admit, x_win, stream, temporal,
):
    total, share = grad.shape
    window = x_win.shape[1]
    rows, width = stream.shape
    wide, seqs = ends.shape[:2]
    tokens = total // seqs
    vmem = pl.BlockSpec(memory_space=pltpu.VMEM)
    anywhere = pl.BlockSpec(memory_space=pl.ANY)
    outs = [
        ((total, share), BF),
        ((total, window), BF),
        ((total, window), BF),
        ((total, window), BF),
        ((8, share), F32),
        ((rows, width), F32),
        ((3, 8, width), F32),
    ]
    return pl.pallas_call(
        middle_kernel,
        in_specs=[vmem] * 12 + [anywhere] * 6,
        out_specs=[vmem] * len(outs),
        out_shape=[jax.ShapeDtypeStruct(shape, kind) for shape, kind in outs],
        scratch_shapes=[
            pltpu.VMEM((total, share), F32),
            pltpu.VMEM((total, share), F32),
            pltpu.VMEM((wide, seqs, share), F32),
            pltpu.VMEM((2, CONV - 1, seqs, 1, share), F32),
            pltpu.VMEM((2, CONV - 1, seqs, 1, share), F32),
            pltpu.VMEM((seqs, 1, share), F32),
            pltpu.VMEM((seqs * HALO, share), F32),
            pltpu.VMEM((tokens, window), F32),
            pltpu.VMEM((total, share), F32),
            pltpu.VMEM((total, share), BF),
            pltpu.VMEM((total, share), BF),
            pltpu.VMEM((total, window), BF),
            pltpu.VMEM((rows, width), F32),
            pltpu.VMEM((rows, width), F32),
            pltpu.VMEM((2, rows // 2, width), BF),
            pltpu.VMEM((3, rows, width), BF),
            pltpu.SemaphoreType.DMA((6,)),
            pltpu.SemaphoreType.DMA((7,)),
            pltpu.SemaphoreType.DMA((7,)),
            pltpu.SemaphoreType.DMA((wide,)),
            pltpu.SemaphoreType.DMA((wide,)),
        ],
        compiler_params=pltpu.CompilerParams(
            collective_id=7, has_side_effects=True, vmem_limit_bytes=60 * 1024 * 1024
        ),
        cost_estimate=pl.CostEstimate(flops=1000, bytes_accessed=1000, transcendentals=0),
        name="middle",
    )(
        grad, y, local, reach, carry[:, None, :], rate, chan, ends, edge, gates, valid, feed,
        conv, forget, admit, x_win, stream, temporal,
    )


def place(k, block, buffer, plan, outs):
    buffer[...] = block[...].astype(F32)
    other = at_seq(k)
    for (first, count, tiles, starts), out in zip(plan, outs):
        base = other * 0
        for j, start_col in enumerate(starts):
            base = jnp.where(other == j, start_col, base)
        for i in range(tiles):
            cols = pl.ds(pl.multiple_of(base + i * LANES, LANES), LANES)
            out[:, cols] += buffer[first + i * count : first + (i + 1) * count, :]


def spread_kernel(first_ref, second_ref, first_out, second_out, first_blocks, second_blocks, sends, recvs):
    greet()
    send = sender(sends, recvs)
    first = both_ways(send, 0, first_ref, first_blocks)
    second = both_ways(send, 6, second_ref, second_blocks)

    def put(k, block, out):
        columns = block.shape[1]
        other = at_seq(k)
        for i in range(columns // LANES):
            start_col = pl.multiple_of(other * columns + i * LANES, LANES)
            out[:, pl.ds(start_col, LANES)] = block[:, i * LANES : (i + 1) * LANES]

    put(0, first_ref, first_out)
    put(0, second_ref, second_out)
    first = pass_on(send, 0, first_blocks, first)
    second = pass_on(send, 6, second_blocks, second)
    settle(first)
    for k in (1, 2, 3):
        put(k, first_blocks.at[k], first_out)
    settle(second)
    for k in (1, 2, 3):
        put(k, second_blocks.at[k], second_out)


def spread(first, second, groups):
    counts = [first.shape[0], second.shape[0]]
    first, second = (jnp.pad(v, ((0, -v.shape[0] % 32), (0, 0))) for v in (first, second))
    wholes = remote_call(
        spread_kernel,
        "spread",
        8,
        [((v.shape[0], groups * v.shape[1]), BF) for v in (first, second)],
        (first, second),
        [
            pltpu.VMEM((groups,) + first.shape, BF),
            pltpu.VMEM((groups,) + second.shape, BF),
            pltpu.SemaphoreType.DMA((12,)),
            pltpu.SemaphoreType.DMA((12,)),
        ],
    )
    return [v[:count] for v, count in zip(wholes, counts)]


def last_kernel(
    plan, parts_ref, sums_ref,
    first_out, second_out, sums_out,
    blocks, buffer, total, got_sums, sends, recvs, sum_sends, sum_recvs,
):
    wide = sums_ref.shape[0]
    w = lax.axis_index("wide")
    barrier = pltpu.get_barrier_semaphore()
    for mask in (1, 2):
        pl.semaphore_signal(barrier, inc=1, device_id=partner(mask), device_id_type=MESH)

    def tell(i, carry):
        other = lax.rem(w + i, wide)
        pl.semaphore_signal(barrier, inc=1, device_id={"wide": other}, device_id_type=MESH)
        return carry

    lax.fori_loop(1, wide, tell, 0)
    pl.semaphore_wait(barrier, wide + 1)
    send = sender(sends, recvs)
    copies = both_ways(send, 0, parts_ref, blocks)

    def chunk(i):
        other = lax.rem(w + i, wide)
        return pltpu.make_async_remote_copy(
            src_ref=sums_ref.at[other],
            dst_ref=got_sums.at[i],
            send_sem=sum_sends.at[i],
            recv_sem=sum_recvs.at[i],
            device_id={"wide": other},
            device_id_type=MESH,
        )

    def begin(i, carry):
        chunk(i).start()
        return carry

    def finish(i, carry):
        copy = chunk(i)
        copy.wait_recv()
        copy.wait_send()
        return carry + got_sums[i]

    lax.fori_loop(1, wide, begin, 0)
    outs = (first_out, second_out)
    for out in outs:
        out[...] = jnp.zeros_like(out)
    place(0, parts_ref, buffer, plan, outs)
    total[0] = lax.fori_loop(1, wide, finish, sums_ref[w])
    to_near = send(6, total.at[0], total.at[1], 1)
    copies = pass_on(send, 0, blocks, copies)
    to_near.wait_recv()
    total[2] = total[0] + total[1]
    to_side = send(7, total.at[2], total.at[3], 2)
    settle(copies)
    for k in (1, 2, 3):
        place(k, blocks.at[k], buffer, plan, outs)
    to_side.wait_recv()
    sums_out[...] = total[2] + total[3]
    to_near.wait_send()
    to_side.wait_send()


def spread_last(parts, sums, plan, shapes):
    wide, count, _unused = sums.shape
    return remote_call(
        functools.partial(last_kernel, plan),
        "spread_last",
        5,
        [(shape, F32) for shape in shapes] + [((count, LANES), F32)],
        (parts, sums),
        [
            pltpu.VMEM((4,) + parts.shape, BF),
            pltpu.VMEM(parts.shape, F32),
            pltpu.VMEM((4, count, LANES), F32),
            pltpu.VMEM((wide, count, LANES), F32),
            pltpu.SemaphoreType.DMA((8,)),
            pltpu.SemaphoreType.DMA((8,)),
            pltpu.SemaphoreType.DMA((wide,)),
            pltpu.SemaphoreType.DMA((wide,)),
        ],
    )


def body(
    inputs,
    lengths,
    norm_gain,
    gelu_weight,
    branch_weight,
    forget_gates,
    admit_gates,
    forget_bias,
    admit_bias,
    decay_rate,
    conv_weight,
    conv_bias,
    out_weight,
    mlp_gain,
    gate_weight,
    up_weight,
    down_weight,
    cotangent,
):
    groups = lax.axis_size("seq")
    wide = lax.axis_size("wide")
    s = lax.axis_index("seq")
    w = lax.axis_index("wide")
    seqs, tokens, width = inputs.shape
    rows = seqs * tokens
    total = groups * rows
    all_seqs = groups * seqs
    channels = gelu_weight.shape[1]
    share = channels // groups
    window = (share + BW - 1) // BW * BW
    blocks = window // BW

    def base_of(index):
        return jnp.minimum(index * share // BW * BW, channels - window)

    base = base_of(s)
    off = s * share - base
    quarter = width // groups
    gate_cols = 2 * BW // groups

    flat_low = inputs.reshape(rows, width)
    upstream = cotangent.reshape(rows, width)
    all_low, edge_low = start(flat_low, groups, seqs)
    all_low = all_low.reshape(total, width)
    edge_low = jnp.where(w == 0, 0.0, edge_low.reshape(all_seqs * ROWS16, width).astype(F32))

    x_y_cols = lax.all_gather(
        jnp.concatenate(
            [
                lax.dynamic_slice_in_dim(branch_weight, base, window, 1),
                lax.dynamic_slice_in_dim(gelu_weight, s * share, share, 1),
            ],
            axis=1,
        ),
        "wide",
        axis=0,
        tiled=True,
    )
    dw, rw = width // wide, channels // wide
    small = jnp.concatenate(
        [norm_gain, mlp_gain, forget_bias, admit_bias, decay_rate, conv_bias, conv_weight.reshape(-1)]
    ).reshape(-1, gate_cols)
    gates_quarter = jnp.concatenate([forget_gates, admit_gates], axis=1)
    small = jnp.concatenate(
        [lax.dynamic_slice_in_dim(gates_quarter, s * gate_cols, gate_cols, 1), small], axis=0
    )
    small, edge_low, later_upstream = lax.optimization_barrier((small, edge_low, upstream))
    upstream_near = swap(later_upstream, 1)
    upstream_side = swap(later_upstream, 2)
    small = lax.all_gather(small, "wide")
    gates_quarter = small[:, :rw].reshape(channels, gate_cols)
    small = small[:, rw:].reshape(wide, -1).astype(F32)
    gain_one = small[:, :dw].reshape(1, width)
    gain_two = small[:, dw : 2 * dw].reshape(1, width)
    per_channel = small[:, 2 * dw :].reshape(wide, 8, rw).transpose(1, 0, 2).reshape(8, channels)
    per_channel = lax.dynamic_slice_in_dim(per_channel, s * share, share, 1)

    out_quarter = lax.all_gather(
        lax.dynamic_slice_in_dim(out_weight, s * quarter, quarter, 1), "wide", axis=0, tiled=True
    )
    mlp_full = lax.all_gather(
        jnp.concatenate([gate_weight, up_weight], axis=1), "wide", axis=0, tiled=True
    )
    down_full = lax.all_gather(down_weight, "wide", axis=1, tiled=True)
    hidden_units = gate_weight.shape[1]

    def in_order(parts):
        near = [jnp.where(s % 2 == 1, parts[k ^ 1], parts[k]) for k in range(groups)]
        return [jnp.where(s // 2 == 1, near[k ^ 2], near[k]) for k in range(groups)]

    def swapped(part_of):
        return [swap(part_of(s ^ k), k) if k else part_of(s) for k in range(groups)]

    gates = jnp.concatenate(
        in_order(
            swapped(lambda j: lax.dynamic_slice_in_dim(gates_quarter, base_of(j), window, 0))
        ),
        axis=1,
    )
    normed_all = rms_norm(all_low.astype(F32), gain_one).astype(BF)
    normed_edge = rms_norm(edge_low, gain_one).astype(BF)
    normed_all, upstream_near, upstream_side = lax.optimization_barrier(
        (normed_all, upstream_near, upstream_side)
    )
    half = rows // 2
    upstream_far = [swap(upstream_near[:half], 2), swap(upstream_side[half:], 1)]

    x_y = dot(normed_all, x_y_cols)
    x_win = x_y[:, :window].astype(BF)
    branch_y = x_y[:, window:]
    x_win, out_quarter, *upstream_far = lax.optimization_barrier(
        (x_win, out_quarter, *upstream_far)
    )
    upstream_all = jnp.concatenate([upstream, upstream_near, upstream_side, *upstream_far], axis=0)
    out_rows = jnp.concatenate(
        in_order(swapped(lambda j: lax.dynamic_slice_in_dim(out_quarter, j * share, share, 0))),
        axis=1,
    )
    edge_win = dot(normed_edge, x_y_cols[:, :window]).astype(BF).astype(F32)
    edge_win = edge_win.reshape(all_seqs, ROWS16, window)[:, ROWS16 - HALO :]
    edge_win = edge_win.reshape(all_seqs * HALO, window)
    offset = off.reshape(1)
    forget, admit, conv_out, rate, local, reach, ends = temporal_forward(
        offset, x_win, edge_win, gates, per_channel, tokens
    )
    ends = lax.all_gather(ends, "wide")[:, :, :, 0]
    carry = jnp.zeros((all_seqs, share), F32)
    for j in range(wide - 1):
        carry = jnp.where(j < w, ends[j, :, 0] * carry + ends[j, :, 1], carry)
    carried = local.reshape(all_seqs, tokens, share) + reach.reshape(
        all_seqs, tokens, share
    ) * carry[:, None, :]
    state = carried.astype(BF).astype(F32).reshape(total, share)

    gelu_y = jax.nn.gelu(branch_y)
    mixed_low = (state * gelu_y).astype(BF)
    stream, temporal, normed_two_all = stream_and_norm(mixed_low, out_rows, flat_low, gain_two)
    normed_two_all = normed_two_all.reshape(total, width)

    gate_up = dot(normed_two_all, mlp_full)
    gate, up_values = gate_up[:, :hidden_units], gate_up[:, hidden_units:]
    gelu_gate = jax.nn.gelu(gate)
    hidden_low = (gelu_gate * up_values).astype(BF)
    down_part = contract_rows(hidden_low, upstream_all).astype(BF)
    hidden_low, down_part, upstream_low = lax.optimization_barrier(
        (hidden_low, down_part, upstream_all)
    )
    down_grad = lax.psum_scatter(down_part, "wide", scatter_dimension=1, tiled=True)
    hidden_grad = contract_last(upstream_low, down_full)
    gate_rows = (hidden_grad * up_values * gelu_parts(gate)[1]).astype(BF)
    up_rows = (hidden_grad * gelu_gate).astype(BF)
    mlp_rows = jnp.concatenate([gate_rows, up_rows], axis=1)
    mlp_part = contract_rows(normed_two_all, mlp_rows).astype(BF)
    mlp_rows, mlp_part = lax.optimization_barrier((mlp_rows, mlp_part))
    mlp_grad = lax.psum_scatter(mlp_part, "wide", scatter_dimension=0, tiled=True)
    stream_grad, stream_low_all, gain_two_grad, feed_parts = stream_back(
        mlp_rows, mlp_full, stream, gain_two, upstream, hidden_low, down_full
    )
    gain_two_grad = jnp.sum(gain_two_grad, axis=0)
    stream_low_all = stream_low_all.reshape(total, width)
    stream_low_all, down_grad = lax.optimization_barrier((stream_low_all, down_grad))
    mixed_grad = contract_last(stream_low_all, out_rows)
    out_grad = contract_rows(mixed_low, stream_low_all).astype(BF)
    mixed_grad, out_grad = lax.optimization_barrier((mixed_grad, out_grad))
    out_parts = swapped(lambda j: lax.dynamic_slice_in_dim(out_grad, j * quarter, quarter, 1))
    position = w * tokens + jnp.arange(tokens, dtype=jnp.int32)
    valid = (position[None, :] < lengths[:, None]).astype(F32).reshape(rows, 1)
    y_rows, branch_rows, forget_win, admit_win, channel_grads, result, squares = middle(
        mixed_grad, branch_y, local, reach, carry, rate, per_channel, ends[:, :, 0],
        edge_win, gates, valid, feed_parts, conv_out, forget, admit, x_win, stream, temporal,
    )
    y_rows, branch_rows, *out_parts = lax.optimization_barrier((y_rows, branch_rows, *out_parts))
    out_cols = jnp.concatenate(in_order(out_parts), axis=0)
    partial_sums = jnp.concatenate([jnp.sum(squares, axis=(1, 2)), jnp.sum(valid).reshape(1)])

    bases = [min(j * share // BW * BW, channels - window) for j in range(groups)]

    def placed(parts, axis):
        rest = [
            tuple(
                (bases[j], channels - window - bases[j]) if d == axis else (0, 0) for d in range(2)
            )
            for j in range(groups)
        ]
        return sum(jnp.pad(p.astype(F32), r) for p, r in zip(parts, rest))

    def stack(values):
        values = values.reshape(wide, values.shape[0] // wide, values.shape[1])
        tiles = values.shape[2] // LANES
        return jnp.concatenate(
            [values[:, :, i * LANES : (i + 1) * LANES] for i in range(tiles)], axis=1
        )

    gelu_part = contract_rows(normed_all, y_rows).astype(BF)

    gate_grads = jnp.concatenate(
        [
            jnp.einsum(
                "tki,tkj->kij",
                x_win.reshape(total, blocks, BW),
                rows_win.reshape(total, blocks, BW),
                preferred_element_type=F32,
            ).reshape(window, BW)
            for rows_win in (forget_win, admit_win)
        ],
        axis=1,
    ).astype(BF)
    branch_part = contract_rows(normed_all, branch_rows).astype(BF)
    def sum_over_wide(values):
        return lax.psum_scatter(values, "wide", scatter_dimension=0, tiled=True)

    out_cols, gelu_part = lax.optimization_barrier((out_cols, gelu_part))
    gate_cols_grad = placed(
        in_order(
            swapped(lambda j: lax.dynamic_slice_in_dim(gate_grads, j * gate_cols, gate_cols, 1))
        ),
        0,
    ).astype(BF)
    out_sum = sum_over_wide(out_cols)
    gelu_sum = sum_over_wide(gelu_part)
    pieces = [(branch_part, window), (gate_cols_grad, gate_cols)]
    stacked = jnp.concatenate([stack(values) for values, _unused in pieces], axis=1)
    stacked = jnp.pad(stacked, ((0, 0), (0, -stacked.shape[1] % 32), (0, 0)))
    stacked, mlp_grad = lax.optimization_barrier((stacked, mlp_grad))
    first_back, gain_one_grad = inputs_back(
        branch_rows, y_rows, x_y_cols, flat_low, gain_one
    )
    gelu_sum, gain_one_grad = lax.optimization_barrier((gelu_sum, gain_one_grad))
    last_sum = sum_over_wide(stacked)

    def plan_of(pieces, starts):
        plan, at = [], 0
        for (values, columns), cols in zip(pieces, starts):
            count = values.shape[0] // wide
            plan.append((at, count, columns // LANES, tuple(cols)))
            at += count * columns // LANES
        return tuple(plan)

    out_whole, gelu_whole = spread(out_sum, gelu_sum, groups)
    earlier = lax.optimization_barrier(
        (
            last_sum,
            result.astype(BF).reshape(seqs, tokens, width),
            (stream_grad + first_back).reshape(seqs, tokens, width),
            gelu_whole.astype(F32),
            out_whole.astype(F32),
            mlp_grad[:, :hidden_units].astype(F32),
            mlp_grad[:, hidden_units:].astype(F32),
            down_grad.astype(F32),
        )
    )
    last_sum, output, inputs_grad, gelu_whole, out_whole, gate_grad, up_grad, down_grad = earlier

    channel_all = lax.dynamic_update_slice_in_dim(
        jnp.zeros((8, channels), F32), channel_grads, s * share, 1
    )
    sums = jnp.concatenate(
        [
            channel_all.reshape(8, wide, rw).transpose(1, 0, 2).reshape(wide, 8 * rw),
            jnp.sum(gain_one_grad, axis=0).reshape(wide, dw),
            gain_two_grad.reshape(wide, dw),
            jnp.tile(partial_sums[None, :], (wide, 1)),
        ],
        axis=1,
    )
    sums = jnp.pad(sums, ((0, 0), (0, -sums.shape[1] % (8 * LANES)))).reshape(wide, -1, LANES)
    branch_whole, gates_whole, sums = spread_last(
        last_sum[0],
        sums,
        plan_of(pieces, (bases, [j * gate_cols for j in range(groups)])),
        ((dw, channels), (rw, 2 * BW)),
    )
    sums = sums.reshape(-1)
    channel_sums = sums[: 8 * rw].reshape(8, rw)
    gain_sums = sums[8 * rw : 8 * rw + 2 * dw].reshape(2, dw)
    totals = sums[8 * rw + 2 * dw : 8 * rw + 2 * dw + 4]

    statistics = jnp.sqrt(totals[0:3] / (totals[3] * width))
    return (
        output,
        inputs_grad,
        gain_sums[0],
        gelu_whole,
        branch_whole,
        gates_whole[:, :BW],
        gates_whole[:, BW:],
        channel_sums[0],
        channel_sums[1],
        channel_sums[2],
        channel_sums[4:8],
        channel_sums[3],
        out_whole,
        gain_sums[1],
        gate_grad,
        up_grad,
        down_grad,
        statistics,
    )


def solution(mesh):
    in_specs = (
        P("seq", "wide", None),
        P("seq"),
        P("wide"),
        P("wide", None),
        P("wide", None),
        P("wide", None),
        P("wide", None),
        P("wide"),
        P("wide"),
        P("wide"),
        P(None, "wide"),
        P("wide"),
        P("wide", None),
        P("wide"),
        P("wide", "seq"),
        P("wide", "seq"),
        P("seq", "wide"),
        P("seq", "wide", None),
    )
    out_specs = (
        P("seq", "wide", None),
        P("seq", "wide", None),
        P("wide"),
        P("wide", None),
        P("wide", None),
        P("wide", None),
        P("wide", None),
        P("wide"),
        P("wide"),
        P("wide"),
        P(None, "wide"),
        P("wide"),
        P("wide", None),
        P("wide"),
        P("wide", "seq"),
        P("wide", "seq"),
        P("seq", "wide"),
        P(),
    )
    return jax.shard_map(body, mesh=mesh, in_specs=in_specs, out_specs=out_specs, check_vma=False)
```

```python
import functools

import jax
import jax.numpy as jnp
from jax import lax
from jax.experimental import pallas as pl
from jax.experimental.pallas import tpu as pltpu
from jax.sharding import PartitionSpec as P

BW = 256
CONV = 4
HALO = 8
BF = jnp.bfloat16
F32 = jnp.float32
LANES = 128
ROWS16 = 16
MESH = pl.DeviceIdType.MESH


def dot(left, right):
    return jnp.dot(left, right, preferred_element_type=F32)


def contract_last(left, right):
    return lax.dot_general(left, right, (((1,), (1,)), ((), ())), preferred_element_type=F32)


def contract_rows(left, right):
    return lax.dot_general(left, right, (((0,), (0,)), ((), ())), preferred_element_type=F32)


def swap(values, mask):
    return lax.ppermute(values, "seq", [(i, i ^ mask) for i in range(lax.axis_size("seq"))])


def inverse_rms(values):
    return lax.rsqrt(jnp.mean(values * values, axis=-1, keepdims=True) + 1e-06)


def rms_norm(values, gain):
    return values * inverse_rms(values) * gain


def sigmoid(values):
    return 0.5 * jnp.tanh(0.5 * values) + 0.5


def gelu_parts(values):
    c = 0.7978845608028654
    sq = values * values
    t = jnp.tanh(c * values * (1.0 + 0.044715 * sq))
    half = 0.5 * (1.0 + t)
    return values * half, half + 0.5 * values * (1.0 - t * t) * (c * (1.0 + 3.0 * 0.044715 * sq))


def drop_of(rate_log):
    u = 2.0 * rate_log
    series = 1.0 + u * (1.0 / 8.0)
    for n in (7, 6, 5, 4, 3, 2):
        series = 1.0 + u * series * (1.0 / n)
    return jnp.where(u > -0.4, -u * series, 1.0 - jnp.exp(u))


def scan_rows(rate, drive, reverse):
    rows, lanes = rate.shape
    count = rows // 8
    rate = rate.reshape(count, 8, lanes)
    drive = drive.reshape(count, 8, lanes)
    row = lax.broadcasted_iota(jnp.int32, (count, 8, lanes), 1)
    for step in (1, 2, 4):
        shift = 8 - step if reverse else step
        keep = row < 8 - step if reverse else row >= step
        drive = drive + rate * jnp.where(keep, pltpu.roll(drive, shift, 1), 0.0)
        rate = rate * jnp.where(keep, pltpu.roll(rate, shift, 1), 1.0)
    state, reach = jnp.zeros((1, lanes), F32), jnp.ones((1, lanes), F32)
    states, reaches = [None] * count, [None] * count
    last = 0 if reverse else 7
    for i in reversed(range(count)) if reverse else range(count):
        states[i] = drive[i] + rate[i] * state
        reaches[i] = rate[i] * reach
        state = states[i][last : last + 1]
        reach = reaches[i][last : last + 1]
    return jnp.concatenate(states, axis=0), jnp.concatenate(reaches, axis=0)


def forward_kernel(
    off_ref, x_ref, edge_ref, gates_ref, chan_ref,
    forget_out, admit_out, conv_out_ref, rate_out, local_out, reach_out, ends_out,
    logits,
):
    q = pl.program_id(0)
    tokens = x_ref.shape[0]
    share = chan_ref.shape[1]
    blocks = x_ref.shape[1] // BW
    off = pl.multiple_of(off_ref[0], LANES)
    for b in range(blocks):
        cols = slice(b * BW, (b + 1) * BW)
        mixed = jnp.dot(x_ref[:, cols], gates_ref[cols, :], preferred_element_type=F32)
        logits[0, :, cols] = mixed[:, :BW]
        logits[1, :, cols] = mixed[:, BW:]
    for j in range(share // LANES):
        lanes = slice(j * LANES, (j + 1) * LANES)
        here = pl.ds(pl.multiple_of(off + j * LANES, LANES), LANES)
        chan = [chan_ref[i : i + 1, lanes] for i in range(8)]
        forget = (logits[0, :, here] + chan[0]).astype(BF)
        admit = (logits[1, :, here] + chan[1]).astype(BF)
        forget_out[:, lanes] = forget
        admit_out[:, lanes] = admit
        edge = edge_ref[pl.ds(pl.multiple_of(q * HALO, HALO), HALO), here]
        padded = jnp.concatenate([edge, x_ref[:, here].astype(F32)], axis=0)
        conv = chan[3] + chan[4] * padded[HALO:]
        for k in range(1, CONV):
            conv = conv + chan[4 + k] * pltpu.roll(padded, k, 0)[HALO:]
        conv_out_ref[:, lanes] = conv
        rate_log = -8.0 * chan[2] * (0.1 + 0.9 * sigmoid(forget.astype(F32)))
        rate = jnp.exp(rate_log)
        drive = jnp.sqrt(drop_of(rate_log)) * sigmoid(admit.astype(F32)) * conv
        state, reach = scan_rows(rate, drive, False)
        rate_out[:, lanes] = rate
        local_out[:, lanes] = state
        reach_out[:, lanes] = reach
        ends_out[0, 0, :, lanes] = reach[tokens - 1 :]
        ends_out[0, 1, :, lanes] = state[tokens - 1 :]


def whole(shape):
    return pl.BlockSpec(shape, lambda q: (0,) * len(shape))


def per_seq(width):
    return pl.BlockSpec((1, 1, width), lambda q: (q, 0, 0))


def temporal_forward(off, x_win, edge, gates, chan, tokens):
    total, window = x_win.shape
    share = chan.shape[1]
    seqs = total // tokens
    part = lambda width: pl.BlockSpec((tokens, width), lambda q: (q, 0))
    return pl.pallas_call(
        forward_kernel,
        grid=(seqs,),
        in_specs=[
            pl.BlockSpec(memory_space=pltpu.SMEM),
            part(window),
            whole(edge.shape),
            whole(gates.shape),
            whole(chan.shape),
        ],
        out_specs=[
            part(share), part(share), part(share), part(share), part(share), part(share),
            pl.BlockSpec((1, 2, 1, share), lambda q: (q, 0, 0, 0)),
        ],
        out_shape=[
            jax.ShapeDtypeStruct((total, share), BF),
            jax.ShapeDtypeStruct((total, share), BF),
            jax.ShapeDtypeStruct((total, share), F32),
            jax.ShapeDtypeStruct((total, share), F32),
            jax.ShapeDtypeStruct((total, share), F32),
            jax.ShapeDtypeStruct((total, share), F32),
            jax.ShapeDtypeStruct((seqs, 2, 1, share), F32),
        ],
        scratch_shapes=[
            pltpu.VMEM((2, tokens, window), F32),
        ],
        compiler_params=pltpu.CompilerParams(vmem_limit_bytes=48 * 1024 * 1024),
        cost_estimate=pl.CostEstimate(flops=1000, bytes_accessed=1000, transcendentals=0),
        name="temporal_forward",
    )(off, x_win, edge, gates, chan)


def partner(mask):
    s = lax.axis_index("seq")
    if mask == 1:
        other = s + 1 - 2 * (s % 2)
    else:
        other = (s + 2) % 4
    return {"seq": other}


def greet():
    barrier = pltpu.get_barrier_semaphore()
    for mask in (1, 2):
        pl.semaphore_signal(barrier, inc=1, device_id=partner(mask), device_id_type=MESH)
    pl.semaphore_wait(barrier, 2)


def sender(sends, recvs):
    def send(slot, source, target, mask):
        copy = pltpu.make_async_remote_copy(
            src_ref=source,
            dst_ref=target,
            send_sem=sends.at[slot],
            recv_sem=recvs.at[slot],
            device_id=partner(mask),
            device_id_type=MESH,
        )
        copy.start()
        return copy

    return send


def over_chunks(rows, run):
    def step(i, carry):
        run(pl.ds(pl.multiple_of(i * ROWS16, ROWS16), ROWS16))
        return carry

    lax.fori_loop(0, rows // ROWS16, step, 0)


def reduce_phase(product, send, first_slot, acc, sent, got):
    rows = acc.shape[1]
    half = rows // 2
    low, high = pl.ds(0, half), pl.ds(half, half)
    product(3, lambda cols, value: sent.__setitem__((0, slice(None), cols), value.astype(BF)))
    far_near = send(first_slot, sent.at[0, low], got.at[0, low], 1)
    far_side = send(first_slot + 1, sent.at[0, high], got.at[0, high], 2)
    product(1, lambda cols, value: acc.__setitem__((1, slice(None), cols), value))
    over_chunks(half, lambda r: sent.__setitem__((1, r), acc[1, r].astype(BF)))
    near_low = send(first_slot + 2, sent.at[1, low], got.at[1, low], 1)
    product(2, lambda cols, value: acc.__setitem__((2, slice(None), cols), value))

    def tail(k):
        def run(r):
            r = pl.ds(pl.multiple_of(r.start + half, ROWS16), ROWS16)
            sent[k, r] = acc[k, r].astype(BF)

        return run

    over_chunks(half, tail(2))
    side_high = send(first_slot + 3, sent.at[2, high], got.at[2, high], 2)
    far_side.wait_recv()

    def add_high(r):
        r = pl.ds(pl.multiple_of(r.start + half, ROWS16), ROWS16)
        sent[1, r] = (acc[1, r] + got[0, r].astype(F32)).astype(BF)

    over_chunks(half, add_high)
    near_high = send(first_slot + 4, sent.at[1, high], got.at[1, high], 1)
    far_near.wait_recv()

    def add_low(r):
        sent[2, r] = (acc[2, r] + got[0, r].astype(F32)).astype(BF)

    over_chunks(half, add_low)
    side_low = send(first_slot + 5, sent.at[2, low], got.at[2, low], 2)
    product(0, lambda cols, value: acc.__setitem__((0, slice(None), cols), value))
    arriving = [near_low, side_high, near_high, side_low]
    for copy in arriving:
        copy.wait_recv()
    return [far_near, far_side] + arriving


def both_ways(send, slot, source, out):
    half = source.shape[0] // 2
    low, high = pl.ds(0, half), pl.ds(half, half)
    return [
        send(slot, source.at[low], out.at[1, low], 1),
        send(slot + 1, source.at[high], out.at[2, high], 2),
        send(slot + 2, source.at[high], out.at[1, high], 1),
        send(slot + 3, source.at[low], out.at[2, low], 2),
    ]


def pass_on(send, slot, out, copies):
    half = out.shape[1] // 2
    low, high = pl.ds(0, half), pl.ds(half, half)
    copies[0].wait_recv()
    far_low = send(slot + 4, out.at[1, low], out.at[3, low], 2)
    copies[1].wait_recv()
    far_high = send(slot + 5, out.at[2, high], out.at[3, high], 1)
    return copies + [far_low, far_high]


def settle(copies):
    for copy in copies[2:]:
        copy.wait_recv()
    for copy in copies:
        copy.wait_send()


def at_seq(k):
    s = lax.axis_index("seq")
    return s if k == 0 else 3 - s if k == 3 else partner(k)["seq"]


def product_of(left, right, contract, rows, tile, ready=None):
    def product(k, store):
        def step(c, carry):
            cols = pl.ds(pl.multiple_of(c * tile, tile), tile)
            if ready is not None and k == 3:
                ready(c)
            total = None
            for a, b in zip(left, right):
                part = b[cols, :] if contract else b[:, cols]
                value = lax.dot_general(
                    a[k * rows : (k + 1) * rows, :],
                    part,
                    (((1,), (1 if contract else 0,)), ((), ())),
                    preferred_element_type=F32,
                )
                total = value if total is None else total + value
            store(cols, total)
            return carry

        width = right[0].shape[0 if contract else 1]
        lax.fori_loop(0, width // tile, step, 0)

    return product


def rms_parts(values):
    return lax.rsqrt(jnp.mean(values * values, axis=-1, keepdims=True) + 1e-06)


def stream_kernel(
    mixed_ref, weight_ref, flat_ref, gain_ref,
    stream_out, temporal_out, normed_out,
    acc, sent, got, sends, recvs,
):
    rows = flat_ref.shape[0]
    greet()
    send = sender(sends, recvs)
    copies = reduce_phase(
        product_of([mixed_ref], [weight_ref], False, rows, 512), send, 0, acc, sent, got
    )

    def finish(r):
        temporal = acc[0, r] + got[1, r].astype(F32) + got[2, r].astype(F32)
        temporal_out[r] = temporal
        stream = flat_ref[r].astype(F32) + temporal
        stream_out[r] = stream
        normed_out[0, r] = (stream * rms_parts(stream) * gain_ref[...]).astype(BF)

    over_chunks(rows, finish)
    gathered = pass_on(send, 6, normed_out, both_ways(send, 6, normed_out.at[0], normed_out))
    settle(gathered)
    for copy in copies:
        copy.wait_send()


def exchange_scratch(rows, width, copies):
    return [
        pltpu.VMEM((3, rows, width), F32),
        pltpu.VMEM((3, rows, width), BF),
        pltpu.VMEM((3, rows, width), BF),
        pltpu.SemaphoreType.DMA((copies,)),
        pltpu.SemaphoreType.DMA((copies,)),
    ]


def remote_call(kernel, name, ident, outs, operands, scratch, far=0):
    return pl.pallas_call(
        kernel,
        in_specs=[pl.BlockSpec(memory_space=pltpu.VMEM)] * (len(operands) - far)
        + [pl.BlockSpec(memory_space=pl.ANY)] * far,
        out_specs=[pl.BlockSpec(memory_space=pltpu.VMEM)] * len(outs),
        out_shape=[jax.ShapeDtypeStruct(shape, kind) for shape, kind in outs],
        scratch_shapes=scratch,
        compiler_params=pltpu.CompilerParams(
            collective_id=ident, has_side_effects=True, vmem_limit_bytes=60 * 1024 * 1024
        ),
        cost_estimate=pl.CostEstimate(flops=1000, bytes_accessed=1000, transcendentals=0),
        name=name,
    )(*operands)


def stream_and_norm(mixed, weight, flat, gain):
    rows, width = flat.shape
    groups = mixed.shape[0] // rows
    return remote_call(
        stream_kernel,
        "stream_and_norm",
        1,
        [((rows, width), F32), ((rows, width), F32), ((groups, rows, width), BF)],
        (mixed, weight, flat, gain),
        exchange_scratch(rows, width, 12),
    )


def stream_back_kernel(
    rows_ref, stream_ref, gain_ref, upstream_ref, weight_far, hidden_far, down_far,
    grad_out, low_out, gain_out, feed_out,
    weight_ref, hidden_ref, down_ref, fetches,
    acc, sent, got, sends, recvs,
):
    rows, width = stream_ref.shape
    tile = 512

    def fetch(c):
        part = pl.ds(pl.multiple_of(c * tile, tile), tile)
        return pltpu.make_async_copy(weight_far.at[part], weight_ref.at[part], fetches.at[c])

    count = width // tile
    for c in range(count):
        fetch(c).start()
    late = [
        pltpu.make_async_copy(hidden_far, hidden_ref, fetches.at[count]),
        pltpu.make_async_copy(down_far, down_ref, fetches.at[count + 1]),
    ]
    for copy in late:
        copy.start()
    greet()
    send = sender(sends, recvs)
    product = product_of(
        [rows_ref], [weight_ref], True, rows, tile, ready=lambda c: fetch(c).wait()
    )
    copies = reduce_phase(product, send, 0, acc, sent, got)
    gain_out[...] = jnp.zeros_like(gain_out)

    def finish(r):
        grad = acc[0, r] + got[1, r].astype(F32) + got[2, r].astype(F32)
        stream = stream_ref[r]
        inv = rms_parts(stream)
        scaled = grad * gain_ref[...]
        inner = jnp.mean(stream * scaled, axis=-1, keepdims=True)
        total = upstream_ref[r].astype(F32) + inv * scaled - stream * (inv * inv * inv * inner)
        grad_out[r] = total
        low_out[0, r] = total.astype(BF)
        gained = grad * stream * inv
        gain_out[...] += gained[:8] + gained[8:]

    over_chunks(rows, finish)
    gathered = both_ways(send, 6, low_out.at[0], low_out)
    for copy in late:
        copy.wait()
    feed = product_of([hidden_ref], [down_ref], False, rows, tile)

    def feed_block(k):
        feed(k, lambda cols, value: feed_out.__setitem__((k, slice(None), cols), value.astype(BF)))

    feed_block(3)
    gathered = pass_on(send, 6, low_out, gathered)
    for k in range(3):
        feed_block(k)
    settle(gathered)
    for copy in copies:
        copy.wait_send()


def stream_back(rows_all, weight, stream, gain, upstream, hidden, down):
    rows, width = stream.shape
    groups = rows_all.shape[0] // rows
    return remote_call(
        stream_back_kernel,
        "stream_back",
        2,
        [
            ((rows, width), F32),
            ((groups, rows, width), BF),
            ((8, width), F32),
            ((groups, rows, width), BF),
        ],
        (rows_all, stream, gain, upstream, weight, hidden, down),
        [
            pltpu.VMEM(weight.shape, BF),
            pltpu.VMEM(hidden.shape, BF),
            pltpu.VMEM(down.shape, BF),
            pltpu.SemaphoreType.DMA((width // 512 + 2,)),
        ]
        + exchange_scratch(rows, width, 12),
        far=3,
    )


def inputs_back_kernel(
    branch_ref, y_ref, weight_ref, flat_ref, gain_ref, columns_ref,
    grad_out, gain_out, columns_out,
    acc, sent, got, sends, recvs,
):
    rows = flat_ref.shape[0]
    s = lax.axis_index("seq")
    count, columns = columns_ref.shape[0], columns_out.shape[1]
    barrier = pltpu.get_barrier_semaphore()
    for k in (1, 2, 3):
        pl.semaphore_signal(barrier, inc=1, device_id={"seq": at_seq(k)}, device_id_type=MESH)
    pl.semaphore_wait(barrier, 3)
    send = sender(sends, recvs)
    here = pl.ds(pl.multiple_of(s * count, ROWS16), count)

    def columns_of(k):
        return columns_ref.at[:, pl.ds(pl.multiple_of(at_seq(k) * columns, LANES), columns)]

    moved = []
    for k in (3, 1, 2):
        copy = pltpu.make_async_remote_copy(
            src_ref=columns_of(k),
            dst_ref=columns_out.at[here],
            send_sem=sends.at[5 + k],
            recv_sem=recvs.at[5 + k],
            device_id={"seq": at_seq(k)},
            device_id_type=MESH,
        )
        moved.append(copy)
    window = branch_ref.shape[1]
    weights = [weight_ref.at[:, :window], weight_ref.at[:, window:]]
    product = product_of([branch_ref, y_ref], weights, True, rows, 512)

    def product_and_move(k, store):
        if k == 0:
            for copy in moved:
                copy.start()
        product(k, store)

    copies = reduce_phase(product_and_move, send, 0, acc, sent, got)
    columns_out[here] = columns_of(0)[...]
    gain_out[...] = jnp.zeros_like(gain_out)

    def finish(r):
        grad = acc[0, r] + got[1, r].astype(F32) + got[2, r].astype(F32)
        values = flat_ref[r].astype(F32)
        inv = rms_parts(values)
        scaled = grad * gain_ref[...]
        inner = jnp.mean(values * scaled, axis=-1, keepdims=True)
        grad_out[r] = inv * scaled - values * (inv * inv * inv * inner)
        gained = grad * values * inv
        gain_out[...] += gained[:8] + gained[8:]

    over_chunks(rows, finish)
    for copy in moved:
        copy.wait_recv()
    for copy in copies + moved:
        copy.wait_send()


def inputs_back(branch_rows, y_rows, weight, flat, gain, columns):
    rows, width = flat.shape
    count, whole = columns.shape
    return remote_call(
        inputs_back_kernel,
        "inputs_back",
        3,
        [((rows, width), F32), ((8, width), F32), ((4 * count, whole // 4), BF)],
        (branch_rows, y_rows, weight, flat, gain, columns),
        exchange_scratch(rows, width, 9),
    )


def start_kernel(inputs_ref, inputs_out, edge_out, sends, recvs):
    seqs = edge_out.shape[1] // ROWS16
    tokens = inputs_ref.shape[0] // seqs
    w = lax.axis_index("wide")
    wide = lax.axis_size("wide")
    after, before = lax.rem(w + 1, wide), lax.rem(w + wide - 1, wide)
    barrier = pltpu.get_barrier_semaphore()
    for mask in (1, 2):
        pl.semaphore_signal(barrier, inc=1, device_id=partner(mask), device_id_type=MESH)
    pl.semaphore_signal(barrier, inc=1, device_id={"wide": before}, device_id_type=MESH)
    pl.semaphore_wait(barrier, 3)
    send = sender(sends, recvs)
    edges = []
    for q in range(seqs):
        copy = pltpu.make_async_remote_copy(
            src_ref=inputs_ref.at[pl.ds((q + 1) * tokens - ROWS16, ROWS16)],
            dst_ref=edge_out.at[0, pl.ds(q * ROWS16, ROWS16)],
            send_sem=sends.at[12 + q],
            recv_sem=recvs.at[12 + q],
            device_id={"wide": after},
            device_id_type=MESH,
        )
        copy.start()
        edges.append(copy)
    blocks = both_ways(send, 0, inputs_ref, inputs_out)
    inputs_out[0] = inputs_ref[...]
    for copy in edges:
        copy.wait_recv()
        copy.wait_send()
    edges = both_ways(send, 6, edge_out.at[0], edge_out)
    blocks = pass_on(send, 0, inputs_out, blocks)
    edges = pass_on(send, 6, edge_out, edges)
    settle(blocks)
    settle(edges)


def start(inputs, groups, seqs):
    rows, width = inputs.shape
    copies = 12 + seqs
    return remote_call(
        start_kernel,
        "start",
        6,
        [((groups, rows, width), BF), ((groups, seqs * ROWS16, width), BF)],
        (inputs,),
        [pltpu.SemaphoreType.DMA((copies,)), pltpu.SemaphoreType.DMA((copies,))],
    )


def middle_kernel(
    grad_ref, y_ref, local_ref, reach_ref, carry_ref, rate_ref, chan_ref, ends_ref,
    edge_ref, gates_ref, valid_ref, feed_ref,
    conv_far, forget_far, admit_far, x_far, stream_far, temporal_far,
    y_rows_out, branch_out, forget_out, admit_out, sums_out, result_out, squares_out,
    adjoint, later, heads, packet, packet_in, tails, after, conv_rows,
    conv_ref, forget_ref, admit_ref, x_ref, stream_ref, temporal_ref,
    sent, got, fetches, sends, recvs, head_sends, head_recvs,
):
    wide, seqs, share = ends_ref.shape
    tokens = grad_ref.shape[0] // seqs
    window = x_ref.shape[1]
    rows, width = stream_ref.shape
    half = rows // 2
    low, high = pl.ds(0, half), pl.ds(half, half)
    w = lax.axis_index("wide")
    first_channel = lax.axis_index("seq") * share
    base = jnp.minimum(first_channel // BW * BW, lax.axis_size("seq") * share - window)
    off = pl.multiple_of(first_channel - base, LANES)
    fetched = []
    for i, (far, near) in enumerate(
        (
            (conv_far, conv_ref),
            (forget_far, forget_ref),
            (admit_far, admit_ref),
            (x_far, x_ref),
            (stream_far, stream_ref),
            (temporal_far, temporal_ref),
        )
    ):
        copy = pltpu.make_async_copy(far, near, fetches.at[i])
        copy.start()
        fetched.append(copy)

    barrier = pltpu.get_barrier_semaphore()
    for mask in (1, 2):
        pl.semaphore_signal(barrier, inc=1, device_id=partner(mask), device_id_type=MESH)

    def tell(i, carry):
        other = lax.rem(w + i, wide)
        pl.semaphore_signal(barrier, inc=1, device_id={"wide": other}, device_id_type=MESH)
        return carry

    lax.fori_loop(1, wide, tell, 0)
    pl.semaphore_wait(barrier, wide + 1)
    send = sender(sends, recvs)
    far_near = send(0, feed_ref.at[3, low], got.at[0, low], 1)
    far_side = send(1, feed_ref.at[3, high], got.at[0, high], 2)
    near_low = send(2, feed_ref.at[1, low], got.at[1, low], 1)
    side_high = send(3, feed_ref.at[2, high], got.at[2, high], 2)

    row = lax.broadcasted_iota(jnp.int32, (tokens, LANES), 0)
    fetched[1].wait()
    fetched[2].wait()

    def scan_step(q, carry):
        r = pl.ds(pl.multiple_of(q * tokens, tokens), tokens)
        head_rows = pl.ds(pl.multiple_of(q * tokens, tokens), ROWS16)
        for j in range(share // LANES):
            lanes = slice(j * LANES, (j + 1) * LANES)
            grad = grad_ref[r, lanes]
            value, slope = gelu_parts(y_ref[r, lanes])
            state = (local_ref[r, lanes] + reach_ref[r, lanes] * carry_ref[q, :, lanes]).astype(BF)
            y_rows_out[r, lanes] = (grad * state.astype(F32) * slope).astype(BF)
            state_grad = (grad * value).astype(BF).astype(F32)
            rate = rate_ref[r, lanes]
            ahead = jnp.where(row == tokens - 1, 1.0, pltpu.roll(rate, tokens - 1, 0))
            adjoints, laters = scan_rows(ahead, state_grad, True)
            adjoint[r, lanes] = adjoints
            later[r, lanes] = laters
            tails[q, :, lanes] = rate[:1] * adjoints[:1]
            forget_sig = sigmoid(forget_ref[head_rows, lanes].astype(F32)[:HALO])
            admit_sig = sigmoid(admit_ref[head_rows, lanes].astype(F32)[:HALO])
            rate_log = -8.0 * chan_ref[2:3, lanes] * (0.1 + 0.9 * forget_sig)
            gain = jnp.sqrt(drop_of(rate_log)) * admit_sig
            for i, values in enumerate((adjoints[:HALO] * gain, laters[:HALO] * gain)):
                for t in range(CONV - 1):
                    packet[i, t, q, :, lanes] = values[t : t + 1]
        return carry

    lax.fori_loop(0, seqs, scan_step, 0)
    for q in range(seqs):
        heads[0, q : q + 1, :] = tails[q]

    def head_copy(i):
        return pltpu.make_async_remote_copy(
            src_ref=heads.at[0],
            dst_ref=heads.at[i],
            send_sem=head_sends.at[i],
            recv_sem=head_recvs.at[i],
            device_id={"wide": lax.rem(w + i, wide)},
            device_id_type=MESH,
        )

    def head_start(i, carry):
        head_copy(i).start()
        return carry

    def head_wait(i, carry):
        copy = head_copy(i)
        copy.wait_recv()
        copy.wait_send()
        return carry

    lax.fori_loop(1, wide, head_start, 0)
    packets = pltpu.make_async_remote_copy(
        src_ref=packet,
        dst_ref=packet_in,
        send_sem=sends.at[6],
        recv_sem=recvs.at[6],
        device_id={"wide": lax.rem(w + wide - 1, wide)},
        device_id_type=MESH,
    )
    packets.start()

    far_side.wait_recv()
    sent[0] = (feed_ref[1, high].astype(F32) + got[0, high].astype(F32)).astype(BF)
    near_high = send(4, sent.at[0], got.at[1, high], 1)
    far_near.wait_recv()
    sent[1] = (feed_ref[2, low].astype(F32) + got[0, low].astype(F32)).astype(BF)
    side_low = send(5, sent.at[1], got.at[2, low], 2)

    lax.fori_loop(1, wide, head_wait, 0)
    packets.wait_recv()
    packets.wait_send()

    def tail_step(i, carry):
        tail, next_tail = carry
        j = wide - i
        stepped = ends_ref[j] * tail + heads[lax.rem(w + i, wide)]
        return jnp.where(j > w, stepped, tail), jnp.where(j > w + 1, stepped, next_tail)

    zero = jnp.zeros((seqs, share), F32)
    tail, next_tail = lax.fori_loop(1, wide, tail_step, (zero, zero))
    next_tail = jnp.where(w == wide - 1, 0.0, next_tail)
    inside = jnp.where(w == wide - 1, 0.0, 1.0)
    after[...] = jnp.zeros_like(after)
    for q in range(seqs):
        tails[q] = tail[q : q + 1]
        for t in range(CONV - 1):
            after[q * HALO + t : q * HALO + t + 1, :] = (
                inside * packet_in[0, t, q] + packet_in[1, t, q] * next_tail[q : q + 1]
            )

    forget_out[...] = jnp.zeros_like(forget_out)
    admit_out[...] = jnp.zeros_like(admit_out)
    conv_rows[...] = jnp.zeros_like(conv_rows)
    sums_out[...] = jnp.zeros_like(sums_out)
    fetched[0].wait()
    fetched[3].wait()

    def rows_step(q, carry):
        r = pl.ds(pl.multiple_of(q * tokens, tokens), tokens)
        pack = pl.ds(pl.multiple_of(q * HALO, HALO), HALO)
        for j in range(share // LANES):
            lanes = slice(j * LANES, (j + 1) * LANES)
            here = pl.ds(pl.multiple_of(off + j * LANES, LANES), LANES)
            chan = [chan_ref[i : i + 1, lanes] for i in range(8)]
            start = carry_ref[q, :, lanes]
            carried = local_ref[r, lanes] + reach_ref[r, lanes] * start
            before = jnp.where(row == 0, start, pltpu.roll(carried, 1, 0))
            full = adjoint[r, lanes] + later[r, lanes] * tails[q, :, lanes]
            forget_sig = sigmoid(forget_ref[r, lanes].astype(F32))
            admit_sig = sigmoid(admit_ref[r, lanes].astype(F32))
            span = 0.1 + 0.9 * forget_sig
            rate = rate_ref[r, lanes]
            scale = jnp.sqrt(drop_of(-8.0 * chan[2] * span))
            gated = admit_sig * conv_ref[r, lanes]
            log_grad = full * (rate * before - rate * rate / scale * gated)
            conv_grad = full * scale * admit_sig
            forget_rows = (
                log_grad * (-7.2) * chan[2] * forget_sig * (1.0 - forget_sig)
            ).astype(BF)
            admit_rows = (full * scale * gated * (1.0 - admit_sig)).astype(BF)
            forget_out[r, here] = forget_rows
            admit_out[r, here] = admit_rows
            ahead = jnp.concatenate([conv_grad, after[pack, lanes]], axis=0)
            back = chan[4] * conv_grad
            for k in range(1, CONV):
                back = back + chan[4 + k] * pltpu.roll(ahead, tokens + HALO - k, 0)[:tokens]
            conv_rows[:, here] = back.astype(BF).astype(F32)
            padded = jnp.concatenate(
                [edge_ref[pack, here], x_ref[r, here].astype(F32)], axis=0
            )
            sums = [
                forget_rows.astype(F32),
                admit_rows.astype(F32),
                log_grad * (-8.0) * span,
                conv_grad,
                conv_grad * padded[HALO:],
            ] + [conv_grad * pltpu.roll(padded, k, 0)[HALO:] for k in range(1, CONV)]
            sums_out[:, lanes] += jnp.concatenate(
                [jnp.sum(v, axis=0, keepdims=True) for v in sums], axis=0
            )
        for b in range(window // BW):
            cols = slice(b * BW, (b + 1) * BW)
            back = conv_rows[:, cols]
            for source, at in ((forget_out, 0), (admit_out, BW)):
                back = back + lax.dot_general(
                    source[r, cols],
                    gates_ref[cols, at : at + BW],
                    (((1,), (1,)), ((), ())),
                    preferred_element_type=F32,
                )
            branch_out[r, cols] = back.astype(BF)
        return carry

    lax.fori_loop(0, seqs, rows_step, 0)
    fetched[4].wait()
    fetched[5].wait()
    for copy in (near_low, side_high, near_high, side_low):
        copy.wait_recv()
    squares_out[...] = jnp.zeros_like(squares_out)

    def finish(r):
        feed = feed_ref[0, r].astype(F32) + got[1, r].astype(F32) + got[2, r].astype(F32)
        result = stream_ref[r] + feed
        result_out[r] = result
        valid = valid_ref[r]
        for i, values in enumerate((result, temporal_ref[r], feed)):
            square = valid * values * values
            squares_out[i] += square[:8] + square[8:]

    over_chunks(rows, finish)
    for copy in (far_near, far_side, near_low, side_high, near_high, side_low):
        copy.wait_send()


def middle(
    grad, y, local, reach, carry, rate, chan, ends, edge, gates, valid, feed,
    conv, forget, admit, x_win, stream, temporal,
):
    total, share = grad.shape
    window = x_win.shape[1]
    rows, width = stream.shape
    wide, seqs = ends.shape[:2]
    tokens = total // seqs
    vmem = pl.BlockSpec(memory_space=pltpu.VMEM)
    anywhere = pl.BlockSpec(memory_space=pl.ANY)
    outs = [
        ((total, share), BF),
        ((total, window), BF),
        ((total, window), BF),
        ((total, window), BF),
        ((8, share), F32),
        ((rows, width), F32),
        ((3, 8, width), F32),
    ]
    return pl.pallas_call(
        middle_kernel,
        in_specs=[vmem] * 12 + [anywhere] * 6,
        out_specs=[vmem] * len(outs),
        out_shape=[jax.ShapeDtypeStruct(shape, kind) for shape, kind in outs],
        scratch_shapes=[
            pltpu.VMEM((total, share), F32),
            pltpu.VMEM((total, share), F32),
            pltpu.VMEM((wide, seqs, share), F32),
            pltpu.VMEM((2, CONV - 1, seqs, 1, share), F32),
            pltpu.VMEM((2, CONV - 1, seqs, 1, share), F32),
            pltpu.VMEM((seqs, 1, share), F32),
            pltpu.VMEM((seqs * HALO, share), F32),
            pltpu.VMEM((tokens, window), F32),
            pltpu.VMEM((total, share), F32),
            pltpu.VMEM((total, share), BF),
            pltpu.VMEM((total, share), BF),
            pltpu.VMEM((total, window), BF),
            pltpu.VMEM((rows, width), F32),
            pltpu.VMEM((rows, width), F32),
            pltpu.VMEM((2, rows // 2, width), BF),
            pltpu.VMEM((3, rows, width), BF),
            pltpu.SemaphoreType.DMA((6,)),
            pltpu.SemaphoreType.DMA((7,)),
            pltpu.SemaphoreType.DMA((7,)),
            pltpu.SemaphoreType.DMA((wide,)),
            pltpu.SemaphoreType.DMA((wide,)),
        ],
        compiler_params=pltpu.CompilerParams(
            collective_id=7, has_side_effects=True, vmem_limit_bytes=60 * 1024 * 1024
        ),
        cost_estimate=pl.CostEstimate(flops=1000, bytes_accessed=1000, transcendentals=0),
        name="middle",
    )(
        grad, y, local, reach, carry[:, None, :], rate, chan, ends, edge, gates, valid, feed,
        conv, forget, admit, x_win, stream, temporal,
    )


def grads_kernel(
    bases, normed_ref, y_ref, branch_ref, x_ref, forget_ref, admit_ref,
    stacked_out,
    gates, blocks, gate_total, sends, recvs,
):
    step = pl.program_id(0)
    wide, stacked_rows, quarter = stacked_out.shape
    window = x_ref.shape[1]
    tiles = (window + y_ref.shape[1]) // LANES
    group = wide // pl.num_programs(0)
    part = normed_ref.shape[1] // group
    room = stacked_rows - tiles * part
    share = gate_total.shape[0] // wide

    def quarter_of(k):
        return pl.ds(pl.multiple_of(at_seq(k) * quarter, LANES), quarter)

    def exchange(k):
        return pltpu.make_async_remote_copy(
            src_ref=gates.at[:, quarter_of(k)],
            dst_ref=blocks.at[k],
            send_sem=sends.at[k],
            recv_sem=recvs.at[k],
            device_id={"seq": at_seq(k)},
            device_id_type=MESH,
        )

    @pl.when(step == 0)
    def _():
        barrier = pltpu.get_barrier_semaphore()
        for k in (1, 2, 3):
            pl.semaphore_signal(barrier, inc=1, device_id={"seq": at_seq(k)}, device_id_type=MESH)
        for b in range(window // BW):
            cols = slice(b * BW, (b + 1) * BW)
            block = x_ref[:, cols].T
            for source, at in ((forget_ref, 0), (admit_ref, BW)):
                gates[cols, at : at + BW] = jnp.dot(
                    block, source[:, cols], preferred_element_type=F32
                ).astype(BF)
        pl.semaphore_wait(barrier, 3)
        for k in (3, 1, 2):
            exchange(k).start()

    left = normed_ref[...].T
    first = 0
    for right in (branch_ref, y_ref):
        sums = jnp.dot(left, right[...], preferred_element_type=F32).astype(BF)
        count = right.shape[1] // LANES
        for g in range(group):
            for i in range(count):
                at = (first + i) * part
                stacked_out[step * group + g, at : at + part, :] = sums[
                    g * part : (g + 1) * part, i * LANES : (i + 1) * LANES
                ]
        first += count

    @pl.when(step == pl.num_programs(0) - 1)
    def _():
        gate_total[...] = jnp.zeros_like(gate_total)
        for k in range(4):
            if k:
                exchange(k).wait_recv()
            other = at_seq(k)
            base = other * 0
            for j, start_row in enumerate(bases):
                base = jnp.where(other == j, start_row, base)
            at = pl.ds(pl.multiple_of(base, 8), window)
            value = blocks[k] if k else gates[:, quarter_of(0)]
            gate_total[at, :] += value.astype(F32)
        for g in range(wide):
            value = gate_total[g * share : (g + 1) * share, :]
            if room > share:
                value = jnp.concatenate([value, jnp.zeros((room - share, quarter), F32)], axis=0)
            stacked_out[g, tiles * part :, :] = value.astype(BF)
        for k in (1, 2, 3):
            exchange(k).wait_send()


def temporal_grads(normed, y_rows, branch_rows, x_win, forget_win, admit_win, wide, bases, stacked_rows):
    total, width = normed.shape
    share, window = y_rows.shape[1], x_win.shape[1]
    quarter = 2 * BW // 4
    return pl.pallas_call(
        functools.partial(grads_kernel, bases),
        grid=(width // BW,),
        in_specs=[pl.BlockSpec((total, BW), lambda i: (0, i))]
        + [whole(v.shape) for v in (y_rows, branch_rows, x_win, forget_win, admit_win)],
        out_specs=whole((wide, stacked_rows, quarter)),
        out_shape=jax.ShapeDtypeStruct((wide, stacked_rows, quarter), BF),
        scratch_shapes=[
            pltpu.VMEM((window, 2 * BW), BF),
            pltpu.VMEM((4, window, quarter), BF),
            pltpu.VMEM((4 * share, quarter), F32),
            pltpu.SemaphoreType.DMA((4,)),
            pltpu.SemaphoreType.DMA((4,)),
        ],
        compiler_params=pltpu.CompilerParams(
            collective_id=9, has_side_effects=True, vmem_limit_bytes=48 * 1024 * 1024
        ),
        cost_estimate=pl.CostEstimate(flops=1000, bytes_accessed=1000, transcendentals=0),
        name="temporal_grads",
    )(normed, y_rows, branch_rows, x_win, forget_win, admit_win)


def place(k, block, buffer, plan, outs):
    buffer[...] = block[...].astype(F32)
    other = at_seq(k)
    for (first, count, tiles, starts), out in zip(plan, outs):
        base = other * 0
        for j, start_col in enumerate(starts):
            base = jnp.where(other == j, start_col, base)
        for i in range(tiles):
            cols = pl.ds(pl.multiple_of(base + i * LANES, LANES), LANES)
            out[:, cols] += buffer[first + i * count : first + (i + 1) * count, :]


def put(k, block, out):
    columns = block.shape[1]
    other = at_seq(k)
    for i in range(columns // LANES):
        start_col = pl.multiple_of(other * columns + i * LANES, LANES)
        out[:, pl.ds(start_col, LANES)] = block[:, i * LANES : (i + 1) * LANES]


def spread_kernel(plan, parts_ref, early_ref, late_ref, *refs):
    outs, refs = refs[: len(plan)], refs[len(plan) :]
    sums_out, blocks, buffer, *refs = refs
    wholes, refs = refs[: len(plan)], refs[len(plan) :]
    total, sums_ref, got_sums, sends, recvs, sum_sends, sum_recvs = refs
    wide = sums_ref.shape[0]
    early = early_ref.shape[1]
    sums_ref[:, :early] = early_ref[...]
    sums_ref[:, early:] = late_ref[...]
    w = lax.axis_index("wide")
    barrier = pltpu.get_barrier_semaphore()
    for mask in (1, 2):
        pl.semaphore_signal(barrier, inc=1, device_id=partner(mask), device_id_type=MESH)

    def tell(i, carry):
        other = lax.rem(w + i, wide)
        pl.semaphore_signal(barrier, inc=1, device_id={"wide": other}, device_id_type=MESH)
        return carry

    lax.fori_loop(1, wide, tell, 0)
    pl.semaphore_wait(barrier, wide + 1)
    send = sender(sends, recvs)

    def chunk(i):
        other = lax.rem(w + i, wide)
        return pltpu.make_async_remote_copy(
            src_ref=sums_ref.at[other],
            dst_ref=got_sums.at[i],
            send_sem=sum_sends.at[i],
            recv_sem=sum_recvs.at[i],
            device_id={"wide": other},
            device_id_type=MESH,
        )

    def begin(i, carry):
        chunk(i).start()
        return carry

    def finish(i, carry):
        copy = chunk(i)
        copy.wait_recv()
        copy.wait_send()
        return carry + got_sums[i]

    lax.fori_loop(1, wide, begin, 0)
    copies = both_ways(send, 0, parts_ref, blocks)
    for out in wholes:
        out[...] = jnp.zeros_like(out)
    place(0, parts_ref, buffer, plan, wholes)
    total[0] = lax.fori_loop(1, wide, finish, sums_ref[w])
    to_near = send(6, total.at[0], total.at[1], 1)
    copies = pass_on(send, 0, blocks, copies)
    to_near.wait_recv()
    total[2] = total[0] + total[1]
    to_side = send(7, total.at[2], total.at[3], 2)
    to_side.wait_recv()
    sums_out[...] = total[2] + total[3]
    settle(copies)
    for k in (1, 2, 3):
        place(k, blocks.at[k], buffer, plan, wholes)
    for out, values in zip(outs, wholes):
        out[...] = values[...].astype(BF)
    to_near.wait_send()
    to_side.wait_send()


def spread(parts, early, late, plan, shapes):
    wide = early.shape[0]
    count = early.shape[1] + late.shape[1]
    return remote_call(
        functools.partial(spread_kernel, plan),
        "spread",
        8,
        [(shape, BF) for shape in shapes] + [((count, LANES), F32)],
        (parts, early, late),
        [pltpu.VMEM((4,) + parts.shape, BF), pltpu.VMEM(parts.shape, F32)]
        + [pltpu.VMEM(shape, F32) for shape in shapes]
        + [
            pltpu.VMEM((4, count, LANES), F32),
            pltpu.VMEM((wide, count, LANES), F32),
            pltpu.VMEM((wide, count, LANES), F32),
            pltpu.SemaphoreType.DMA((8,)),
            pltpu.SemaphoreType.DMA((8,)),
            pltpu.SemaphoreType.DMA((wide,)),
            pltpu.SemaphoreType.DMA((wide,)),
        ],
    )


def last_kernel(columns_ref, columns_out, column_blocks, sends, recvs):
    greet()
    send = sender(sends, recvs)
    copies = both_ways(send, 0, columns_ref, column_blocks)
    put(0, columns_ref, columns_out)
    copies = pass_on(send, 0, column_blocks, copies)
    settle(copies)
    for k in (1, 2, 3):
        put(k, column_blocks.at[k], columns_out)


def spread_last(columns):
    count = columns.shape[0]
    columns = jnp.pad(columns, ((0, -count % 32), (0, 0)))
    (wholes,) = remote_call(
        last_kernel,
        "spread_last",
        5,
        [((columns.shape[0], 4 * columns.shape[1]), BF)],
        (columns,),
        [
            pltpu.VMEM((4,) + columns.shape, BF),
            pltpu.SemaphoreType.DMA((6,)),
            pltpu.SemaphoreType.DMA((6,)),
        ],
    )
    return wholes[:count]


def body(
    inputs,
    lengths,
    norm_gain,
    gelu_weight,
    branch_weight,
    forget_gates,
    admit_gates,
    forget_bias,
    admit_bias,
    decay_rate,
    conv_weight,
    conv_bias,
    out_weight,
    mlp_gain,
    gate_weight,
    up_weight,
    down_weight,
    cotangent,
):
    groups = lax.axis_size("seq")
    wide = lax.axis_size("wide")
    s = lax.axis_index("seq")
    w = lax.axis_index("wide")
    seqs, tokens, width = inputs.shape
    rows = seqs * tokens
    total = groups * rows
    all_seqs = groups * seqs
    channels = gelu_weight.shape[1]
    share = channels // groups
    window = (share + BW - 1) // BW * BW
    blocks = window // BW

    def base_of(index):
        return jnp.minimum(index * share // BW * BW, channels - window)

    base = base_of(s)
    off = s * share - base
    quarter = width // groups
    gate_cols = 2 * BW // groups

    flat_low = inputs.reshape(rows, width)
    upstream = cotangent.reshape(rows, width)
    all_low, edge_low = start(flat_low, groups, seqs)
    all_low = all_low.reshape(total, width)
    edge_low = jnp.where(w == 0, 0.0, edge_low.reshape(all_seqs * ROWS16, width).astype(F32))

    x_y_cols = lax.all_gather(
        jnp.concatenate(
            [
                lax.dynamic_slice_in_dim(branch_weight, base, window, 1),
                lax.dynamic_slice_in_dim(gelu_weight, s * share, share, 1),
            ],
            axis=1,
        ),
        "wide",
        axis=0,
        tiled=True,
    )
    dw, rw = width // wide, channels // wide
    small = jnp.concatenate(
        [norm_gain, mlp_gain, forget_bias, admit_bias, decay_rate, conv_bias, conv_weight.reshape(-1)]
    ).reshape(-1, gate_cols)
    gates_quarter = jnp.concatenate([forget_gates, admit_gates], axis=1)
    small = jnp.concatenate(
        [lax.dynamic_slice_in_dim(gates_quarter, s * gate_cols, gate_cols, 1), small], axis=0
    )
    small, edge_low, later_upstream = lax.optimization_barrier((small, edge_low, upstream))
    upstream_near = swap(later_upstream, 1)
    upstream_side = swap(later_upstream, 2)
    small = lax.all_gather(small, "wide")
    gates_quarter = small[:, :rw].reshape(channels, gate_cols)
    small = small[:, rw:].reshape(wide, -1).astype(F32)
    gain_one = small[:, :dw].reshape(1, width)
    gain_two = small[:, dw : 2 * dw].reshape(1, width)
    per_channel = small[:, 2 * dw :].reshape(wide, 8, rw).transpose(1, 0, 2).reshape(8, channels)
    per_channel = lax.dynamic_slice_in_dim(per_channel, s * share, share, 1)

    out_quarter = lax.all_gather(
        lax.dynamic_slice_in_dim(out_weight, s * quarter, quarter, 1), "wide", axis=0, tiled=True
    )
    mlp_full = lax.all_gather(
        jnp.concatenate([gate_weight, up_weight], axis=1), "wide", axis=0, tiled=True
    )
    down_full = lax.all_gather(down_weight, "wide", axis=1, tiled=True)
    hidden_units = gate_weight.shape[1]

    def in_order(parts):
        near = [jnp.where(s % 2 == 1, parts[k ^ 1], parts[k]) for k in range(groups)]
        return [jnp.where(s // 2 == 1, near[k ^ 2], near[k]) for k in range(groups)]

    def swapped(part_of):
        return [swap(part_of(s ^ k), k) if k else part_of(s) for k in range(groups)]

    gates = jnp.concatenate(
        in_order(
            swapped(lambda j: lax.dynamic_slice_in_dim(gates_quarter, base_of(j), window, 0))
        ),
        axis=1,
    )
    normed_all = rms_norm(all_low.astype(F32), gain_one).astype(BF)
    normed_edge = rms_norm(edge_low, gain_one).astype(BF)
    normed_all, upstream_near, upstream_side = lax.optimization_barrier(
        (normed_all, upstream_near, upstream_side)
    )
    half = rows // 2
    upstream_far = [swap(upstream_near[:half], 2), swap(upstream_side[half:], 1)]

    x_y = dot(normed_all, x_y_cols)
    x_win = x_y[:, :window].astype(BF)
    branch_y = x_y[:, window:]
    x_win, out_quarter, *upstream_far = lax.optimization_barrier(
        (x_win, out_quarter, *upstream_far)
    )
    upstream_all = jnp.concatenate([upstream, upstream_near, upstream_side, *upstream_far], axis=0)
    out_rows = jnp.concatenate(
        in_order(swapped(lambda j: lax.dynamic_slice_in_dim(out_quarter, j * share, share, 0))),
        axis=1,
    )
    edge_win = dot(normed_edge, x_y_cols[:, :window]).astype(BF).astype(F32)
    edge_win = edge_win.reshape(all_seqs, ROWS16, window)[:, ROWS16 - HALO :]
    edge_win = edge_win.reshape(all_seqs * HALO, window)
    offset = off.reshape(1)
    forget, admit, conv_out, rate, local, reach, ends = temporal_forward(
        offset, x_win, edge_win, gates, per_channel, tokens
    )
    ends = lax.all_gather(ends, "wide")[:, :, :, 0]
    carry = jnp.zeros((all_seqs, share), F32)
    for j in range(wide - 1):
        carry = jnp.where(j < w, ends[j, :, 0] * carry + ends[j, :, 1], carry)
    carried = local.reshape(all_seqs, tokens, share) + reach.reshape(
        all_seqs, tokens, share
    ) * carry[:, None, :]
    state = carried.astype(BF).astype(F32).reshape(total, share)

    gelu_y = jax.nn.gelu(branch_y)
    mixed_low = (state * gelu_y).astype(BF)
    stream, temporal, normed_two_all = stream_and_norm(mixed_low, out_rows, flat_low, gain_two)
    normed_two_all = normed_two_all.reshape(total, width)

    gate_up = dot(normed_two_all, mlp_full)
    gate, up_values = gate_up[:, :hidden_units], gate_up[:, hidden_units:]
    gelu_gate = jax.nn.gelu(gate)
    hidden_low = (gelu_gate * up_values).astype(BF)
    down_part = contract_rows(hidden_low, upstream_all).astype(BF)
    hidden_low, down_part, upstream_low = lax.optimization_barrier(
        (hidden_low, down_part, upstream_all)
    )
    down_grad = lax.psum_scatter(down_part, "wide", scatter_dimension=1, tiled=True)
    hidden_grad = contract_last(upstream_low, down_full)
    gate_rows = (hidden_grad * up_values * gelu_parts(gate)[1]).astype(BF)
    up_rows = (hidden_grad * gelu_gate).astype(BF)
    mlp_rows = jnp.concatenate([gate_rows, up_rows], axis=1)
    mlp_part = contract_rows(normed_two_all, mlp_rows).astype(BF)
    mlp_rows, mlp_part = lax.optimization_barrier((mlp_rows, mlp_part))
    mlp_grad = lax.psum_scatter(mlp_part, "wide", scatter_dimension=0, tiled=True)
    stream_grad, stream_low_all, gain_two_grad, feed_parts = stream_back(
        mlp_rows, mlp_full, stream, gain_two, upstream, hidden_low, down_full
    )
    gain_two_grad = jnp.sum(gain_two_grad, axis=0)
    stream_low_all = stream_low_all.reshape(total, width)
    stream_low_all, down_grad = lax.optimization_barrier((stream_low_all, down_grad))
    mixed_grad = contract_last(stream_low_all, out_rows)
    out_grad = contract_rows(mixed_low, stream_low_all).astype(BF)
    mixed_grad, out_grad = lax.optimization_barrier((mixed_grad, out_grad))
    position = w * tokens + jnp.arange(tokens, dtype=jnp.int32)
    valid = (position[None, :] < lengths[:, None]).astype(F32).reshape(rows, 1)
    y_rows, branch_rows, forget_win, admit_win, channel_grads, result, squares = middle(
        mixed_grad, branch_y, local, reach, carry, rate, per_channel, ends[:, :, 0],
        edge_win, gates, valid, feed_parts, conv_out, forget, admit, x_win, stream, temporal,
    )
    partial_sums = jnp.concatenate([jnp.sum(squares, axis=(1, 2)), jnp.sum(valid).reshape(1)])

    bases = tuple(min(j * share // BW * BW, channels - window) for j in range(groups))
    branch_size = dw * window // LANES
    gates_at = branch_size + dw * share // LANES
    stacked_rows = (gates_at + rw + 31) // 32 * 32
    stacked = temporal_grads(
        normed_all, y_rows, branch_rows, x_win, forget_win, admit_win, wide, bases, stacked_rows
    )

    def sum_over_wide(values):
        return lax.psum_scatter(values, "wide", scatter_dimension=0, tiled=True)

    stacked, mlp_grad = lax.optimization_barrier((stacked, mlp_grad))
    temporal_sum = sum_over_wide(stacked)
    channel_all = lax.dynamic_update_slice_in_dim(
        jnp.zeros((8, channels), F32), channel_grads, s * share, 1
    )
    early_sums = jnp.concatenate(
        [
            channel_all.reshape(8, wide, rw).transpose(1, 0, 2).reshape(wide, 8 * rw),
            gain_two_grad.reshape(wide, dw),
            jnp.tile(partial_sums[None, :], (wide, 1)),
        ],
        axis=1,
    )
    early_sums = jnp.pad(early_sums, ((0, 0), (0, -early_sums.shape[1] % (8 * LANES))))
    early_sums = early_sums.reshape(wide, -1, LANES)
    branch_late, early_sums = lax.optimization_barrier((branch_rows, early_sums))
    first_back, gain_one_grad, out_cols = inputs_back(
        branch_late, y_rows, x_y_cols, flat_low, gain_one, out_grad
    )
    out_sum = sum_over_wide(out_cols)
    late_sums = jnp.sum(gain_one_grad, axis=0).reshape(wide, dw)
    late_sums = jnp.pad(late_sums, ((0, 0), (0, -dw % (8 * LANES)))).reshape(wide, -1, LANES)
    temporal_sum, late_sums = lax.optimization_barrier((temporal_sum, late_sums))

    plan = (
        (0, dw, window // LANES, bases),
        (branch_size, dw, share // LANES, tuple(j * share for j in range(groups))),
        (gates_at, rw, gate_cols // LANES, tuple(j * gate_cols for j in range(groups))),
    )
    branch_whole, gelu_whole, gates_whole, sums = spread(
        temporal_sum[0],
        early_sums,
        late_sums,
        plan,
        ((dw, channels), (dw, channels), (rw, 2 * BW)),
    )
    late_at = early_sums.shape[1]
    gain_one_sum = sums[late_at:].reshape(-1)[:dw]
    sums = sums[:late_at].reshape(-1)
    channel_sums = sums[: 8 * rw].reshape(8, rw)
    gain_two_sum = sums[8 * rw : 8 * rw + dw]
    totals = sums[8 * rw + dw : 8 * rw + dw + 4]
    statistics = jnp.sqrt(totals[0:3] / (totals[3] * width))
    earlier = lax.optimization_barrier(
        (
            out_sum,
            result.astype(BF).reshape(seqs, tokens, width),
            (stream_grad + first_back).reshape(seqs, tokens, width),
            gain_one_sum,
            gelu_whole.astype(F32),
            branch_whole.astype(F32),
            gates_whole[:, :BW].astype(F32),
            gates_whole[:, BW:].astype(F32),
            channel_sums[0],
            channel_sums[1],
            channel_sums[2],
            channel_sums[4:8],
            channel_sums[3],
            gain_two_sum,
            mlp_grad[:, :hidden_units].astype(F32),
            mlp_grad[:, hidden_units:].astype(F32),
            down_grad.astype(F32),
            statistics,
        )
    )
    out_sum, *outputs = earlier
    outputs.insert(12, spread_last(out_sum).astype(F32))
    return tuple(outputs)


def solution(mesh):
    in_specs = (
        P("seq", "wide", None),
        P("seq"),
        P("wide"),
        P("wide", None),
        P("wide", None),
        P("wide", None),
        P("wide", None),
        P("wide"),
        P("wide"),
        P("wide"),
        P(None, "wide"),
        P("wide"),
        P("wide", None),
        P("wide"),
        P("wide", "seq"),
        P("wide", "seq"),
        P("seq", "wide"),
        P("seq", "wide", None),
    )
    out_specs = (
        P("seq", "wide", None),
        P("seq", "wide", None),
        P("wide"),
        P("wide", None),
        P("wide", None),
        P("wide", None),
        P("wide", None),
        P("wide"),
        P("wide"),
        P("wide"),
        P(None, "wide"),
        P("wide"),
        P("wide", None),
        P("wide"),
        P("wide", "seq"),
        P("wide", "seq"),
        P("seq", "wide"),
        P(),
    )
    return jax.shard_map(body, mesh=mesh, in_specs=in_specs, out_specs=out_specs, check_vma=False)
```

```python
import functools

import jax
import jax.numpy as jnp
from jax import lax
from jax.experimental import pallas as pl
from jax.experimental.pallas import tpu as pltpu
from jax.sharding import PartitionSpec as P

BW = 256
CONV = 4
HALO = 8
BF = jnp.bfloat16
F32 = jnp.float32
LANES = 128
ROWS16 = 16
MESH = pl.DeviceIdType.MESH


def dot(left, right):
    return jnp.dot(left, right, preferred_element_type=F32)


def contract_last(left, right):
    return lax.dot_general(left, right, (((1,), (1,)), ((), ())), preferred_element_type=F32)


def contract_rows(left, right):
    return lax.dot_general(left, right, (((0,), (0,)), ((), ())), preferred_element_type=F32)


def swap(values, mask):
    return lax.ppermute(values, "seq", [(i, i ^ mask) for i in range(lax.axis_size("seq"))])


def inverse_rms(values):
    return lax.rsqrt(jnp.mean(values * values, axis=-1, keepdims=True) + 1e-06)


def rms_norm(values, gain):
    return values * inverse_rms(values) * gain


def sigmoid(values):
    return 0.5 * jnp.tanh(0.5 * values) + 0.5


def gelu_parts(values):
    c = 0.7978845608028654
    sq = values * values
    t = jnp.tanh(c * values * (1.0 + 0.044715 * sq))
    half = 0.5 * (1.0 + t)
    return values * half, half + 0.5 * values * (1.0 - t * t) * (c * (1.0 + 3.0 * 0.044715 * sq))


def drop_of(rate_log):
    u = 2.0 * rate_log
    series = 1.0 + u * (1.0 / 8.0)
    for n in (7, 6, 5, 4, 3, 2):
        series = 1.0 + u * series * (1.0 / n)
    return jnp.where(u > -0.4, -u * series, 1.0 - jnp.exp(u))


def scan_rows(rate, drive, reverse):
    rows, lanes = rate.shape
    count = rows // 8
    rate = rate.reshape(count, 8, lanes)
    drive = drive.reshape(count, 8, lanes)
    row = lax.broadcasted_iota(jnp.int32, (count, 8, lanes), 1)
    for step in (1, 2, 4):
        shift = 8 - step if reverse else step
        keep = row < 8 - step if reverse else row >= step
        drive = drive + rate * jnp.where(keep, pltpu.roll(drive, shift, 1), 0.0)
        rate = rate * jnp.where(keep, pltpu.roll(rate, shift, 1), 1.0)
    state, reach = jnp.zeros((1, lanes), F32), jnp.ones((1, lanes), F32)
    states, reaches = [None] * count, [None] * count
    last = 0 if reverse else 7
    for i in reversed(range(count)) if reverse else range(count):
        states[i] = drive[i] + rate[i] * state
        reaches[i] = rate[i] * reach
        state = states[i][last : last + 1]
        reach = reaches[i][last : last + 1]
    return jnp.concatenate(states, axis=0), jnp.concatenate(reaches, axis=0)


def forward_kernel(
    off_ref, x_ref, edge_ref, gates_ref, chan_ref,
    forget_out, admit_out, conv_out_ref, rate_out, local_out, reach_out, ends_out,
    logits,
):
    q = pl.program_id(0)
    tokens = x_ref.shape[0]
    share = chan_ref.shape[1]
    blocks = x_ref.shape[1] // BW
    off = pl.multiple_of(off_ref[0], LANES)
    for b in range(blocks):
        cols = slice(b * BW, (b + 1) * BW)
        mixed = jnp.dot(x_ref[:, cols], gates_ref[cols, :], preferred_element_type=F32)
        logits[0, :, cols] = mixed[:, :BW]
        logits[1, :, cols] = mixed[:, BW:]
    for j in range(share // LANES):
        lanes = slice(j * LANES, (j + 1) * LANES)
        here = pl.ds(pl.multiple_of(off + j * LANES, LANES), LANES)
        chan = [chan_ref[i : i + 1, lanes] for i in range(8)]
        forget = (logits[0, :, here] + chan[0]).astype(BF)
        admit = (logits[1, :, here] + chan[1]).astype(BF)
        forget_out[:, lanes] = forget
        admit_out[:, lanes] = admit
        edge = edge_ref[pl.ds(pl.multiple_of(q * HALO, HALO), HALO), here]
        padded = jnp.concatenate([edge, x_ref[:, here].astype(F32)], axis=0)
        conv = chan[3] + chan[4] * padded[HALO:]
        for k in range(1, CONV):
            conv = conv + chan[4 + k] * pltpu.roll(padded, k, 0)[HALO:]
        conv_out_ref[:, lanes] = conv
        rate_log = -8.0 * chan[2] * (0.1 + 0.9 * sigmoid(forget.astype(F32)))
        rate = jnp.exp(rate_log)
        drive = jnp.sqrt(drop_of(rate_log)) * sigmoid(admit.astype(F32)) * conv
        state, reach = scan_rows(rate, drive, False)
        rate_out[:, lanes] = rate
        local_out[:, lanes] = state
        reach_out[:, lanes] = reach
        ends_out[0, 0, :, lanes] = reach[tokens - 1 :]
        ends_out[0, 1, :, lanes] = state[tokens - 1 :]


def whole(shape):
    return pl.BlockSpec(shape, lambda q: (0,) * len(shape))


def per_seq(width):
    return pl.BlockSpec((1, 1, width), lambda q: (q, 0, 0))


def temporal_forward(off, x_win, edge, gates, chan, tokens):
    total, window = x_win.shape
    share = chan.shape[1]
    seqs = total // tokens
    part = lambda width: pl.BlockSpec((tokens, width), lambda q: (q, 0))
    return pl.pallas_call(
        forward_kernel,
        grid=(seqs,),
        in_specs=[
            pl.BlockSpec(memory_space=pltpu.SMEM),
            part(window),
            whole(edge.shape),
            whole(gates.shape),
            whole(chan.shape),
        ],
        out_specs=[
            part(share), part(share), part(share), part(share), part(share), part(share),
            pl.BlockSpec((1, 2, 1, share), lambda q: (q, 0, 0, 0)),
        ],
        out_shape=[
            jax.ShapeDtypeStruct((total, share), BF),
            jax.ShapeDtypeStruct((total, share), BF),
            jax.ShapeDtypeStruct((total, share), F32),
            jax.ShapeDtypeStruct((total, share), F32),
            jax.ShapeDtypeStruct((total, share), F32),
            jax.ShapeDtypeStruct((total, share), F32),
            jax.ShapeDtypeStruct((seqs, 2, 1, share), F32),
        ],
        scratch_shapes=[
            pltpu.VMEM((2, tokens, window), F32),
        ],
        compiler_params=pltpu.CompilerParams(vmem_limit_bytes=48 * 1024 * 1024),
        cost_estimate=pl.CostEstimate(flops=1000, bytes_accessed=1000, transcendentals=0),
        name="temporal_forward",
    )(off, x_win, edge, gates, chan)


def partner(mask):
    s = lax.axis_index("seq")
    if mask == 1:
        other = s + 1 - 2 * (s % 2)
    else:
        other = (s + 2) % 4
    return {"seq": other}


def greet():
    barrier = pltpu.get_barrier_semaphore()
    for mask in (1, 2):
        pl.semaphore_signal(barrier, inc=1, device_id=partner(mask), device_id_type=MESH)
    pl.semaphore_wait(barrier, 2)


def sender(sends, recvs):
    def send(slot, source, target, mask):
        copy = pltpu.make_async_remote_copy(
            src_ref=source,
            dst_ref=target,
            send_sem=sends.at[slot],
            recv_sem=recvs.at[slot],
            device_id=partner(mask),
            device_id_type=MESH,
        )
        copy.start()
        return copy

    return send


def over_chunks(rows, run):
    def step(i, carry):
        run(pl.ds(pl.multiple_of(i * ROWS16, ROWS16), ROWS16))
        return carry

    lax.fori_loop(0, rows // ROWS16, step, 0)


def reduce_phase(product, send, first_slot, acc, sent, got):
    rows = acc.shape[1]
    half = rows // 2
    low, high = pl.ds(0, half), pl.ds(half, half)
    product(3, lambda cols, value: sent.__setitem__((0, slice(None), cols), value.astype(BF)))
    far_near = send(first_slot, sent.at[0, low], got.at[0, low], 1)
    far_side = send(first_slot + 1, sent.at[0, high], got.at[0, high], 2)
    product(1, lambda cols, value: acc.__setitem__((1, slice(None), cols), value))
    over_chunks(half, lambda r: sent.__setitem__((1, r), acc[1, r].astype(BF)))
    near_low = send(first_slot + 2, sent.at[1, low], got.at[1, low], 1)
    product(2, lambda cols, value: acc.__setitem__((2, slice(None), cols), value))

    def tail(k):
        def run(r):
            r = pl.ds(pl.multiple_of(r.start + half, ROWS16), ROWS16)
            sent[k, r] = acc[k, r].astype(BF)

        return run

    over_chunks(half, tail(2))
    side_high = send(first_slot + 3, sent.at[2, high], got.at[2, high], 2)
    far_side.wait_recv()

    def add_high(r):
        r = pl.ds(pl.multiple_of(r.start + half, ROWS16), ROWS16)
        sent[1, r] = (acc[1, r] + got[0, r].astype(F32)).astype(BF)

    over_chunks(half, add_high)
    near_high = send(first_slot + 4, sent.at[1, high], got.at[1, high], 1)
    far_near.wait_recv()

    def add_low(r):
        sent[2, r] = (acc[2, r] + got[0, r].astype(F32)).astype(BF)

    over_chunks(half, add_low)
    side_low = send(first_slot + 5, sent.at[2, low], got.at[2, low], 2)
    product(0, lambda cols, value: acc.__setitem__((0, slice(None), cols), value))
    arriving = [near_low, side_high, near_high, side_low]
    for copy in arriving:
        copy.wait_recv()
    return [far_near, far_side] + arriving


def both_ways(send, slot, source, out):
    half = source.shape[0] // 2
    low, high = pl.ds(0, half), pl.ds(half, half)
    return [
        send(slot, source.at[low], out.at[1, low], 1),
        send(slot + 1, source.at[high], out.at[2, high], 2),
        send(slot + 2, source.at[high], out.at[1, high], 1),
        send(slot + 3, source.at[low], out.at[2, low], 2),
    ]


def pass_on(send, slot, out, copies):
    half = out.shape[1] // 2
    low, high = pl.ds(0, half), pl.ds(half, half)
    copies[0].wait_recv()
    far_low = send(slot + 4, out.at[1, low], out.at[3, low], 2)
    copies[1].wait_recv()
    far_high = send(slot + 5, out.at[2, high], out.at[3, high], 1)
    return copies + [far_low, far_high]


def settle(copies):
    for copy in copies[2:]:
        copy.wait_recv()
    for copy in copies:
        copy.wait_send()


def at_seq(k):
    s = lax.axis_index("seq")
    return s if k == 0 else 3 - s if k == 3 else partner(k)["seq"]


def product_of(left, right, contract, rows, tile, ready=None):
    def product(k, store):
        def step(c, carry):
            cols = pl.ds(pl.multiple_of(c * tile, tile), tile)
            if ready is not None and k == 3:
                ready(c)
            total = None
            for a, b in zip(left, right):
                part = b[cols, :] if contract else b[:, cols]
                value = lax.dot_general(
                    a[k * rows : (k + 1) * rows, :],
                    part,
                    (((1,), (1 if contract else 0,)), ((), ())),
                    preferred_element_type=F32,
                )
                total = value if total is None else total + value
            store(cols, total)
            return carry

        width = right[0].shape[0 if contract else 1]
        lax.fori_loop(0, width // tile, step, 0)

    return product


def rms_parts(values):
    return lax.rsqrt(jnp.mean(values * values, axis=-1, keepdims=True) + 1e-06)


def stream_kernel(
    mixed_ref, weight_ref, flat_ref, gain_ref,
    stream_out, temporal_out, normed_out,
    acc, sent, got, sends, recvs,
):
    rows = flat_ref.shape[0]
    greet()
    send = sender(sends, recvs)
    copies = reduce_phase(
        product_of([mixed_ref], [weight_ref], False, rows, 512), send, 0, acc, sent, got
    )

    def finish(r):
        temporal = acc[0, r] + got[1, r].astype(F32) + got[2, r].astype(F32)
        temporal_out[r] = temporal
        stream = flat_ref[r].astype(F32) + temporal
        stream_out[r] = stream
        normed_out[0, r] = (stream * rms_parts(stream) * gain_ref[...]).astype(BF)

    over_chunks(rows, finish)
    gathered = pass_on(send, 6, normed_out, both_ways(send, 6, normed_out.at[0], normed_out))
    settle(gathered)
    for copy in copies:
        copy.wait_send()


def exchange_scratch(rows, width, copies):
    return [
        pltpu.VMEM((3, rows, width), F32),
        pltpu.VMEM((3, rows, width), BF),
        pltpu.VMEM((3, rows, width), BF),
        pltpu.SemaphoreType.DMA((copies,)),
        pltpu.SemaphoreType.DMA((copies,)),
    ]


def remote_call(kernel, name, ident, outs, operands, scratch, far=0):
    return pl.pallas_call(
        kernel,
        in_specs=[pl.BlockSpec(memory_space=pltpu.VMEM)] * (len(operands) - far)
        + [pl.BlockSpec(memory_space=pl.ANY)] * far,
        out_specs=[pl.BlockSpec(memory_space=pltpu.VMEM)] * len(outs),
        out_shape=[jax.ShapeDtypeStruct(shape, kind) for shape, kind in outs],
        scratch_shapes=scratch,
        compiler_params=pltpu.CompilerParams(
            collective_id=ident, has_side_effects=True, vmem_limit_bytes=60 * 1024 * 1024
        ),
        cost_estimate=pl.CostEstimate(flops=1000, bytes_accessed=1000, transcendentals=0),
        name=name,
    )(*operands)


def stream_and_norm(mixed, weight, flat, gain):
    rows, width = flat.shape
    groups = mixed.shape[0] // rows
    return remote_call(
        stream_kernel,
        "stream_and_norm",
        1,
        [((rows, width), F32), ((rows, width), F32), ((groups, rows, width), BF)],
        (mixed, weight, flat, gain),
        exchange_scratch(rows, width, 12),
    )


def rows_kernel(upstream_ref, down_ref, gate_ref, up_ref, rows_out):
    tile = gate_ref.shape[1]
    hidden = rows_out.shape[1] // 2
    grad = lax.dot_general(
        upstream_ref[...], down_ref[...], (((1,), (1,)), ((), ())), preferred_element_type=F32
    )
    value, slope = gelu_parts(gate_ref[...])
    at = pl.multiple_of(pl.program_id(0) * tile, tile)
    rows_out[:, pl.ds(at, tile)] = (grad * up_ref[...] * slope).astype(BF)
    rows_out[:, pl.ds(hidden + at, tile)] = (grad * value).astype(BF)


def mlp_rows(upstream, down, gate_up):
    total, width = upstream.shape
    hidden = down.shape[0]
    tile = BW
    half = hidden // tile
    return pl.pallas_call(
        rows_kernel,
        grid=(half,),
        in_specs=[
            whole(upstream.shape),
            pl.BlockSpec((tile, width), lambda j: (j, 0)),
            pl.BlockSpec((total, tile), lambda j: (0, j)),
            pl.BlockSpec((total, tile), lambda j: (0, half + j)),
        ],
        out_specs=whole((total, 2 * hidden)),
        out_shape=jax.ShapeDtypeStruct((total, 2 * hidden), BF),
        compiler_params=pltpu.CompilerParams(vmem_limit_bytes=48 * 1024 * 1024),
        cost_estimate=pl.CostEstimate(flops=1000, bytes_accessed=1000, transcendentals=0),
        name="mlp_rows",
    )(upstream, down, gate_up, gate_up)


def stream_back_kernel(
    rows_ref, stream_ref, gain_ref, upstream_ref, weight_far, hidden_far, down_far, out_far,
    grad_out, low_out, gain_out, feed_out, mixed_out,
    weight_ref, hidden_ref, down_ref, out_ref, fetches,
    acc, sent, got, sends, recvs,
):
    rows, width = stream_ref.shape
    tile = 512

    def fetch(c):
        part = pl.ds(pl.multiple_of(c * tile, tile), tile)
        return pltpu.make_async_copy(weight_far.at[part], weight_ref.at[part], fetches.at[c])

    count = width // tile
    for c in range(count):
        fetch(c).start()
    late = [
        pltpu.make_async_copy(hidden_far, hidden_ref, fetches.at[count]),
        pltpu.make_async_copy(down_far, down_ref, fetches.at[count + 1]),
        pltpu.make_async_copy(out_far, out_ref, fetches.at[count + 2]),
    ]
    for copy in late:
        copy.start()
    greet()
    send = sender(sends, recvs)
    product = product_of(
        [rows_ref], [weight_ref], True, rows, tile, ready=lambda c: fetch(c).wait()
    )
    copies = reduce_phase(product, send, 0, acc, sent, got)
    gain_out[...] = jnp.zeros_like(gain_out)

    def finish(r):
        grad = acc[0, r] + got[1, r].astype(F32) + got[2, r].astype(F32)
        stream = stream_ref[r]
        inv = rms_parts(stream)
        scaled = grad * gain_ref[...]
        inner = jnp.mean(stream * scaled, axis=-1, keepdims=True)
        total = upstream_ref[r].astype(F32) + inv * scaled - stream * (inv * inv * inv * inner)
        grad_out[r] = total
        low_out[0, r] = total.astype(BF)
        gained = grad * stream * inv
        gain_out[...] += gained[:8] + gained[8:]

    over_chunks(rows, finish)
    gathered = both_ways(send, 6, low_out.at[0], low_out)
    for copy in late:
        copy.wait()
    feed = product_of([hidden_ref], [down_ref], False, rows, tile)

    def feed_block(k):
        feed(k, lambda cols, value: feed_out.__setitem__((k, slice(None), cols), value.astype(BF)))

    def mixed_block(k):
        mixed_out[k] = lax.dot_general(
            low_out[k], out_ref[...], (((1,), (1,)), ((), ())), preferred_element_type=F32
        )

    feed_block(3)
    gathered = pass_on(send, 6, low_out, gathered)
    feed_block(0)
    mixed_block(0)
    feed_block(1)
    feed_block(2)
    near_low, side_high, near_high, side_low, far_low, far_high = gathered
    near_high.wait_recv()
    mixed_block(1)
    side_low.wait_recv()
    mixed_block(2)
    far_low.wait_recv()
    far_high.wait_recv()
    mixed_block(3)
    for copy in gathered:
        copy.wait_send()
    for copy in copies:
        copy.wait_send()


def stream_back(rows_all, weight, stream, gain, upstream, hidden, down, out_rows):
    rows, width = stream.shape
    groups = rows_all.shape[0] // rows
    return remote_call(
        stream_back_kernel,
        "stream_back",
        2,
        [
            ((rows, width), F32),
            ((groups, rows, width), BF),
            ((8, width), F32),
            ((groups, rows, width), BF),
            ((groups, rows, out_rows.shape[0]), F32),
        ],
        (rows_all, stream, gain, upstream, weight, hidden, down, out_rows),
        [
            pltpu.VMEM(weight.shape, BF),
            pltpu.VMEM(hidden.shape, BF),
            pltpu.VMEM(down.shape, BF),
            pltpu.VMEM(out_rows.shape, BF),
            pltpu.SemaphoreType.DMA((width // 512 + 3,)),
        ]
        + exchange_scratch(rows, width, 12),
        far=4,
    )


def inputs_back_kernel(
    branch_ref, y_ref, weight_ref, flat_ref, gain_ref, mixed_ref, low_ref,
    grad_out, gain_out, columns_out,
    columns_ref, acc, sent, got, sends, recvs,
):
    rows = flat_ref.shape[0]
    s = lax.axis_index("seq")
    count, columns = columns_ref.shape[0], columns_out.shape[1]
    barrier = pltpu.get_barrier_semaphore()
    for k in (1, 2, 3):
        pl.semaphore_signal(barrier, inc=1, device_id={"seq": at_seq(k)}, device_id_type=MESH)
    pl.semaphore_wait(barrier, 3)
    send = sender(sends, recvs)
    here = pl.ds(pl.multiple_of(s * count, ROWS16), count)

    def columns_of(k):
        return columns_ref.at[:, pl.ds(pl.multiple_of(at_seq(k) * columns, LANES), columns)]

    moved = []
    for k in (3, 1, 2):
        copy = pltpu.make_async_remote_copy(
            src_ref=columns_of(k),
            dst_ref=columns_out.at[here],
            send_sem=sends.at[5 + k],
            recv_sem=recvs.at[5 + k],
            device_id={"seq": at_seq(k)},
            device_id_type=MESH,
        )
        moved.append(copy)
    window = branch_ref.shape[1]
    weights = [weight_ref.at[:, :window], weight_ref.at[:, window:]]
    product = product_of([branch_ref, y_ref], weights, True, rows, 512)

    def product_and_move(k, store):
        if k == 0:
            left = mixed_ref[...].T
            tile = 512
            for c in range(columns_ref.shape[1] // tile):
                cols = slice(c * tile, (c + 1) * tile)
                columns_ref[:, cols] = jnp.dot(
                    left, low_ref[:, cols], preferred_element_type=F32
                ).astype(BF)
            for copy in moved:
                copy.start()
        product(k, store)

    copies = reduce_phase(product_and_move, send, 0, acc, sent, got)
    columns_out[here] = columns_of(0)[...]
    gain_out[...] = jnp.zeros_like(gain_out)

    def finish(r):
        grad = acc[0, r] + got[1, r].astype(F32) + got[2, r].astype(F32)
        values = flat_ref[r].astype(F32)
        inv = rms_parts(values)
        scaled = grad * gain_ref[...]
        inner = jnp.mean(values * scaled, axis=-1, keepdims=True)
        grad_out[r] = inv * scaled - values * (inv * inv * inv * inner)
        gained = grad * values * inv
        gain_out[...] += gained[:8] + gained[8:]

    over_chunks(rows, finish)
    for copy in moved:
        copy.wait_recv()
    for copy in copies + moved:
        copy.wait_send()


def inputs_back(branch_rows, y_rows, weight, flat, gain, mixed, low):
    rows, width = flat.shape
    count, columns = mixed.shape[1], low.shape[1]
    return remote_call(
        inputs_back_kernel,
        "inputs_back",
        3,
        [((rows, width), F32), ((8, width), F32), ((4 * count, columns // 4), BF)],
        (branch_rows, y_rows, weight, flat, gain, mixed, low),
        [pltpu.VMEM((count, columns), BF)] + exchange_scratch(rows, width, 9),
    )


def start_kernel(inputs_ref, inputs_out, edge_out, sends, recvs):
    seqs = edge_out.shape[1] // ROWS16
    tokens = inputs_ref.shape[0] // seqs
    w = lax.axis_index("wide")
    wide = lax.axis_size("wide")
    after, before = lax.rem(w + 1, wide), lax.rem(w + wide - 1, wide)
    barrier = pltpu.get_barrier_semaphore()
    for mask in (1, 2):
        pl.semaphore_signal(barrier, inc=1, device_id=partner(mask), device_id_type=MESH)
    pl.semaphore_signal(barrier, inc=1, device_id={"wide": before}, device_id_type=MESH)
    pl.semaphore_wait(barrier, 3)
    send = sender(sends, recvs)
    edges = []
    for q in range(seqs):
        copy = pltpu.make_async_remote_copy(
            src_ref=inputs_ref.at[pl.ds((q + 1) * tokens - ROWS16, ROWS16)],
            dst_ref=edge_out.at[0, pl.ds(q * ROWS16, ROWS16)],
            send_sem=sends.at[12 + q],
            recv_sem=recvs.at[12 + q],
            device_id={"wide": after},
            device_id_type=MESH,
        )
        copy.start()
        edges.append(copy)
    blocks = both_ways(send, 0, inputs_ref, inputs_out)
    inputs_out[0] = inputs_ref[...]
    for copy in edges:
        copy.wait_recv()
        copy.wait_send()
    edges = both_ways(send, 6, edge_out.at[0], edge_out)
    blocks = pass_on(send, 0, inputs_out, blocks)
    edges = pass_on(send, 6, edge_out, edges)
    settle(blocks)
    settle(edges)


def start(inputs, groups, seqs):
    rows, width = inputs.shape
    copies = 12 + seqs
    return remote_call(
        start_kernel,
        "start",
        6,
        [((groups, rows, width), BF), ((groups, seqs * ROWS16, width), BF)],
        (inputs,),
        [pltpu.SemaphoreType.DMA((copies,)), pltpu.SemaphoreType.DMA((copies,))],
    )


def middle_kernel(
    grad_ref, y_ref, local_ref, reach_ref, carry_ref, rate_ref, chan_ref, ends_ref,
    edge_ref, gates_ref, valid_ref, feed_ref,
    conv_far, forget_far, admit_far, x_far, stream_far, temporal_far,
    y_rows_out, branch_out, forget_out, admit_out, sums_out, result_out, squares_out,
    adjoint, later, heads, packet, packet_in, tails, after, conv_rows,
    conv_ref, forget_ref, admit_ref, x_ref, stream_ref, temporal_ref,
    sent, got, fetches, sends, recvs, head_sends, head_recvs,
):
    wide, seqs, share = ends_ref.shape
    tokens = grad_ref.shape[0] // seqs
    window = x_ref.shape[1]
    rows, width = stream_ref.shape
    half = rows // 2
    low, high = pl.ds(0, half), pl.ds(half, half)
    w = lax.axis_index("wide")
    first_channel = lax.axis_index("seq") * share
    base = jnp.minimum(first_channel // BW * BW, lax.axis_size("seq") * share - window)
    off = pl.multiple_of(first_channel - base, LANES)
    fetched = []
    for i, (far, near) in enumerate(
        (
            (conv_far, conv_ref),
            (forget_far, forget_ref),
            (admit_far, admit_ref),
            (x_far, x_ref),
            (stream_far, stream_ref),
            (temporal_far, temporal_ref),
        )
    ):
        copy = pltpu.make_async_copy(far, near, fetches.at[i])
        copy.start()
        fetched.append(copy)

    barrier = pltpu.get_barrier_semaphore()
    for mask in (1, 2):
        pl.semaphore_signal(barrier, inc=1, device_id=partner(mask), device_id_type=MESH)

    def tell(i, carry):
        other = lax.rem(w + i, wide)
        pl.semaphore_signal(barrier, inc=1, device_id={"wide": other}, device_id_type=MESH)
        return carry

    lax.fori_loop(1, wide, tell, 0)
    pl.semaphore_wait(barrier, wide + 1)
    send = sender(sends, recvs)
    far_near = send(0, feed_ref.at[3, low], got.at[0, low], 1)
    far_side = send(1, feed_ref.at[3, high], got.at[0, high], 2)
    near_low = send(2, feed_ref.at[1, low], got.at[1, low], 1)
    side_high = send(3, feed_ref.at[2, high], got.at[2, high], 2)

    row = lax.broadcasted_iota(jnp.int32, (tokens, LANES), 0)
    fetched[1].wait()
    fetched[2].wait()

    def scan_step(q, carry):
        r = pl.ds(pl.multiple_of(q * tokens, tokens), tokens)
        head_rows = pl.ds(pl.multiple_of(q * tokens, tokens), ROWS16)
        for j in range(share // LANES):
            lanes = slice(j * LANES, (j + 1) * LANES)
            grad = grad_ref[r, lanes]
            value, slope = gelu_parts(y_ref[r, lanes])
            state = (local_ref[r, lanes] + reach_ref[r, lanes] * carry_ref[q, :, lanes]).astype(BF)
            y_rows_out[r, lanes] = (grad * state.astype(F32) * slope).astype(BF)
            state_grad = (grad * value).astype(BF).astype(F32)
            rate = rate_ref[r, lanes]
            ahead = jnp.where(row == tokens - 1, 1.0, pltpu.roll(rate, tokens - 1, 0))
            adjoints, laters = scan_rows(ahead, state_grad, True)
            adjoint[r, lanes] = adjoints
            later[r, lanes] = laters
            tails[q, :, lanes] = rate[:1] * adjoints[:1]
            forget_sig = sigmoid(forget_ref[head_rows, lanes].astype(F32)[:HALO])
            admit_sig = sigmoid(admit_ref[head_rows, lanes].astype(F32)[:HALO])
            rate_log = -8.0 * chan_ref[2:3, lanes] * (0.1 + 0.9 * forget_sig)
            gain = jnp.sqrt(drop_of(rate_log)) * admit_sig
            for i, values in enumerate((adjoints[:HALO] * gain, laters[:HALO] * gain)):
                for t in range(CONV - 1):
                    packet[i, t, q, :, lanes] = values[t : t + 1]
        return carry

    lax.fori_loop(0, seqs, scan_step, 0)
    for q in range(seqs):
        heads[0, q : q + 1, :] = tails[q]

    def head_copy(i):
        return pltpu.make_async_remote_copy(
            src_ref=heads.at[0],
            dst_ref=heads.at[i],
            send_sem=head_sends.at[i],
            recv_sem=head_recvs.at[i],
            device_id={"wide": lax.rem(w + i, wide)},
            device_id_type=MESH,
        )

    def head_start(i, carry):
        head_copy(i).start()
        return carry

    def head_wait(i, carry):
        copy = head_copy(i)
        copy.wait_recv()
        copy.wait_send()
        return carry

    lax.fori_loop(1, wide, head_start, 0)
    packets = pltpu.make_async_remote_copy(
        src_ref=packet,
        dst_ref=packet_in,
        send_sem=sends.at[6],
        recv_sem=recvs.at[6],
        device_id={"wide": lax.rem(w + wide - 1, wide)},
        device_id_type=MESH,
    )
    packets.start()

    far_side.wait_recv()
    sent[0] = (feed_ref[1, high].astype(F32) + got[0, high].astype(F32)).astype(BF)
    near_high = send(4, sent.at[0], got.at[1, high], 1)
    far_near.wait_recv()
    sent[1] = (feed_ref[2, low].astype(F32) + got[0, low].astype(F32)).astype(BF)
    side_low = send(5, sent.at[1], got.at[2, low], 2)

    lax.fori_loop(1, wide, head_wait, 0)
    packets.wait_recv()
    packets.wait_send()

    def tail_step(i, carry):
        tail, next_tail = carry
        j = wide - i
        stepped = ends_ref[j] * tail + heads[lax.rem(w + i, wide)]
        return jnp.where(j > w, stepped, tail), jnp.where(j > w + 1, stepped, next_tail)

    zero = jnp.zeros((seqs, share), F32)
    tail, next_tail = lax.fori_loop(1, wide, tail_step, (zero, zero))
    next_tail = jnp.where(w == wide - 1, 0.0, next_tail)
    inside = jnp.where(w == wide - 1, 0.0, 1.0)
    after[...] = jnp.zeros_like(after)
    for q in range(seqs):
        tails[q] = tail[q : q + 1]
        for t in range(CONV - 1):
            after[q * HALO + t : q * HALO + t + 1, :] = (
                inside * packet_in[0, t, q] + packet_in[1, t, q] * next_tail[q : q + 1]
            )

    forget_out[...] = jnp.zeros_like(forget_out)
    admit_out[...] = jnp.zeros_like(admit_out)
    conv_rows[...] = jnp.zeros_like(conv_rows)
    sums_out[...] = jnp.zeros_like(sums_out)
    fetched[0].wait()
    fetched[3].wait()

    def rows_step(q, carry):
        r = pl.ds(pl.multiple_of(q * tokens, tokens), tokens)
        pack = pl.ds(pl.multiple_of(q * HALO, HALO), HALO)
        for j in range(share // LANES):
            lanes = slice(j * LANES, (j + 1) * LANES)
            here = pl.ds(pl.multiple_of(off + j * LANES, LANES), LANES)
            chan = [chan_ref[i : i + 1, lanes] for i in range(8)]
            start = carry_ref[q, :, lanes]
            carried = local_ref[r, lanes] + reach_ref[r, lanes] * start
            before = jnp.where(row == 0, start, pltpu.roll(carried, 1, 0))
            full = adjoint[r, lanes] + later[r, lanes] * tails[q, :, lanes]
            forget_sig = sigmoid(forget_ref[r, lanes].astype(F32))
            admit_sig = sigmoid(admit_ref[r, lanes].astype(F32))
            span = 0.1 + 0.9 * forget_sig
            rate = rate_ref[r, lanes]
            scale = jnp.sqrt(drop_of(-8.0 * chan[2] * span))
            gated = admit_sig * conv_ref[r, lanes]
            log_grad = full * (rate * before - rate * rate / scale * gated)
            conv_grad = full * scale * admit_sig
            forget_rows = (
                log_grad * (-7.2) * chan[2] * forget_sig * (1.0 - forget_sig)
            ).astype(BF)
            admit_rows = (full * scale * gated * (1.0 - admit_sig)).astype(BF)
            forget_out[r, here] = forget_rows
            admit_out[r, here] = admit_rows
            ahead = jnp.concatenate([conv_grad, after[pack, lanes]], axis=0)
            back = chan[4] * conv_grad
            for k in range(1, CONV):
                back = back + chan[4 + k] * pltpu.roll(ahead, tokens + HALO - k, 0)[:tokens]
            conv_rows[:, here] = back.astype(BF).astype(F32)
            padded = jnp.concatenate(
                [edge_ref[pack, here], x_ref[r, here].astype(F32)], axis=0
            )
            sums = [
                forget_rows.astype(F32),
                admit_rows.astype(F32),
                log_grad * (-8.0) * span,
                conv_grad,
                conv_grad * padded[HALO:],
            ] + [conv_grad * pltpu.roll(padded, k, 0)[HALO:] for k in range(1, CONV)]
            sums_out[:, lanes] += jnp.concatenate(
                [jnp.sum(v, axis=0, keepdims=True) for v in sums], axis=0
            )
        for b in range(window // BW):
            cols = slice(b * BW, (b + 1) * BW)
            back = conv_rows[:, cols]
            for source, at in ((forget_out, 0), (admit_out, BW)):
                back = back + lax.dot_general(
                    source[r, cols],
                    gates_ref[cols, at : at + BW],
                    (((1,), (1,)), ((), ())),
                    preferred_element_type=F32,
                )
            branch_out[r, cols] = back.astype(BF)
        return carry

    lax.fori_loop(0, seqs, rows_step, 0)
    fetched[4].wait()
    fetched[5].wait()
    for copy in (near_low, side_high, near_high, side_low):
        copy.wait_recv()
    squares_out[...] = jnp.zeros_like(squares_out)

    def finish(r):
        feed = feed_ref[0, r].astype(F32) + got[1, r].astype(F32) + got[2, r].astype(F32)
        result = stream_ref[r] + feed
        result_out[r] = result
        valid = valid_ref[r]
        for i, values in enumerate((result, temporal_ref[r], feed)):
            square = valid * values * values
            squares_out[i] += square[:8] + square[8:]

    over_chunks(rows, finish)
    for copy in (far_near, far_side, near_low, side_high, near_high, side_low):
        copy.wait_send()


def middle(
    grad, y, local, reach, carry, rate, chan, ends, edge, gates, valid, feed,
    conv, forget, admit, x_win, stream, temporal,
):
    total, share = grad.shape
    window = x_win.shape[1]
    rows, width = stream.shape
    wide, seqs = ends.shape[:2]
    tokens = total // seqs
    vmem = pl.BlockSpec(memory_space=pltpu.VMEM)
    anywhere = pl.BlockSpec(memory_space=pl.ANY)
    outs = [
        ((total, share), BF),
        ((total, window), BF),
        ((total, window), BF),
        ((total, window), BF),
        ((8, share), F32),
        ((rows, width), F32),
        ((3, 8, width), F32),
    ]
    return pl.pallas_call(
        middle_kernel,
        in_specs=[vmem] * 12 + [anywhere] * 6,
        out_specs=[vmem] * len(outs),
        out_shape=[jax.ShapeDtypeStruct(shape, kind) for shape, kind in outs],
        scratch_shapes=[
            pltpu.VMEM((total, share), F32),
            pltpu.VMEM((total, share), F32),
            pltpu.VMEM((wide, seqs, share), F32),
            pltpu.VMEM((2, CONV - 1, seqs, 1, share), F32),
            pltpu.VMEM((2, CONV - 1, seqs, 1, share), F32),
            pltpu.VMEM((seqs, 1, share), F32),
            pltpu.VMEM((seqs * HALO, share), F32),
            pltpu.VMEM((tokens, window), F32),
            pltpu.VMEM((total, share), F32),
            pltpu.VMEM((total, share), BF),
            pltpu.VMEM((total, share), BF),
            pltpu.VMEM((total, window), BF),
            pltpu.VMEM((rows, width), F32),
            pltpu.VMEM((rows, width), F32),
            pltpu.VMEM((2, rows // 2, width), BF),
            pltpu.VMEM((3, rows, width), BF),
            pltpu.SemaphoreType.DMA((6,)),
            pltpu.SemaphoreType.DMA((7,)),
            pltpu.SemaphoreType.DMA((7,)),
            pltpu.SemaphoreType.DMA((wide,)),
            pltpu.SemaphoreType.DMA((wide,)),
        ],
        compiler_params=pltpu.CompilerParams(
            collective_id=7, has_side_effects=True, vmem_limit_bytes=60 * 1024 * 1024
        ),
        cost_estimate=pl.CostEstimate(flops=1000, bytes_accessed=1000, transcendentals=0),
        name="middle",
    )(
        grad, y, local, reach, carry[:, None, :], rate, chan, ends, edge, gates, valid, feed,
        conv, forget, admit, x_win, stream, temporal,
    )


def grads_kernel(
    bases, normed_ref, y_ref, branch_ref, x_ref, forget_ref, admit_ref,
    stacked_out,
    gates, blocks, gate_total, sends, recvs,
):
    step = pl.program_id(0)
    wide, stacked_rows, quarter = stacked_out.shape
    window = x_ref.shape[1]
    tiles = (window + y_ref.shape[1]) // LANES
    group = wide // pl.num_programs(0)
    part = normed_ref.shape[1] // group
    room = stacked_rows - tiles * part
    share = gate_total.shape[0] // wide

    def quarter_of(k):
        return pl.ds(pl.multiple_of(at_seq(k) * quarter, LANES), quarter)

    def exchange(k):
        return pltpu.make_async_remote_copy(
            src_ref=gates.at[:, quarter_of(k)],
            dst_ref=blocks.at[k],
            send_sem=sends.at[k],
            recv_sem=recvs.at[k],
            device_id={"seq": at_seq(k)},
            device_id_type=MESH,
        )

    @pl.when(step == 0)
    def _():
        barrier = pltpu.get_barrier_semaphore()
        for k in (1, 2, 3):
            pl.semaphore_signal(barrier, inc=1, device_id={"seq": at_seq(k)}, device_id_type=MESH)
        for b in range(window // BW):
            cols = slice(b * BW, (b + 1) * BW)
            block = x_ref[:, cols].T
            for source, at in ((forget_ref, 0), (admit_ref, BW)):
                gates[cols, at : at + BW] = jnp.dot(
                    block, source[:, cols], preferred_element_type=F32
                ).astype(BF)
        pl.semaphore_wait(barrier, 3)
        for k in (3, 1, 2):
            exchange(k).start()

    left = normed_ref[...].T
    first = 0
    for right in (branch_ref, y_ref):
        sums = jnp.dot(left, right[...], preferred_element_type=F32).astype(BF)
        count = right.shape[1] // LANES
        for g in range(group):
            for i in range(count):
                at = (first + i) * part
                stacked_out[step * group + g, at : at + part, :] = sums[
                    g * part : (g + 1) * part, i * LANES : (i + 1) * LANES
                ]
        first += count

    @pl.when(step == pl.num_programs(0) - 1)
    def _():
        gate_total[...] = jnp.zeros_like(gate_total)
        for k in range(4):
            if k:
                exchange(k).wait_recv()
            other = at_seq(k)
            base = other * 0
            for j, start_row in enumerate(bases):
                base = jnp.where(other == j, start_row, base)
            at = pl.ds(pl.multiple_of(base, 8), window)
            value = blocks[k] if k else gates[:, quarter_of(0)]
            gate_total[at, :] += value.astype(F32)
        for g in range(wide):
            value = gate_total[g * share : (g + 1) * share, :]
            if room > share:
                value = jnp.concatenate([value, jnp.zeros((room - share, quarter), F32)], axis=0)
            stacked_out[g, tiles * part :, :] = value.astype(BF)
        for k in (1, 2, 3):
            exchange(k).wait_send()


def temporal_grads(normed, y_rows, branch_rows, x_win, forget_win, admit_win, wide, bases, stacked_rows):
    total, width = normed.shape
    share, window = y_rows.shape[1], x_win.shape[1]
    quarter = 2 * BW // 4
    return pl.pallas_call(
        functools.partial(grads_kernel, bases),
        grid=(width // BW,),
        in_specs=[pl.BlockSpec((total, BW), lambda i: (0, i))]
        + [whole(v.shape) for v in (y_rows, branch_rows, x_win, forget_win, admit_win)],
        out_specs=whole((wide, stacked_rows, quarter)),
        out_shape=jax.ShapeDtypeStruct((wide, stacked_rows, quarter), BF),
        scratch_shapes=[
            pltpu.VMEM((window, 2 * BW), BF),
            pltpu.VMEM((4, window, quarter), BF),
            pltpu.VMEM((4 * share, quarter), F32),
            pltpu.SemaphoreType.DMA((4,)),
            pltpu.SemaphoreType.DMA((4,)),
        ],
        compiler_params=pltpu.CompilerParams(
            collective_id=9, has_side_effects=True, vmem_limit_bytes=48 * 1024 * 1024
        ),
        cost_estimate=pl.CostEstimate(flops=1000, bytes_accessed=1000, transcendentals=0),
        name="temporal_grads",
    )(normed, y_rows, branch_rows, x_win, forget_win, admit_win)


def place(k, block, buffer, plan, outs):
    buffer[...] = block[...].astype(F32)
    other = at_seq(k)
    for (first, count, tiles, starts), out in zip(plan, outs):
        base = other * 0
        for j, start_col in enumerate(starts):
            base = jnp.where(other == j, start_col, base)
        for i in range(tiles):
            cols = pl.ds(pl.multiple_of(base + i * LANES, LANES), LANES)
            out[:, cols] += buffer[first + i * count : first + (i + 1) * count, :]


def put(k, block, out):
    columns = block.shape[1]
    other = at_seq(k)
    for i in range(columns // LANES):
        start_col = pl.multiple_of(other * columns + i * LANES, LANES)
        out[:, pl.ds(start_col, LANES)] = block[:, i * LANES : (i + 1) * LANES]


def spread_kernel(plan, parts_ref, early_ref, late_ref, *refs):
    outs, refs = refs[: len(plan)], refs[len(plan) :]
    sums_out, blocks, buffer, *refs = refs
    wholes, refs = refs[: len(plan)], refs[len(plan) :]
    total, sums_ref, got_sums, sends, recvs, sum_sends, sum_recvs = refs
    wide = sums_ref.shape[0]
    early = early_ref.shape[1]
    sums_ref[:, :early] = early_ref[...]
    sums_ref[:, early:] = late_ref[...]
    w = lax.axis_index("wide")
    barrier = pltpu.get_barrier_semaphore()
    for mask in (1, 2):
        pl.semaphore_signal(barrier, inc=1, device_id=partner(mask), device_id_type=MESH)

    def tell(i, carry):
        other = lax.rem(w + i, wide)
        pl.semaphore_signal(barrier, inc=1, device_id={"wide": other}, device_id_type=MESH)
        return carry

    lax.fori_loop(1, wide, tell, 0)
    pl.semaphore_wait(barrier, wide + 1)
    send = sender(sends, recvs)

    def chunk(i):
        other = lax.rem(w + i, wide)
        return pltpu.make_async_remote_copy(
            src_ref=sums_ref.at[other],
            dst_ref=got_sums.at[i],
            send_sem=sum_sends.at[i],
            recv_sem=sum_recvs.at[i],
            device_id={"wide": other},
            device_id_type=MESH,
        )

    def begin(i, carry):
        chunk(i).start()
        return carry

    def finish(i, carry):
        copy = chunk(i)
        copy.wait_recv()
        copy.wait_send()
        return carry + got_sums[i]

    lax.fori_loop(1, wide, begin, 0)
    copies = both_ways(send, 0, parts_ref, blocks)
    for out in wholes:
        out[...] = jnp.zeros_like(out)
    place(0, parts_ref, buffer, plan, wholes)
    total[0] = lax.fori_loop(1, wide, finish, sums_ref[w])
    to_near = send(6, total.at[0], total.at[1], 1)
    copies = pass_on(send, 0, blocks, copies)
    to_near.wait_recv()
    total[2] = total[0] + total[1]
    to_side = send(7, total.at[2], total.at[3], 2)
    to_side.wait_recv()
    sums_out[...] = total[2] + total[3]
    settle(copies)
    for k in (1, 2, 3):
        place(k, blocks.at[k], buffer, plan, wholes)
    for out, values in zip(outs, wholes):
        out[...] = values[...].astype(BF)
    to_near.wait_send()
    to_side.wait_send()


def spread(parts, early, late, plan, shapes):
    wide = early.shape[0]
    count = early.shape[1] + late.shape[1]
    return remote_call(
        functools.partial(spread_kernel, plan),
        "spread",
        8,
        [(shape, BF) for shape in shapes] + [((count, LANES), F32)],
        (parts, early, late),
        [pltpu.VMEM((4,) + parts.shape, BF), pltpu.VMEM(parts.shape, F32)]
        + [pltpu.VMEM(shape, F32) for shape in shapes]
        + [
            pltpu.VMEM((4, count, LANES), F32),
            pltpu.VMEM((wide, count, LANES), F32),
            pltpu.VMEM((wide, count, LANES), F32),
            pltpu.SemaphoreType.DMA((8,)),
            pltpu.SemaphoreType.DMA((8,)),
            pltpu.SemaphoreType.DMA((wide,)),
            pltpu.SemaphoreType.DMA((wide,)),
        ],
    )


def last_kernel(columns_ref, columns_out, column_blocks, sends, recvs):
    greet()
    send = sender(sends, recvs)
    copies = both_ways(send, 0, columns_ref, column_blocks)
    put(0, columns_ref, columns_out)
    copies = pass_on(send, 0, column_blocks, copies)
    settle(copies)
    for k in (1, 2, 3):
        put(k, column_blocks.at[k], columns_out)


def spread_last(columns):
    count = columns.shape[0]
    columns = jnp.pad(columns, ((0, -count % 32), (0, 0)))
    (wholes,) = remote_call(
        last_kernel,
        "spread_last",
        5,
        [((columns.shape[0], 4 * columns.shape[1]), BF)],
        (columns,),
        [
            pltpu.VMEM((4,) + columns.shape, BF),
            pltpu.SemaphoreType.DMA((6,)),
            pltpu.SemaphoreType.DMA((6,)),
        ],
    )
    return wholes[:count]


def finish_kernel(
    mlp_ref, down_ref, stream_ref, first_ref, result_ref, gelu_ref, branch_ref,
    gate_out, up_out, down_out, inputs_out, result_out, gelu_out, branch_out,
):
    hidden = gate_out.shape[1]
    gate_out[...] = mlp_ref[:, :hidden].astype(F32)
    up_out[...] = mlp_ref[:, hidden:].astype(F32)
    down_out[...] = down_ref[...].astype(F32)
    inputs_out[...] = stream_ref[...] + first_ref[...]
    result_out[...] = result_ref[...].astype(BF)
    gelu_out[...] = gelu_ref[...].astype(F32)
    branch_out[...] = branch_ref[...].astype(F32)


def finish(mlp, down, stream_grad, first_back, result, gelu, branch):
    steps = max(1, min(8, mlp.shape[0] // 16))
    half = (mlp.shape[0], mlp.shape[1] // 2)
    operands = (mlp, down, stream_grad, first_back, result, gelu, branch)
    outs = [
        (half, F32), (half, F32), (down.shape, F32), (stream_grad.shape, F32),
        (result.shape, BF), (gelu.shape, F32), (branch.shape, F32),
    ]

    def part(shape):
        return pl.BlockSpec((shape[0] // steps, shape[1]), lambda i: (i, 0))

    return pl.pallas_call(
        finish_kernel,
        grid=(steps,),
        in_specs=[part(v.shape) for v in operands],
        out_specs=[part(shape) for shape, _unused in outs],
        out_shape=[jax.ShapeDtypeStruct(shape, kind) for shape, kind in outs],
        compiler_params=pltpu.CompilerParams(vmem_limit_bytes=48 * 1024 * 1024),
        cost_estimate=pl.CostEstimate(flops=1000, bytes_accessed=1000, transcendentals=0),
        name="finish",
    )(*operands)


def body(
    inputs,
    lengths,
    norm_gain,
    gelu_weight,
    branch_weight,
    forget_gates,
    admit_gates,
    forget_bias,
    admit_bias,
    decay_rate,
    conv_weight,
    conv_bias,
    out_weight,
    mlp_gain,
    gate_weight,
    up_weight,
    down_weight,
    cotangent,
):
    groups = lax.axis_size("seq")
    wide = lax.axis_size("wide")
    s = lax.axis_index("seq")
    w = lax.axis_index("wide")
    seqs, tokens, width = inputs.shape
    rows = seqs * tokens
    total = groups * rows
    all_seqs = groups * seqs
    channels = gelu_weight.shape[1]
    share = channels // groups
    window = (share + BW - 1) // BW * BW
    blocks = window // BW

    def base_of(index):
        return jnp.minimum(index * share // BW * BW, channels - window)

    base = base_of(s)
    off = s * share - base
    quarter = width // groups
    gate_cols = 2 * BW // groups

    flat_low = inputs.reshape(rows, width)
    upstream = cotangent.reshape(rows, width)
    all_low, edge_low = start(flat_low, groups, seqs)
    all_low = all_low.reshape(total, width)
    edge_low = jnp.where(w == 0, 0.0, edge_low.reshape(all_seqs * ROWS16, width).astype(F32))

    x_y_cols = lax.all_gather(
        jnp.concatenate(
            [
                lax.dynamic_slice_in_dim(branch_weight, base, window, 1),
                lax.dynamic_slice_in_dim(gelu_weight, s * share, share, 1),
            ],
            axis=1,
        ),
        "wide",
        axis=0,
        tiled=True,
    )
    dw, rw = width // wide, channels // wide
    small = jnp.concatenate(
        [norm_gain, mlp_gain, forget_bias, admit_bias, decay_rate, conv_bias, conv_weight.reshape(-1)]
    ).reshape(-1, gate_cols)
    gates_quarter = jnp.concatenate([forget_gates, admit_gates], axis=1)
    small = jnp.concatenate(
        [lax.dynamic_slice_in_dim(gates_quarter, s * gate_cols, gate_cols, 1), small], axis=0
    )
    small, edge_low, later_upstream = lax.optimization_barrier((small, edge_low, upstream))
    upstream_near = swap(later_upstream, 1)
    upstream_side = swap(later_upstream, 2)
    small = lax.all_gather(small, "wide")
    gates_quarter = small[:, :rw].reshape(channels, gate_cols)
    small = small[:, rw:].reshape(wide, -1).astype(F32)
    gain_one = small[:, :dw].reshape(1, width)
    gain_two = small[:, dw : 2 * dw].reshape(1, width)
    per_channel = small[:, 2 * dw :].reshape(wide, 8, rw).transpose(1, 0, 2).reshape(8, channels)
    per_channel = lax.dynamic_slice_in_dim(per_channel, s * share, share, 1)

    out_quarter = lax.all_gather(
        lax.dynamic_slice_in_dim(out_weight, s * quarter, quarter, 1), "wide", axis=0, tiled=True
    )
    mlp_full = lax.all_gather(
        jnp.concatenate([gate_weight, up_weight], axis=1), "wide", axis=0, tiled=True
    )
    down_full = lax.all_gather(down_weight, "wide", axis=1, tiled=True)
    hidden_units = gate_weight.shape[1]

    def in_order(parts):
        near = [jnp.where(s % 2 == 1, parts[k ^ 1], parts[k]) for k in range(groups)]
        return [jnp.where(s // 2 == 1, near[k ^ 2], near[k]) for k in range(groups)]

    def swapped(part_of):
        return [swap(part_of(s ^ k), k) if k else part_of(s) for k in range(groups)]

    gates = jnp.concatenate(
        in_order(
            swapped(lambda j: lax.dynamic_slice_in_dim(gates_quarter, base_of(j), window, 0))
        ),
        axis=1,
    )
    normed_all = rms_norm(all_low.astype(F32), gain_one).astype(BF)
    normed_edge = rms_norm(edge_low, gain_one).astype(BF)
    normed_all, upstream_near, upstream_side = lax.optimization_barrier(
        (normed_all, upstream_near, upstream_side)
    )
    half = rows // 2
    upstream_far = [swap(upstream_near[:half], 2), swap(upstream_side[half:], 1)]

    x_y = dot(normed_all, x_y_cols)
    x_win = x_y[:, :window].astype(BF)
    branch_y = x_y[:, window:]
    x_win, out_quarter, *upstream_far = lax.optimization_barrier(
        (x_win, out_quarter, *upstream_far)
    )
    upstream_all = jnp.concatenate([upstream, upstream_near, upstream_side, *upstream_far], axis=0)
    out_rows = jnp.concatenate(
        in_order(swapped(lambda j: lax.dynamic_slice_in_dim(out_quarter, j * share, share, 0))),
        axis=1,
    )
    edge_win = dot(normed_edge, x_y_cols[:, :window]).astype(BF).astype(F32)
    edge_win = edge_win.reshape(all_seqs, ROWS16, window)[:, ROWS16 - HALO :]
    edge_win = edge_win.reshape(all_seqs * HALO, window)
    offset = off.reshape(1)
    forget, admit, conv_out, rate, local, reach, ends = temporal_forward(
        offset, x_win, edge_win, gates, per_channel, tokens
    )
    ends = lax.all_gather(ends, "wide")[:, :, :, 0]
    carry = jnp.zeros((all_seqs, share), F32)
    for j in range(wide - 1):
        carry = jnp.where(j < w, ends[j, :, 0] * carry + ends[j, :, 1], carry)
    carried = local.reshape(all_seqs, tokens, share) + reach.reshape(
        all_seqs, tokens, share
    ) * carry[:, None, :]
    state = carried.astype(BF).astype(F32).reshape(total, share)

    gelu_y = jax.nn.gelu(branch_y)
    mixed_low = (state * gelu_y).astype(BF)
    stream, temporal, normed_two_all = stream_and_norm(mixed_low, out_rows, flat_low, gain_two)
    normed_two_all = normed_two_all.reshape(total, width)

    gate_up = dot(normed_two_all, mlp_full)
    gate, up_values = gate_up[:, :hidden_units], gate_up[:, hidden_units:]
    gelu_gate = jax.nn.gelu(gate)
    hidden_low = (gelu_gate * up_values).astype(BF)
    down_part = contract_rows(hidden_low, upstream_all).astype(BF)
    hidden_low, down_part, upstream_low = lax.optimization_barrier(
        (hidden_low, down_part, upstream_all)
    )
    down_grad = lax.psum_scatter(down_part, "wide", scatter_dimension=1, tiled=True)
    rows_all = mlp_rows(upstream_low, down_full, gate_up)
    mlp_part = contract_rows(normed_two_all, rows_all).astype(BF)
    rows_all, mlp_part = lax.optimization_barrier((rows_all, mlp_part))
    mlp_grad = lax.psum_scatter(mlp_part, "wide", scatter_dimension=0, tiled=True)
    stream_grad, stream_low_all, gain_two_grad, feed_parts, mixed_grad = stream_back(
        rows_all, mlp_full, stream, gain_two, upstream, hidden_low, down_full, out_rows
    )
    mixed_grad = mixed_grad.reshape(total, share)
    gain_two_grad = jnp.sum(gain_two_grad, axis=0)
    stream_low_all = stream_low_all.reshape(total, width)
    mixed_grad, down_grad = lax.optimization_barrier((mixed_grad, down_grad))
    position = w * tokens + jnp.arange(tokens, dtype=jnp.int32)
    valid = (position[None, :] < lengths[:, None]).astype(F32).reshape(rows, 1)
    y_rows, branch_rows, forget_win, admit_win, channel_grads, result, squares = middle(
        mixed_grad, branch_y, local, reach, carry, rate, per_channel, ends[:, :, 0],
        edge_win, gates, valid, feed_parts, conv_out, forget, admit, x_win, stream, temporal,
    )
    partial_sums = jnp.concatenate([jnp.sum(squares, axis=(1, 2)), jnp.sum(valid).reshape(1)])

    bases = tuple(min(j * share // BW * BW, channels - window) for j in range(groups))
    branch_size = dw * window // LANES
    gates_at = branch_size + dw * share // LANES
    stacked_rows = (gates_at + rw + 31) // 32 * 32
    stacked = temporal_grads(
        normed_all, y_rows, branch_rows, x_win, forget_win, admit_win, wide, bases, stacked_rows
    )

    def sum_over_wide(values):
        return lax.psum_scatter(values, "wide", scatter_dimension=0, tiled=True)

    stacked, mlp_grad = lax.optimization_barrier((stacked, mlp_grad))
    temporal_sum = sum_over_wide(stacked)
    channel_all = lax.dynamic_update_slice_in_dim(
        jnp.zeros((8, channels), F32), channel_grads, s * share, 1
    )
    early_sums = jnp.concatenate(
        [
            channel_all.reshape(8, wide, rw).transpose(1, 0, 2).reshape(wide, 8 * rw),
            gain_two_grad.reshape(wide, dw),
            jnp.tile(partial_sums[None, :], (wide, 1)),
        ],
        axis=1,
    )
    early_sums = jnp.pad(early_sums, ((0, 0), (0, -early_sums.shape[1] % (8 * LANES))))
    early_sums = early_sums.reshape(wide, -1, LANES)
    branch_late, early_sums = lax.optimization_barrier((branch_rows, early_sums))
    first_back, gain_one_grad, out_cols = inputs_back(
        branch_late, y_rows, x_y_cols, flat_low, gain_one, mixed_low, stream_low_all
    )
    out_sum = sum_over_wide(out_cols)
    late_sums = jnp.sum(gain_one_grad, axis=0).reshape(wide, dw)
    late_sums = jnp.pad(late_sums, ((0, 0), (0, -dw % (8 * LANES)))).reshape(wide, -1, LANES)
    temporal_sum, late_sums = lax.optimization_barrier((temporal_sum, late_sums))

    plan = (
        (0, dw, window // LANES, bases),
        (branch_size, dw, share // LANES, tuple(j * share for j in range(groups))),
        (gates_at, rw, gate_cols // LANES, tuple(j * gate_cols for j in range(groups))),
    )
    branch_whole, gelu_whole, gates_whole, sums = spread(
        temporal_sum[0],
        early_sums,
        late_sums,
        plan,
        ((dw, channels), (dw, channels), (rw, 2 * BW)),
    )
    late_at = early_sums.shape[1]
    gain_one_sum = sums[late_at:].reshape(-1)[:dw]
    sums = sums[:late_at].reshape(-1)
    channel_sums = sums[: 8 * rw].reshape(8, rw)
    gain_two_sum = sums[8 * rw : 8 * rw + dw]
    totals = sums[8 * rw + dw : 8 * rw + dw + 4]
    statistics = jnp.sqrt(totals[0:3] / (totals[3] * width))
    gate_grad, up_grad, down_grad, inputs_grad, output, gelu_whole, branch_whole = finish(
        mlp_grad, down_grad, stream_grad, first_back, result, gelu_whole, branch_whole
    )
    earlier = lax.optimization_barrier(
        (
            out_sum,
            output.reshape(seqs, tokens, width),
            inputs_grad.reshape(seqs, tokens, width),
            gain_one_sum,
            gelu_whole,
            branch_whole,
            gates_whole[:, :BW].astype(F32),
            gates_whole[:, BW:].astype(F32),
            channel_sums[0],
            channel_sums[1],
            channel_sums[2],
            channel_sums[4:8],
            channel_sums[3],
            gain_two_sum,
            gate_grad,
            up_grad,
            down_grad,
            statistics,
        )
    )
    out_sum, *outputs = earlier
    outputs.insert(12, spread_last(out_sum).astype(F32))
    return tuple(outputs)


def solution(mesh):
    in_specs = (
        P("seq", "wide", None),
        P("seq"),
        P("wide"),
        P("wide", None),
        P("wide", None),
        P("wide", None),
        P("wide", None),
        P("wide"),
        P("wide"),
        P("wide"),
        P(None, "wide"),
        P("wide"),
        P("wide", None),
        P("wide"),
        P("wide", "seq"),
        P("wide", "seq"),
        P("seq", "wide"),
        P("seq", "wide", None),
    )
    out_specs = (
        P("seq", "wide", None),
        P("seq", "wide", None),
        P("wide"),
        P("wide", None),
        P("wide", None),
        P("wide", None),
        P("wide", None),
        P("wide"),
        P("wide"),
        P("wide"),
        P(None, "wide"),
        P("wide"),
        P("wide", None),
        P("wide"),
        P("wide", "seq"),
        P("wide", "seq"),
        P("seq", "wide"),
        P(),
    )
    return jax.shard_map(body, mesh=mesh, in_specs=in_specs, out_specs=out_specs, check_vma=False)
```

```python
import functools

import jax
import jax.numpy as jnp
from jax import lax
from jax.experimental import pallas as pl
from jax.experimental.pallas import tpu as pltpu
from jax.sharding import PartitionSpec as P

BW = 256
CONV = 4
HALO = 8
BF = jnp.bfloat16
F32 = jnp.float32
LANES = 128
ROWS16 = 16
MESH = pl.DeviceIdType.MESH


def dot(left, right):
    return jnp.dot(left, right, preferred_element_type=F32)


def contract_last(left, right):
    return lax.dot_general(left, right, (((1,), (1,)), ((), ())), preferred_element_type=F32)


def contract_rows(left, right):
    return lax.dot_general(left, right, (((0,), (0,)), ((), ())), preferred_element_type=F32)


def swap(values, mask):
    return lax.ppermute(values, "seq", [(i, i ^ mask) for i in range(lax.axis_size("seq"))])


def inverse_rms(values):
    return lax.rsqrt(jnp.mean(values * values, axis=-1, keepdims=True) + 1e-06)


def rms_norm(values, gain):
    return values * inverse_rms(values) * gain


def sigmoid(values):
    return 0.5 * jnp.tanh(0.5 * values) + 0.5


def gelu_parts(values):
    c = 0.7978845608028654
    sq = values * values
    t = jnp.tanh(c * values * (1.0 + 0.044715 * sq))
    half = 0.5 * (1.0 + t)
    return values * half, half + 0.5 * values * (1.0 - t * t) * (c * (1.0 + 3.0 * 0.044715 * sq))


def drop_of(rate_log):
    u = 2.0 * rate_log
    series = 1.0 + u * (1.0 / 8.0)
    for n in (7, 6, 5, 4, 3, 2):
        series = 1.0 + u * series * (1.0 / n)
    return jnp.where(u > -0.4, -u * series, 1.0 - jnp.exp(u))


def scan_rows(rate, drive, reverse):
    rows, lanes = rate.shape
    count = rows // 8
    rate = rate.reshape(count, 8, lanes)
    drive = drive.reshape(count, 8, lanes)
    row = lax.broadcasted_iota(jnp.int32, (count, 8, lanes), 1)
    for step in (1, 2, 4):
        shift = 8 - step if reverse else step
        keep = row < 8 - step if reverse else row >= step
        drive = drive + rate * jnp.where(keep, pltpu.roll(drive, shift, 1), 0.0)
        rate = rate * jnp.where(keep, pltpu.roll(rate, shift, 1), 1.0)
    state, reach = jnp.zeros((1, lanes), F32), jnp.ones((1, lanes), F32)
    states, reaches = [None] * count, [None] * count
    last = 0 if reverse else 7
    for i in reversed(range(count)) if reverse else range(count):
        states[i] = drive[i] + rate[i] * state
        reaches[i] = rate[i] * reach
        state = states[i][last : last + 1]
        reach = reaches[i][last : last + 1]
    return jnp.concatenate(states, axis=0), jnp.concatenate(reaches, axis=0)


def forward_kernel(
    off_ref, x_ref, edge_ref, gates_ref, chan_ref,
    forget_out, admit_out, conv_out_ref, rate_out, local_out, reach_out, ends_out,
    logits,
):
    q = pl.program_id(0)
    tokens = x_ref.shape[0]
    share = chan_ref.shape[1]
    blocks = x_ref.shape[1] // BW
    off = pl.multiple_of(off_ref[0], LANES)
    for b in range(blocks):
        cols = slice(b * BW, (b + 1) * BW)
        mixed = jnp.dot(x_ref[:, cols], gates_ref[cols, :], preferred_element_type=F32)
        logits[0, :, cols] = mixed[:, :BW]
        logits[1, :, cols] = mixed[:, BW:]
    for j in range(share // LANES):
        lanes = slice(j * LANES, (j + 1) * LANES)
        here = pl.ds(pl.multiple_of(off + j * LANES, LANES), LANES)
        chan = [chan_ref[i : i + 1, lanes] for i in range(8)]
        forget = (logits[0, :, here] + chan[0]).astype(BF)
        admit = (logits[1, :, here] + chan[1]).astype(BF)
        forget_out[:, lanes] = forget
        admit_out[:, lanes] = admit
        edge = edge_ref[pl.ds(pl.multiple_of(q * HALO, HALO), HALO), here]
        padded = jnp.concatenate([edge, x_ref[:, here].astype(F32)], axis=0)
        conv = chan[3] + chan[4] * padded[HALO:]
        for k in range(1, CONV):
            conv = conv + chan[4 + k] * pltpu.roll(padded, k, 0)[HALO:]
        conv_out_ref[:, lanes] = conv
        rate_log = -8.0 * chan[2] * (0.1 + 0.9 * sigmoid(forget.astype(F32)))
        rate = jnp.exp(rate_log)
        drive = jnp.sqrt(drop_of(rate_log)) * sigmoid(admit.astype(F32)) * conv
        state, reach = scan_rows(rate, drive, False)
        rate_out[:, lanes] = rate
        local_out[:, lanes] = state
        reach_out[:, lanes] = reach
        ends_out[0, 0, :, lanes] = reach[tokens - 1 :]
        ends_out[0, 1, :, lanes] = state[tokens - 1 :]


def whole(shape):
    return pl.BlockSpec(shape, lambda q: (0,) * len(shape))


def per_seq(width):
    return pl.BlockSpec((1, 1, width), lambda q: (q, 0, 0))


def temporal_forward(off, x_win, edge, gates, chan, tokens):
    total, window = x_win.shape
    share = chan.shape[1]
    seqs = total // tokens
    part = lambda width: pl.BlockSpec((tokens, width), lambda q: (q, 0))
    return pl.pallas_call(
        forward_kernel,
        grid=(seqs,),
        in_specs=[
            pl.BlockSpec(memory_space=pltpu.SMEM),
            part(window),
            whole(edge.shape),
            whole(gates.shape),
            whole(chan.shape),
        ],
        out_specs=[
            part(share), part(share), part(share), part(share), part(share), part(share),
            pl.BlockSpec((1, 2, 1, share), lambda q: (q, 0, 0, 0)),
        ],
        out_shape=[
            jax.ShapeDtypeStruct((total, share), BF),
            jax.ShapeDtypeStruct((total, share), BF),
            jax.ShapeDtypeStruct((total, share), F32),
            jax.ShapeDtypeStruct((total, share), F32),
            jax.ShapeDtypeStruct((total, share), F32),
            jax.ShapeDtypeStruct((total, share), F32),
            jax.ShapeDtypeStruct((seqs, 2, 1, share), F32),
        ],
        scratch_shapes=[
            pltpu.VMEM((2, tokens, window), F32),
        ],
        compiler_params=pltpu.CompilerParams(vmem_limit_bytes=60 * 1024 * 1024),
        cost_estimate=pl.CostEstimate(flops=1000, bytes_accessed=1000, transcendentals=0),
        name="temporal_forward",
    )(off, x_win, edge, gates, chan)


def partner(mask):
    s = lax.axis_index("seq")
    if mask == 1:
        other = s + 1 - 2 * (s % 2)
    else:
        other = (s + 2) % 4
    return {"seq": other}


def greet():
    barrier = pltpu.get_barrier_semaphore()
    for mask in (1, 2):
        pl.semaphore_signal(barrier, inc=1, device_id=partner(mask), device_id_type=MESH)
    pl.semaphore_wait(barrier, 2)


def sender(sends, recvs):
    def send(slot, source, target, mask):
        copy = pltpu.make_async_remote_copy(
            src_ref=source,
            dst_ref=target,
            send_sem=sends.at[slot],
            recv_sem=recvs.at[slot],
            device_id=partner(mask),
            device_id_type=MESH,
        )
        copy.start()
        return copy

    return send


def over_chunks(rows, run):
    def step(i, carry):
        run(pl.ds(pl.multiple_of(i * ROWS16, ROWS16), ROWS16))
        return carry

    lax.fori_loop(0, rows // ROWS16, step, 0)


def reduce_phase(product, send, first_slot, acc, sent, got):
    rows = acc.shape[1]
    half = rows // 2
    low, high = pl.ds(0, half), pl.ds(half, half)
    product(3, lambda cols, value: sent.__setitem__((0, slice(None), cols), value.astype(BF)))
    far_near = send(first_slot, sent.at[0, low], got.at[0, low], 1)
    far_side = send(first_slot + 1, sent.at[0, high], got.at[0, high], 2)
    product(1, lambda cols, value: acc.__setitem__((1, slice(None), cols), value))
    over_chunks(half, lambda r: sent.__setitem__((1, r), acc[1, r].astype(BF)))
    near_low = send(first_slot + 2, sent.at[1, low], got.at[1, low], 1)
    product(2, lambda cols, value: acc.__setitem__((2, slice(None), cols), value))

    def tail(k):
        def run(r):
            r = pl.ds(pl.multiple_of(r.start + half, ROWS16), ROWS16)
            sent[k, r] = acc[k, r].astype(BF)

        return run

    over_chunks(half, tail(2))
    side_high = send(first_slot + 3, sent.at[2, high], got.at[2, high], 2)
    far_side.wait_recv()

    def add_high(r):
        r = pl.ds(pl.multiple_of(r.start + half, ROWS16), ROWS16)
        sent[1, r] = (acc[1, r] + got[0, r].astype(F32)).astype(BF)

    over_chunks(half, add_high)
    near_high = send(first_slot + 4, sent.at[1, high], got.at[1, high], 1)
    far_near.wait_recv()

    def add_low(r):
        sent[2, r] = (acc[2, r] + got[0, r].astype(F32)).astype(BF)

    over_chunks(half, add_low)
    side_low = send(first_slot + 5, sent.at[2, low], got.at[2, low], 2)
    product(0, lambda cols, value: acc.__setitem__((0, slice(None), cols), value))
    arriving = [near_low, side_high, near_high, side_low]
    for copy in arriving:
        copy.wait_recv()
    return [far_near, far_side] + arriving


def both_ways(send, slot, source, out):
    half = source.shape[0] // 2
    low, high = pl.ds(0, half), pl.ds(half, half)
    return [
        send(slot, source.at[low], out.at[1, low], 1),
        send(slot + 1, source.at[high], out.at[2, high], 2),
        send(slot + 2, source.at[high], out.at[1, high], 1),
        send(slot + 3, source.at[low], out.at[2, low], 2),
    ]


def pass_on(send, slot, out, copies):
    half = out.shape[1] // 2
    low, high = pl.ds(0, half), pl.ds(half, half)
    copies[0].wait_recv()
    far_low = send(slot + 4, out.at[1, low], out.at[3, low], 2)
    copies[1].wait_recv()
    far_high = send(slot + 5, out.at[2, high], out.at[3, high], 1)
    return copies + [far_low, far_high]


def settle(copies):
    for copy in copies[2:]:
        copy.wait_recv()
    for copy in copies:
        copy.wait_send()


def at_seq(k):
    s = lax.axis_index("seq")
    return s if k == 0 else 3 - s if k == 3 else partner(k)["seq"]


def product_of(left, right, contract, rows, tile, ready=None):
    def product(k, store):
        def step(c, carry):
            cols = pl.ds(pl.multiple_of(c * tile, tile), tile)
            if ready is not None and k == 3:
                ready(c)
            total = None
            for a, b in zip(left, right):
                part = b[cols, :] if contract else b[:, cols]
                value = lax.dot_general(
                    a[k * rows : (k + 1) * rows, :],
                    part,
                    (((1,), (1 if contract else 0,)), ((), ())),
                    preferred_element_type=F32,
                )
                total = value if total is None else total + value
            store(cols, total)
            return carry

        width = right[0].shape[0 if contract else 1]
        lax.fori_loop(0, width // tile, step, 0)

    return product


def rms_parts(values):
    return lax.rsqrt(jnp.mean(values * values, axis=-1, keepdims=True) + 1e-06)


def stream_kernel(
    mixed_ref, weight_ref, flat_ref, gain_ref,
    stream_out, temporal_out, normed_out,
    acc, sent, got, sends, recvs,
):
    rows = flat_ref.shape[0]
    greet()
    send = sender(sends, recvs)
    copies = reduce_phase(
        product_of([mixed_ref], [weight_ref], False, rows, 512), send, 0, acc, sent, got
    )

    def finish(r):
        temporal = acc[0, r] + got[1, r].astype(F32) + got[2, r].astype(F32)
        temporal_out[r] = temporal
        stream = flat_ref[r].astype(F32) + temporal
        stream_out[r] = stream
        normed_out[0, r] = (stream * rms_parts(stream) * gain_ref[...]).astype(BF)

    over_chunks(rows, finish)
    gathered = pass_on(send, 6, normed_out, both_ways(send, 6, normed_out.at[0], normed_out))
    settle(gathered)
    for copy in copies:
        copy.wait_send()


def exchange_scratch(rows, width, copies):
    return [
        pltpu.VMEM((3, rows, width), F32),
        pltpu.VMEM((3, rows, width), BF),
        pltpu.VMEM((3, rows, width), BF),
        pltpu.SemaphoreType.DMA((copies,)),
        pltpu.SemaphoreType.DMA((copies,)),
    ]


def remote_call(kernel, name, ident, outs, operands, scratch, far=0):
    return pl.pallas_call(
        kernel,
        in_specs=[pl.BlockSpec(memory_space=pltpu.VMEM)] * (len(operands) - far)
        + [pl.BlockSpec(memory_space=pl.ANY)] * far,
        out_specs=[pl.BlockSpec(memory_space=pltpu.VMEM)] * len(outs),
        out_shape=[jax.ShapeDtypeStruct(shape, kind) for shape, kind in outs],
        scratch_shapes=scratch,
        compiler_params=pltpu.CompilerParams(
            collective_id=ident, has_side_effects=True, vmem_limit_bytes=60 * 1024 * 1024
        ),
        cost_estimate=pl.CostEstimate(flops=1000, bytes_accessed=1000, transcendentals=0),
        name=name,
    )(*operands)


def stream_and_norm(mixed, weight, flat, gain):
    rows, width = flat.shape
    groups = mixed.shape[0] // rows
    return remote_call(
        stream_kernel,
        "stream_and_norm",
        1,
        [((rows, width), F32), ((rows, width), F32), ((groups, rows, width), BF)],
        (mixed, weight, flat, gain),
        exchange_scratch(rows, width, 12),
    )


def rows_kernel(upstream_ref, down_ref, gate_ref, up_ref, rows_out):
    tile = gate_ref.shape[1]
    hidden = rows_out.shape[1] // 2
    grad = lax.dot_general(
        upstream_ref[...], down_ref[...], (((1,), (1,)), ((), ())), preferred_element_type=F32
    )
    value, slope = gelu_parts(gate_ref[...])
    at = pl.multiple_of(pl.program_id(0) * tile, tile)
    rows_out[:, pl.ds(at, tile)] = (grad * up_ref[...] * slope).astype(BF)
    rows_out[:, pl.ds(hidden + at, tile)] = (grad * value).astype(BF)


def mlp_rows(upstream, down, gate_up):
    total, width = upstream.shape
    hidden = down.shape[0]
    tile = BW
    half = hidden // tile
    return pl.pallas_call(
        rows_kernel,
        grid=(half,),
        in_specs=[
            whole(upstream.shape),
            pl.BlockSpec((tile, width), lambda j: (j, 0)),
            pl.BlockSpec((total, tile), lambda j: (0, j)),
            pl.BlockSpec((total, tile), lambda j: (0, half + j)),
        ],
        out_specs=whole((total, 2 * hidden)),
        out_shape=jax.ShapeDtypeStruct((total, 2 * hidden), BF),
        compiler_params=pltpu.CompilerParams(vmem_limit_bytes=60 * 1024 * 1024),
        cost_estimate=pl.CostEstimate(flops=1000, bytes_accessed=1000, transcendentals=0),
        name="mlp_rows",
    )(upstream, down, gate_up, gate_up)


def stream_back_kernel(
    rows_ref, stream_ref, gain_ref, upstream_ref, weight_far, hidden_far, down_far, out_far,
    grad_out, low_out, gain_out, feed_out, mixed_out,
    weight_ref, hidden_ref, down_ref, out_ref, fetches,
    acc, sent, got, sends, recvs,
):
    rows, width = stream_ref.shape
    tile = 512

    def fetch(c):
        part = pl.ds(pl.multiple_of(c * tile, tile), tile)
        return pltpu.make_async_copy(weight_far.at[part], weight_ref.at[part], fetches.at[c])

    count = width // tile
    for c in range(count):
        fetch(c).start()
    late = [
        pltpu.make_async_copy(hidden_far, hidden_ref, fetches.at[count]),
        pltpu.make_async_copy(down_far, down_ref, fetches.at[count + 1]),
        pltpu.make_async_copy(out_far, out_ref, fetches.at[count + 2]),
    ]
    for copy in late:
        copy.start()
    greet()
    send = sender(sends, recvs)
    product = product_of(
        [rows_ref], [weight_ref], True, rows, tile, ready=lambda c: fetch(c).wait()
    )
    copies = reduce_phase(product, send, 0, acc, sent, got)
    gain_out[...] = jnp.zeros_like(gain_out)

    def finish(r):
        grad = acc[0, r] + got[1, r].astype(F32) + got[2, r].astype(F32)
        stream = stream_ref[r]
        inv = rms_parts(stream)
        scaled = grad * gain_ref[...]
        inner = jnp.mean(stream * scaled, axis=-1, keepdims=True)
        total = upstream_ref[r].astype(F32) + inv * scaled - stream * (inv * inv * inv * inner)
        grad_out[r] = total
        low_out[0, r] = total.astype(BF)
        gained = grad * stream * inv
        gain_out[...] += gained[:8] + gained[8:]

    over_chunks(rows, finish)
    gathered = both_ways(send, 6, low_out.at[0], low_out)
    for copy in late:
        copy.wait()
    feed = product_of([hidden_ref], [down_ref], False, rows, tile)

    def feed_block(k):
        feed(k, lambda cols, value: feed_out.__setitem__((k, slice(None), cols), value.astype(BF)))

    def mixed_block(k):
        mixed_out[k] = lax.dot_general(
            low_out[k], out_ref[...], (((1,), (1,)), ((), ())), preferred_element_type=F32
        )

    feed_block(3)
    gathered = pass_on(send, 6, low_out, gathered)
    feed_block(0)
    mixed_block(0)
    feed_block(1)
    feed_block(2)
    near_low, side_high, near_high, side_low, far_low, far_high = gathered
    near_high.wait_recv()
    mixed_block(1)
    side_low.wait_recv()
    mixed_block(2)
    far_low.wait_recv()
    far_high.wait_recv()
    mixed_block(3)
    for copy in gathered:
        copy.wait_send()
    for copy in copies:
        copy.wait_send()


def stream_back(rows_all, weight, stream, gain, upstream, hidden, down, out_rows):
    rows, width = stream.shape
    groups = rows_all.shape[0] // rows
    return remote_call(
        stream_back_kernel,
        "stream_back",
        2,
        [
            ((rows, width), F32),
            ((groups, rows, width), BF),
            ((8, width), F32),
            ((groups, rows, width), BF),
            ((groups, rows, out_rows.shape[0]), F32),
        ],
        (rows_all, stream, gain, upstream, weight, hidden, down, out_rows),
        [
            pltpu.VMEM(weight.shape, BF),
            pltpu.VMEM(hidden.shape, BF),
            pltpu.VMEM(down.shape, BF),
            pltpu.VMEM(out_rows.shape, BF),
            pltpu.SemaphoreType.DMA((width // 512 + 3,)),
        ]
        + exchange_scratch(rows, width, 12),
        far=4,
    )


def inputs_back_kernel(
    branch_ref, y_ref, flat_ref, gain_ref, weight_far, mixed_far, low_far,
    grad_out, gain_out, columns_out,
    weight_ref, mixed_ref, low_ref, fetches, columns_ref, acc, sent, got, sends, recvs,
):
    rows = flat_ref.shape[0]
    tile = 512
    parts = weight_ref.shape[0] // tile

    def fetch(c):
        part = pl.ds(pl.multiple_of(c * tile, tile), tile)
        return pltpu.make_async_copy(weight_far.at[part], weight_ref.at[part], fetches.at[c])

    for c in range(parts):
        fetch(c).start()
    late = [
        pltpu.make_async_copy(mixed_far, mixed_ref, fetches.at[parts]),
        pltpu.make_async_copy(low_far, low_ref, fetches.at[parts + 1]),
    ]
    for copy in late:
        copy.start()
    s = lax.axis_index("seq")
    count, columns = columns_ref.shape[0], columns_out.shape[1]
    barrier = pltpu.get_barrier_semaphore()
    for k in (1, 2, 3):
        pl.semaphore_signal(barrier, inc=1, device_id={"seq": at_seq(k)}, device_id_type=MESH)
    pl.semaphore_wait(barrier, 3)
    send = sender(sends, recvs)
    here = pl.ds(pl.multiple_of(s * count, ROWS16), count)

    def columns_of(k):
        return columns_ref.at[:, pl.ds(pl.multiple_of(at_seq(k) * columns, LANES), columns)]

    moved = []
    for k in (3, 1, 2):
        copy = pltpu.make_async_remote_copy(
            src_ref=columns_of(k),
            dst_ref=columns_out.at[here],
            send_sem=sends.at[5 + k],
            recv_sem=recvs.at[5 + k],
            device_id={"seq": at_seq(k)},
            device_id_type=MESH,
        )
        moved.append(copy)
    window = branch_ref.shape[1]
    weights = [weight_ref.at[:, :window], weight_ref.at[:, window:]]
    product = product_of(
        [branch_ref, y_ref], weights, True, rows, tile, ready=lambda c: fetch(c).wait()
    )

    def product_and_move(k, store):
        if k == 0:
            for copy in late:
                copy.wait()
            left = mixed_ref[...].T
            for c in range(columns_ref.shape[1] // tile):
                cols = slice(c * tile, (c + 1) * tile)
                columns_ref[:, cols] = jnp.dot(
                    left, low_ref[:, cols], preferred_element_type=F32
                ).astype(BF)
            for copy in moved:
                copy.start()
        product(k, store)

    copies = reduce_phase(product_and_move, send, 0, acc, sent, got)
    columns_out[here] = columns_of(0)[...]
    gain_out[...] = jnp.zeros_like(gain_out)

    def finish(r):
        grad = acc[0, r] + got[1, r].astype(F32) + got[2, r].astype(F32)
        values = flat_ref[r].astype(F32)
        inv = rms_parts(values)
        scaled = grad * gain_ref[...]
        inner = jnp.mean(values * scaled, axis=-1, keepdims=True)
        grad_out[r] = inv * scaled - values * (inv * inv * inv * inner)
        gained = grad * values * inv
        gain_out[...] += gained[:8] + gained[8:]

    over_chunks(rows, finish)
    for copy in moved:
        copy.wait_recv()
    for copy in copies + moved:
        copy.wait_send()


def inputs_back(branch_rows, y_rows, weight, flat, gain, mixed, low):
    rows, width = flat.shape
    count, columns = mixed.shape[1], low.shape[1]
    return remote_call(
        inputs_back_kernel,
        "inputs_back",
        3,
        [((rows, width), F32), ((8, width), F32), ((4 * count, columns // 4), BF)],
        (branch_rows, y_rows, flat, gain, weight, mixed, low),
        [
            pltpu.VMEM(weight.shape, BF),
            pltpu.VMEM(mixed.shape, BF),
            pltpu.VMEM(low.shape, BF),
            pltpu.SemaphoreType.DMA((width // 512 + 2,)),
            pltpu.VMEM((count, columns), BF),
        ]
        + exchange_scratch(rows, width, 9),
        far=3,
    )


def start_kernel(inputs_ref, inputs_out, edge_out, sends, recvs):
    seqs = edge_out.shape[1] // ROWS16
    tokens = inputs_ref.shape[0] // seqs
    w = lax.axis_index("wide")
    wide = lax.axis_size("wide")
    after, before = lax.rem(w + 1, wide), lax.rem(w + wide - 1, wide)
    barrier = pltpu.get_barrier_semaphore()
    for mask in (1, 2):
        pl.semaphore_signal(barrier, inc=1, device_id=partner(mask), device_id_type=MESH)
    pl.semaphore_signal(barrier, inc=1, device_id={"wide": before}, device_id_type=MESH)
    pl.semaphore_wait(barrier, 3)
    send = sender(sends, recvs)
    edges = []
    for q in range(seqs):
        copy = pltpu.make_async_remote_copy(
            src_ref=inputs_ref.at[pl.ds((q + 1) * tokens - ROWS16, ROWS16)],
            dst_ref=edge_out.at[0, pl.ds(q * ROWS16, ROWS16)],
            send_sem=sends.at[12 + q],
            recv_sem=recvs.at[12 + q],
            device_id={"wide": after},
            device_id_type=MESH,
        )
        copy.start()
        edges.append(copy)
    blocks = both_ways(send, 0, inputs_ref, inputs_out)
    inputs_out[0] = inputs_ref[...]
    for copy in edges:
        copy.wait_recv()
        copy.wait_send()
    edges = both_ways(send, 6, edge_out.at[0], edge_out)
    blocks = pass_on(send, 0, inputs_out, blocks)
    edges = pass_on(send, 6, edge_out, edges)
    settle(blocks)
    settle(edges)


def start(inputs, groups, seqs):
    rows, width = inputs.shape
    copies = 12 + seqs
    return remote_call(
        start_kernel,
        "start",
        6,
        [((groups, rows, width), BF), ((groups, seqs * ROWS16, width), BF)],
        (inputs,),
        [pltpu.SemaphoreType.DMA((copies,)), pltpu.SemaphoreType.DMA((copies,))],
    )


def middle_kernel(
    grad_ref, y_ref, local_ref, reach_ref, carry_ref, rate_ref, chan_ref, ends_ref,
    edge_ref, gates_ref, valid_ref, feed_ref,
    conv_far, forget_far, admit_far, x_far, stream_far, temporal_far,
    y_rows_out, branch_out, forget_out, admit_out, sums_out, result_out, squares_out,
    adjoint, later, heads, packet, packet_in, tails, after, conv_rows,
    conv_ref, forget_ref, admit_ref, x_ref, stream_ref, temporal_ref,
    sent, got, fetches, sends, recvs, head_sends, head_recvs,
):
    wide, seqs, share = ends_ref.shape
    tokens = grad_ref.shape[0] // seqs
    window = x_ref.shape[1]
    rows, width = stream_ref.shape
    half = rows // 2
    low, high = pl.ds(0, half), pl.ds(half, half)
    w = lax.axis_index("wide")
    first_channel = lax.axis_index("seq") * share
    base = jnp.minimum(first_channel // BW * BW, lax.axis_size("seq") * share - window)
    off = pl.multiple_of(first_channel - base, LANES)
    fetched = []
    for i, (far, near) in enumerate(
        (
            (conv_far, conv_ref),
            (forget_far, forget_ref),
            (admit_far, admit_ref),
            (x_far, x_ref),
            (stream_far, stream_ref),
            (temporal_far, temporal_ref),
        )
    ):
        copy = pltpu.make_async_copy(far, near, fetches.at[i])
        copy.start()
        fetched.append(copy)

    barrier = pltpu.get_barrier_semaphore()
    for mask in (1, 2):
        pl.semaphore_signal(barrier, inc=1, device_id=partner(mask), device_id_type=MESH)

    def tell(i, carry):
        other = lax.rem(w + i, wide)
        pl.semaphore_signal(barrier, inc=1, device_id={"wide": other}, device_id_type=MESH)
        return carry

    lax.fori_loop(1, wide, tell, 0)
    pl.semaphore_wait(barrier, wide + 1)
    send = sender(sends, recvs)
    far_near = send(0, feed_ref.at[3, low], got.at[0, low], 1)
    far_side = send(1, feed_ref.at[3, high], got.at[0, high], 2)
    near_low = send(2, feed_ref.at[1, low], got.at[1, low], 1)
    side_high = send(3, feed_ref.at[2, high], got.at[2, high], 2)

    row = lax.broadcasted_iota(jnp.int32, (tokens, LANES), 0)
    fetched[1].wait()
    fetched[2].wait()

    def scan_step(q, carry):
        r = pl.ds(pl.multiple_of(q * tokens, tokens), tokens)
        head_rows = pl.ds(pl.multiple_of(q * tokens, tokens), ROWS16)
        for j in range(share // LANES):
            lanes = slice(j * LANES, (j + 1) * LANES)
            grad = grad_ref[r, lanes]
            value, slope = gelu_parts(y_ref[r, lanes])
            state = (local_ref[r, lanes] + reach_ref[r, lanes] * carry_ref[q, :, lanes]).astype(BF)
            y_rows_out[r, lanes] = (grad * state.astype(F32) * slope).astype(BF)
            state_grad = (grad * value).astype(BF).astype(F32)
            rate = rate_ref[r, lanes]
            ahead = jnp.where(row == tokens - 1, 1.0, pltpu.roll(rate, tokens - 1, 0))
            adjoints, laters = scan_rows(ahead, state_grad, True)
            adjoint[r, lanes] = adjoints
            later[r, lanes] = laters
            tails[q, :, lanes] = rate[:1] * adjoints[:1]
            forget_sig = sigmoid(forget_ref[head_rows, lanes].astype(F32)[:HALO])
            admit_sig = sigmoid(admit_ref[head_rows, lanes].astype(F32)[:HALO])
            rate_log = -8.0 * chan_ref[2:3, lanes] * (0.1 + 0.9 * forget_sig)
            gain = jnp.sqrt(drop_of(rate_log)) * admit_sig
            for i, values in enumerate((adjoints[:HALO] * gain, laters[:HALO] * gain)):
                for t in range(CONV - 1):
                    packet[i, t, q, :, lanes] = values[t : t + 1]
        return carry

    lax.fori_loop(0, seqs, scan_step, 0)
    for q in range(seqs):
        heads[0, q : q + 1, :] = tails[q]

    def head_copy(i):
        return pltpu.make_async_remote_copy(
            src_ref=heads.at[0],
            dst_ref=heads.at[i],
            send_sem=head_sends.at[i],
            recv_sem=head_recvs.at[i],
            device_id={"wide": lax.rem(w + i, wide)},
            device_id_type=MESH,
        )

    def head_start(i, carry):
        head_copy(i).start()
        return carry

    def head_wait(i, carry):
        copy = head_copy(i)
        copy.wait_recv()
        copy.wait_send()
        return carry

    lax.fori_loop(1, wide, head_start, 0)
    packets = pltpu.make_async_remote_copy(
        src_ref=packet,
        dst_ref=packet_in,
        send_sem=sends.at[6],
        recv_sem=recvs.at[6],
        device_id={"wide": lax.rem(w + wide - 1, wide)},
        device_id_type=MESH,
    )
    packets.start()

    far_side.wait_recv()
    sent[0] = (feed_ref[1, high].astype(F32) + got[0, high].astype(F32)).astype(BF)
    near_high = send(4, sent.at[0], got.at[1, high], 1)
    far_near.wait_recv()
    sent[1] = (feed_ref[2, low].astype(F32) + got[0, low].astype(F32)).astype(BF)
    side_low = send(5, sent.at[1], got.at[2, low], 2)

    lax.fori_loop(1, wide, head_wait, 0)
    packets.wait_recv()
    packets.wait_send()

    def tail_step(i, carry):
        tail, next_tail = carry
        j = wide - i
        stepped = ends_ref[j] * tail + heads[lax.rem(w + i, wide)]
        return jnp.where(j > w, stepped, tail), jnp.where(j > w + 1, stepped, next_tail)

    zero = jnp.zeros((seqs, share), F32)
    tail, next_tail = lax.fori_loop(1, wide, tail_step, (zero, zero))
    next_tail = jnp.where(w == wide - 1, 0.0, next_tail)
    inside = jnp.where(w == wide - 1, 0.0, 1.0)
    after[...] = jnp.zeros_like(after)
    for q in range(seqs):
        tails[q] = tail[q : q + 1]
        for t in range(CONV - 1):
            after[q * HALO + t : q * HALO + t + 1, :] = (
                inside * packet_in[0, t, q] + packet_in[1, t, q] * next_tail[q : q + 1]
            )

    forget_out[...] = jnp.zeros_like(forget_out)
    admit_out[...] = jnp.zeros_like(admit_out)
    conv_rows[...] = jnp.zeros_like(conv_rows)
    sums_out[...] = jnp.zeros_like(sums_out)
    fetched[0].wait()
    fetched[3].wait()

    def rows_step(q, carry):
        r = pl.ds(pl.multiple_of(q * tokens, tokens), tokens)
        pack = pl.ds(pl.multiple_of(q * HALO, HALO), HALO)
        for j in range(share // LANES):
            lanes = slice(j * LANES, (j + 1) * LANES)
            here = pl.ds(pl.multiple_of(off + j * LANES, LANES), LANES)
            chan = [chan_ref[i : i + 1, lanes] for i in range(8)]
            start = carry_ref[q, :, lanes]
            carried = local_ref[r, lanes] + reach_ref[r, lanes] * start
            before = jnp.where(row == 0, start, pltpu.roll(carried, 1, 0))
            full = adjoint[r, lanes] + later[r, lanes] * tails[q, :, lanes]
            forget_sig = sigmoid(forget_ref[r, lanes].astype(F32))
            admit_sig = sigmoid(admit_ref[r, lanes].astype(F32))
            span = 0.1 + 0.9 * forget_sig
            rate = rate_ref[r, lanes]
            scale = jnp.sqrt(drop_of(-8.0 * chan[2] * span))
            gated = admit_sig * conv_ref[r, lanes]
            log_grad = full * (rate * before - rate * rate / scale * gated)
            conv_grad = full * scale * admit_sig
            forget_rows = (
                log_grad * (-7.2) * chan[2] * forget_sig * (1.0 - forget_sig)
            ).astype(BF)
            admit_rows = (full * scale * gated * (1.0 - admit_sig)).astype(BF)
            forget_out[r, here] = forget_rows
            admit_out[r, here] = admit_rows
            ahead = jnp.concatenate([conv_grad, after[pack, lanes]], axis=0)
            back = chan[4] * conv_grad
            for k in range(1, CONV):
                back = back + chan[4 + k] * pltpu.roll(ahead, tokens + HALO - k, 0)[:tokens]
            conv_rows[:, here] = back.astype(BF).astype(F32)
            padded = jnp.concatenate(
                [edge_ref[pack, here], x_ref[r, here].astype(F32)], axis=0
            )
            sums = [
                forget_rows.astype(F32),
                admit_rows.astype(F32),
                log_grad * (-8.0) * span,
                conv_grad,
                conv_grad * padded[HALO:],
            ] + [conv_grad * pltpu.roll(padded, k, 0)[HALO:] for k in range(1, CONV)]
            sums_out[:, lanes] += jnp.concatenate(
                [jnp.sum(v, axis=0, keepdims=True) for v in sums], axis=0
            )
        for b in range(window // BW):
            cols = slice(b * BW, (b + 1) * BW)
            back = conv_rows[:, cols]
            for source, at in ((forget_out, 0), (admit_out, BW)):
                back = back + lax.dot_general(
                    source[r, cols],
                    gates_ref[cols, at : at + BW],
                    (((1,), (1,)), ((), ())),
                    preferred_element_type=F32,
                )
            branch_out[r, cols] = back.astype(BF)
        return carry

    lax.fori_loop(0, seqs, rows_step, 0)
    fetched[4].wait()
    fetched[5].wait()
    for copy in (near_low, side_high, near_high, side_low):
        copy.wait_recv()
    squares_out[...] = jnp.zeros_like(squares_out)

    def finish(r):
        feed = feed_ref[0, r].astype(F32) + got[1, r].astype(F32) + got[2, r].astype(F32)
        result = stream_ref[r] + feed
        result_out[r] = result
        valid = valid_ref[r]
        for i, values in enumerate((result, temporal_ref[r], feed)):
            square = valid * values * values
            squares_out[i] += square[:8] + square[8:]

    over_chunks(rows, finish)
    for copy in (far_near, far_side, near_low, side_high, near_high, side_low):
        copy.wait_send()


def middle(
    grad, y, local, reach, carry, rate, chan, ends, edge, gates, valid, feed,
    conv, forget, admit, x_win, stream, temporal,
):
    total, share = grad.shape
    window = x_win.shape[1]
    rows, width = stream.shape
    wide, seqs = ends.shape[:2]
    tokens = total // seqs
    vmem = pl.BlockSpec(memory_space=pltpu.VMEM)
    anywhere = pl.BlockSpec(memory_space=pl.ANY)
    outs = [
        ((total, share), BF),
        ((total, window), BF),
        ((total, window), BF),
        ((total, window), BF),
        ((8, share), F32),
        ((rows, width), F32),
        ((3, 8, width), F32),
    ]
    return pl.pallas_call(
        middle_kernel,
        in_specs=[vmem] * 12 + [anywhere] * 6,
        out_specs=[vmem] * len(outs),
        out_shape=[jax.ShapeDtypeStruct(shape, kind) for shape, kind in outs],
        scratch_shapes=[
            pltpu.VMEM((total, share), F32),
            pltpu.VMEM((total, share), F32),
            pltpu.VMEM((wide, seqs, share), F32),
            pltpu.VMEM((2, CONV - 1, seqs, 1, share), F32),
            pltpu.VMEM((2, CONV - 1, seqs, 1, share), F32),
            pltpu.VMEM((seqs, 1, share), F32),
            pltpu.VMEM((seqs * HALO, share), F32),
            pltpu.VMEM((tokens, window), F32),
            pltpu.VMEM((total, share), F32),
            pltpu.VMEM((total, share), BF),
            pltpu.VMEM((total, share), BF),
            pltpu.VMEM((total, window), BF),
            pltpu.VMEM((rows, width), F32),
            pltpu.VMEM((rows, width), F32),
            pltpu.VMEM((2, rows // 2, width), BF),
            pltpu.VMEM((3, rows, width), BF),
            pltpu.SemaphoreType.DMA((6,)),
            pltpu.SemaphoreType.DMA((7,)),
            pltpu.SemaphoreType.DMA((7,)),
            pltpu.SemaphoreType.DMA((wide,)),
            pltpu.SemaphoreType.DMA((wide,)),
        ],
        compiler_params=pltpu.CompilerParams(
            collective_id=7, has_side_effects=True, vmem_limit_bytes=60 * 1024 * 1024
        ),
        cost_estimate=pl.CostEstimate(flops=1000, bytes_accessed=1000, transcendentals=0),
        name="middle",
    )(
        grad, y, local, reach, carry[:, None, :], rate, chan, ends, edge, gates, valid, feed,
        conv, forget, admit, x_win, stream, temporal,
    )


def grads_kernel(
    bases, normed_ref, y_ref, branch_ref, x_ref, forget_ref, admit_ref,
    stacked_out,
    gates, blocks, gate_total, sends, recvs,
):
    step = pl.program_id(0)
    wide, stacked_rows, quarter = stacked_out.shape
    window = x_ref.shape[1]
    tiles = (window + y_ref.shape[1]) // LANES
    group = wide // pl.num_programs(0)
    part = normed_ref.shape[1] // group
    room = stacked_rows - tiles * part
    share = gate_total.shape[0] // wide

    def quarter_of(k):
        return pl.ds(pl.multiple_of(at_seq(k) * quarter, LANES), quarter)

    def exchange(k):
        return pltpu.make_async_remote_copy(
            src_ref=gates.at[:, quarter_of(k)],
            dst_ref=blocks.at[k],
            send_sem=sends.at[k],
            recv_sem=recvs.at[k],
            device_id={"seq": at_seq(k)},
            device_id_type=MESH,
        )

    @pl.when(step == 0)
    def _():
        barrier = pltpu.get_barrier_semaphore()
        for k in (1, 2, 3):
            pl.semaphore_signal(barrier, inc=1, device_id={"seq": at_seq(k)}, device_id_type=MESH)
        for b in range(window // BW):
            cols = slice(b * BW, (b + 1) * BW)
            block = x_ref[:, cols].T
            for source, at in ((forget_ref, 0), (admit_ref, BW)):
                gates[cols, at : at + BW] = jnp.dot(
                    block, source[:, cols], preferred_element_type=F32
                ).astype(BF)
        pl.semaphore_wait(barrier, 3)
        for k in (3, 1, 2):
            exchange(k).start()

    left = normed_ref[...].T
    first = 0
    for right in (branch_ref, y_ref):
        sums = jnp.dot(left, right[...], preferred_element_type=F32).astype(BF)
        count = right.shape[1] // LANES
        for g in range(group):
            for i in range(count):
                at = (first + i) * part
                stacked_out[step * group + g, at : at + part, :] = sums[
                    g * part : (g + 1) * part, i * LANES : (i + 1) * LANES
                ]
        first += count

    @pl.when(step == pl.num_programs(0) - 1)
    def _():
        gate_total[...] = jnp.zeros_like(gate_total)
        for k in range(4):
            if k:
                exchange(k).wait_recv()
            other = at_seq(k)
            base = other * 0
            for j, start_row in enumerate(bases):
                base = jnp.where(other == j, start_row, base)
            at = pl.ds(pl.multiple_of(base, 8), window)
            value = blocks[k] if k else gates[:, quarter_of(0)]
            gate_total[at, :] += value.astype(F32)
        for g in range(wide):
            value = gate_total[g * share : (g + 1) * share, :]
            if room > share:
                value = jnp.concatenate([value, jnp.zeros((room - share, quarter), F32)], axis=0)
            stacked_out[g, tiles * part :, :] = value.astype(BF)
        for k in (1, 2, 3):
            exchange(k).wait_send()


def temporal_grads(normed, y_rows, branch_rows, x_win, forget_win, admit_win, wide, bases, stacked_rows):
    total, width = normed.shape
    share, window = y_rows.shape[1], x_win.shape[1]
    quarter = 2 * BW // 4
    return pl.pallas_call(
        functools.partial(grads_kernel, bases),
        grid=(width // BW,),
        in_specs=[pl.BlockSpec((total, BW), lambda i: (0, i))]
        + [whole(v.shape) for v in (y_rows, branch_rows, x_win, forget_win, admit_win)],
        out_specs=whole((wide, stacked_rows, quarter)),
        out_shape=jax.ShapeDtypeStruct((wide, stacked_rows, quarter), BF),
        scratch_shapes=[
            pltpu.VMEM((window, 2 * BW), BF),
            pltpu.VMEM((4, window, quarter), BF),
            pltpu.VMEM((4 * share, quarter), F32),
            pltpu.SemaphoreType.DMA((4,)),
            pltpu.SemaphoreType.DMA((4,)),
        ],
        compiler_params=pltpu.CompilerParams(
            collective_id=9, has_side_effects=True, vmem_limit_bytes=60 * 1024 * 1024
        ),
        cost_estimate=pl.CostEstimate(flops=1000, bytes_accessed=1000, transcendentals=0),
        name="temporal_grads",
    )(normed, y_rows, branch_rows, x_win, forget_win, admit_win)


def place(k, block, buffer, plan, outs):
    buffer[...] = block[...].astype(F32)
    other = at_seq(k)
    for (first, count, tiles, starts), out in zip(plan, outs):
        base = other * 0
        for j, start_col in enumerate(starts):
            base = jnp.where(other == j, start_col, base)
        for i in range(tiles):
            cols = pl.ds(pl.multiple_of(base + i * LANES, LANES), LANES)
            out[:, cols] += buffer[first + i * count : first + (i + 1) * count, :]


def spread_kernel(plan, parts_ref, early_ref, late_ref, *refs):
    outs, refs = refs[: len(plan)], refs[len(plan) :]
    sums_out, blocks, buffer, *refs = refs
    wholes, refs = refs[: len(plan)], refs[len(plan) :]
    total, sums_ref, got_sums, sends, recvs, sum_sends, sum_recvs = refs
    wide = sums_ref.shape[0]
    early = early_ref.shape[1]
    sums_ref[:, :early] = early_ref[...]
    sums_ref[:, early:] = late_ref[...]
    w = lax.axis_index("wide")
    barrier = pltpu.get_barrier_semaphore()
    for mask in (1, 2):
        pl.semaphore_signal(barrier, inc=1, device_id=partner(mask), device_id_type=MESH)

    def tell(i, carry):
        other = lax.rem(w + i, wide)
        pl.semaphore_signal(barrier, inc=1, device_id={"wide": other}, device_id_type=MESH)
        return carry

    lax.fori_loop(1, wide, tell, 0)
    pl.semaphore_wait(barrier, wide + 1)
    send = sender(sends, recvs)

    def chunk(i):
        other = lax.rem(w + i, wide)
        return pltpu.make_async_remote_copy(
            src_ref=sums_ref.at[other],
            dst_ref=got_sums.at[i],
            send_sem=sum_sends.at[i],
            recv_sem=sum_recvs.at[i],
            device_id={"wide": other},
            device_id_type=MESH,
        )

    def begin(i, carry):
        chunk(i).start()
        return carry

    def finish(i, carry):
        copy = chunk(i)
        copy.wait_recv()
        copy.wait_send()
        return carry + got_sums[i]

    lax.fori_loop(1, wide, begin, 0)
    copies = both_ways(send, 0, parts_ref, blocks)
    for out in wholes:
        out[...] = jnp.zeros_like(out)
    place(0, parts_ref, buffer, plan, wholes)
    total[0] = lax.fori_loop(1, wide, finish, sums_ref[w])
    to_near = send(6, total.at[0], total.at[1], 1)
    copies = pass_on(send, 0, blocks, copies)
    to_near.wait_recv()
    total[2] = total[0] + total[1]
    to_side = send(7, total.at[2], total.at[3], 2)
    to_side.wait_recv()
    sums_out[...] = total[2] + total[3]
    settle(copies)
    for k in (1, 2, 3):
        place(k, blocks.at[k], buffer, plan, wholes)
    for out, values in zip(outs, wholes):
        out[...] = values[...].astype(BF)
    to_near.wait_send()
    to_side.wait_send()


def spread(parts, early, late, plan, shapes):
    wide = early.shape[0]
    count = early.shape[1] + late.shape[1]
    return remote_call(
        functools.partial(spread_kernel, plan),
        "spread",
        8,
        [(shape, BF) for shape in shapes] + [((count, LANES), F32)],
        (parts, early, late),
        [pltpu.VMEM((4,) + parts.shape, BF), pltpu.VMEM(parts.shape, F32)]
        + [pltpu.VMEM(shape, F32) for shape in shapes]
        + [
            pltpu.VMEM((4, count, LANES), F32),
            pltpu.VMEM((wide, count, LANES), F32),
            pltpu.VMEM((wide, count, LANES), F32),
            pltpu.SemaphoreType.DMA((8,)),
            pltpu.SemaphoreType.DMA((8,)),
            pltpu.SemaphoreType.DMA((wide,)),
            pltpu.SemaphoreType.DMA((wide,)),
        ],
    )


def finish_kernel(
    mlp_ref, down_ref, stream_ref, first_ref, result_ref, gelu_ref, branch_ref,
    gate_out, up_out, down_out, inputs_out, result_out, gelu_out, branch_out,
):
    hidden = gate_out.shape[1]
    gate_out[...] = mlp_ref[:, :hidden].astype(F32)
    up_out[...] = mlp_ref[:, hidden:].astype(F32)
    down_out[...] = down_ref[...].astype(F32)
    inputs_out[...] = stream_ref[...] + first_ref[...]
    result_out[...] = result_ref[...].astype(BF)
    gelu_out[...] = gelu_ref[...].astype(F32)
    branch_out[...] = branch_ref[...].astype(F32)


def finish(mlp, down, stream_grad, first_back, result, gelu, branch):
    steps = max(1, min(8, mlp.shape[0] // 16))
    half = (mlp.shape[0], mlp.shape[1] // 2)
    operands = (mlp, down, stream_grad, first_back, result, gelu, branch)
    outs = [
        (half, F32), (half, F32), (down.shape, F32), (stream_grad.shape, F32),
        (result.shape, BF), (gelu.shape, F32), (branch.shape, F32),
    ]

    def part(shape):
        return pl.BlockSpec((shape[0] // steps, shape[1]), lambda i: (i, 0))

    return pl.pallas_call(
        finish_kernel,
        grid=(steps,),
        in_specs=[part(v.shape) for v in operands],
        out_specs=[part(shape) for shape, _unused in outs],
        out_shape=[jax.ShapeDtypeStruct(shape, kind) for shape, kind in outs],
        compiler_params=pltpu.CompilerParams(vmem_limit_bytes=60 * 1024 * 1024),
        cost_estimate=pl.CostEstimate(
            flops=8 * result.size, bytes_accessed=24 * 1024 * 1024, transcendentals=0
        ),
        name="finish",
    )(*operands)


def body(
    inputs,
    lengths,
    norm_gain,
    gelu_weight,
    branch_weight,
    forget_gates,
    admit_gates,
    forget_bias,
    admit_bias,
    decay_rate,
    conv_weight,
    conv_bias,
    out_weight,
    mlp_gain,
    gate_weight,
    up_weight,
    down_weight,
    cotangent,
):
    groups = lax.axis_size("seq")
    wide = lax.axis_size("wide")
    s = lax.axis_index("seq")
    w = lax.axis_index("wide")
    seqs, tokens, width = inputs.shape
    rows = seqs * tokens
    total = groups * rows
    all_seqs = groups * seqs
    channels = gelu_weight.shape[1]
    share = channels // groups
    window = (share + BW - 1) // BW * BW
    blocks = window // BW

    def base_of(index):
        return jnp.minimum(index * share // BW * BW, channels - window)

    base = base_of(s)
    off = s * share - base
    quarter = width // groups
    gate_cols = 2 * BW // groups

    flat_low = inputs.reshape(rows, width)
    upstream = cotangent.reshape(rows, width)
    all_low, edge_low = start(flat_low, groups, seqs)
    all_low = all_low.reshape(total, width)
    edge_low = jnp.where(w == 0, 0.0, edge_low.reshape(all_seqs * ROWS16, width).astype(F32))

    x_y_cols = lax.all_gather(
        jnp.concatenate(
            [
                lax.dynamic_slice_in_dim(branch_weight, base, window, 1),
                lax.dynamic_slice_in_dim(gelu_weight, s * share, share, 1),
            ],
            axis=1,
        ),
        "wide",
        axis=0,
        tiled=True,
    )
    dw, rw = width // wide, channels // wide
    small = jnp.concatenate(
        [norm_gain, mlp_gain, forget_bias, admit_bias, decay_rate, conv_bias, conv_weight.reshape(-1)]
    ).reshape(-1, gate_cols)
    gates_quarter = jnp.concatenate([forget_gates, admit_gates], axis=1)
    small = jnp.concatenate(
        [lax.dynamic_slice_in_dim(gates_quarter, s * gate_cols, gate_cols, 1), small], axis=0
    )
    small, edge_low, later_upstream = lax.optimization_barrier((small, edge_low, upstream))
    upstream_near = swap(later_upstream, 1)
    upstream_side = swap(later_upstream, 2)
    small = lax.all_gather(small, "wide")
    gates_quarter = small[:, :rw].reshape(channels, gate_cols)
    small = small[:, rw:].reshape(wide, -1).astype(F32)
    gain_one = small[:, :dw].reshape(1, width)
    gain_two = small[:, dw : 2 * dw].reshape(1, width)
    per_channel = small[:, 2 * dw :].reshape(wide, 8, rw).transpose(1, 0, 2).reshape(8, channels)
    per_channel = lax.dynamic_slice_in_dim(per_channel, s * share, share, 1)

    out_quarter = lax.all_gather(
        lax.dynamic_slice_in_dim(out_weight, s * quarter, quarter, 1), "wide", axis=0, tiled=True
    )
    mlp_full = lax.all_gather(
        jnp.concatenate([gate_weight, up_weight], axis=1), "wide", axis=0, tiled=True
    )
    down_full = lax.all_gather(down_weight, "wide", axis=1, tiled=True)
    hidden_units = gate_weight.shape[1]

    def in_order(parts):
        near = [jnp.where(s % 2 == 1, parts[k ^ 1], parts[k]) for k in range(groups)]
        return [jnp.where(s // 2 == 1, near[k ^ 2], near[k]) for k in range(groups)]

    def swapped(part_of):
        return [swap(part_of(s ^ k), k) if k else part_of(s) for k in range(groups)]

    gates = jnp.concatenate(
        in_order(
            swapped(lambda j: lax.dynamic_slice_in_dim(gates_quarter, base_of(j), window, 0))
        ),
        axis=1,
    )
    normed_all = rms_norm(all_low.astype(F32), gain_one).astype(BF)
    normed_edge = rms_norm(edge_low, gain_one).astype(BF)
    normed_all, upstream_near, upstream_side = lax.optimization_barrier(
        (normed_all, upstream_near, upstream_side)
    )
    half = rows // 2
    upstream_far = [swap(upstream_near[:half], 2), swap(upstream_side[half:], 1)]

    x_y = dot(normed_all, x_y_cols)
    x_win = x_y[:, :window].astype(BF)
    branch_y = x_y[:, window:]
    x_win, out_quarter, *upstream_far = lax.optimization_barrier(
        (x_win, out_quarter, *upstream_far)
    )
    upstream_all = jnp.concatenate([upstream, upstream_near, upstream_side, *upstream_far], axis=0)
    out_rows = jnp.concatenate(
        in_order(swapped(lambda j: lax.dynamic_slice_in_dim(out_quarter, j * share, share, 0))),
        axis=1,
    )
    edge_win = dot(normed_edge, x_y_cols[:, :window]).astype(BF).astype(F32)
    edge_win = edge_win.reshape(all_seqs, ROWS16, window)[:, ROWS16 - HALO :]
    edge_win = edge_win.reshape(all_seqs * HALO, window)
    offset = off.reshape(1)
    forget, admit, conv_out, rate, local, reach, ends = temporal_forward(
        offset, x_win, edge_win, gates, per_channel, tokens
    )
    ends = lax.all_gather(ends, "wide")[:, :, :, 0]
    carry = jnp.zeros((all_seqs, share), F32)
    for j in range(wide - 1):
        carry = jnp.where(j < w, ends[j, :, 0] * carry + ends[j, :, 1], carry)
    carried = local.reshape(all_seqs, tokens, share) + reach.reshape(
        all_seqs, tokens, share
    ) * carry[:, None, :]
    state = carried.astype(BF).astype(F32).reshape(total, share)

    gelu_y = jax.nn.gelu(branch_y)
    mixed_low = (state * gelu_y).astype(BF)
    stream, temporal, normed_two_all = stream_and_norm(mixed_low, out_rows, flat_low, gain_two)
    normed_two_all = normed_two_all.reshape(total, width)

    gate_up = dot(normed_two_all, mlp_full)
    gate, up_values = gate_up[:, :hidden_units], gate_up[:, hidden_units:]
    gelu_gate = jax.nn.gelu(gate)
    hidden_low = (gelu_gate * up_values).astype(BF)
    down_part = contract_rows(hidden_low, upstream_all).astype(BF)
    hidden_low, down_part, upstream_low = lax.optimization_barrier(
        (hidden_low, down_part, upstream_all)
    )
    down_grad = lax.psum_scatter(down_part, "wide", scatter_dimension=1, tiled=True)
    rows_all = mlp_rows(upstream_low, down_full, gate_up)
    mlp_part = contract_rows(normed_two_all, rows_all).astype(BF)
    rows_all, mlp_part = lax.optimization_barrier((rows_all, mlp_part))
    mlp_grad = lax.psum_scatter(mlp_part, "wide", scatter_dimension=0, tiled=True)
    stream_grad, stream_low_all, gain_two_grad, feed_parts, mixed_grad = stream_back(
        rows_all, mlp_full, stream, gain_two, upstream, hidden_low, down_full, out_rows
    )
    mixed_grad = mixed_grad.reshape(total, share)
    gain_two_grad = jnp.sum(gain_two_grad, axis=0)
    stream_low_all = stream_low_all.reshape(total, width)
    mixed_grad, down_grad = lax.optimization_barrier((mixed_grad, down_grad))
    position = w * tokens + jnp.arange(tokens, dtype=jnp.int32)
    valid = (position[None, :] < lengths[:, None]).astype(F32).reshape(rows, 1)
    y_rows, branch_rows, forget_win, admit_win, channel_grads, result, squares = middle(
        mixed_grad, branch_y, local, reach, carry, rate, per_channel, ends[:, :, 0],
        edge_win, gates, valid, feed_parts, conv_out, forget, admit, x_win, stream, temporal,
    )
    partial_sums = jnp.concatenate([jnp.sum(squares, axis=(1, 2)), jnp.sum(valid).reshape(1)])

    bases = tuple(min(j * share // BW * BW, channels - window) for j in range(groups))
    branch_size = dw * window // LANES
    gates_at = branch_size + dw * share // LANES
    stacked_rows = (gates_at + rw + 31) // 32 * 32
    stacked = temporal_grads(
        normed_all, y_rows, branch_rows, x_win, forget_win, admit_win, wide, bases, stacked_rows
    )

    def sum_over_wide(values):
        return lax.psum_scatter(values, "wide", scatter_dimension=0, tiled=True)

    stacked, mlp_grad = lax.optimization_barrier((stacked, mlp_grad))
    channel_all = lax.dynamic_update_slice_in_dim(
        jnp.zeros((8, channels), F32), channel_grads, s * share, 1
    )
    early_sums = jnp.concatenate(
        [
            channel_all.reshape(8, wide, rw).transpose(1, 0, 2).reshape(wide, 8 * rw),
            gain_two_grad.reshape(wide, dw),
            jnp.tile(partial_sums[None, :], (wide, 1)),
        ],
        axis=1,
    )
    early_sums = jnp.pad(early_sums, ((0, 0), (0, -early_sums.shape[1] % (8 * LANES))))
    early_sums = early_sums.reshape(wide, -1, LANES)
    branch_late, early_sums, stacked = lax.optimization_barrier((branch_rows, early_sums, stacked))
    temporal_sum = sum_over_wide(stacked)
    first_back, gain_one_grad, out_cols = inputs_back(
        branch_late, y_rows, x_y_cols, flat_low, gain_one, mixed_low, stream_low_all
    )
    out_sum = sum_over_wide(out_cols)
    late_sums = jnp.sum(gain_one_grad, axis=0).reshape(wide, dw)
    late_sums = jnp.pad(late_sums, ((0, 0), (0, -dw % (8 * LANES)))).reshape(wide, -1, LANES)
    temporal_sum, late_sums = lax.optimization_barrier((temporal_sum, late_sums))

    plan = (
        (0, dw, window // LANES, bases),
        (branch_size, dw, share // LANES, tuple(j * share for j in range(groups))),
        (gates_at, rw, gate_cols // LANES, tuple(j * gate_cols for j in range(groups))),
    )
    branch_whole, gelu_whole, gates_whole, sums = spread(
        temporal_sum[0],
        early_sums,
        late_sums,
        plan,
        ((dw, channels), (dw, channels), (rw, 2 * BW)),
    )
    late_at = early_sums.shape[1]
    gain_one_sum = sums[late_at:].reshape(-1)[:dw]
    sums = sums[:late_at].reshape(-1)
    channel_sums = sums[: 8 * rw].reshape(8, rw)
    gain_two_sum = sums[8 * rw : 8 * rw + dw]
    totals = sums[8 * rw + dw : 8 * rw + dw + 4]
    statistics = jnp.sqrt(totals[0:3] / (totals[3] * width))
    out_sum, gelu_whole = lax.optimization_barrier((out_sum, gelu_whole))
    result, *vectors = lax.optimization_barrier(
        (
            result,
            gain_one_sum,
            gates_whole[:, :BW].astype(F32),
            gates_whole[:, BW:].astype(F32),
            channel_sums[0],
            channel_sums[1],
            channel_sums[2],
            channel_sums[4:8],
            channel_sums[3],
            gain_two_sum,
            statistics,
        )
    )
    gain_one_sum, forget_whole, admit_whole, *channel_out, gain_two_sum, statistics = vectors
    out_whole = jnp.concatenate(in_order(swapped(lambda j: out_sum)), axis=1).astype(F32)
    gate_grad, up_grad, down_grad, inputs_grad, output, gelu_whole, branch_whole = finish(
        mlp_grad, down_grad, stream_grad, first_back, result, gelu_whole, branch_whole
    )
    return (
        output.reshape(seqs, tokens, width),
        inputs_grad.reshape(seqs, tokens, width),
        gain_one_sum,
        gelu_whole,
        branch_whole,
        forget_whole,
        admit_whole,
        *channel_out,
        out_whole,
        gain_two_sum,
        gate_grad,
        up_grad,
        down_grad,
        statistics,
    )


def solution(mesh):
    in_specs = (
        P("seq", "wide", None),
        P("seq"),
        P("wide"),
        P("wide", None),
        P("wide", None),
        P("wide", None),
        P("wide", None),
        P("wide"),
        P("wide"),
        P("wide"),
        P(None, "wide"),
        P("wide"),
        P("wide", None),
        P("wide"),
        P("wide", "seq"),
        P("wide", "seq"),
        P("seq", "wide"),
        P("seq", "wide", None),
    )
    out_specs = (
        P("seq", "wide", None),
        P("seq", "wide", None),
        P("wide"),
        P("wide", None),
        P("wide", None),
        P("wide", None),
        P("wide", None),
        P("wide"),
        P("wide"),
        P("wide"),
        P(None, "wide"),
        P("wide"),
        P("wide", None),
        P("wide"),
        P("wide", "seq"),
        P("wide", "seq"),
        P("seq", "wide"),
        P(),
    )
    return jax.shard_map(body, mesh=mesh, in_specs=in_specs, out_specs=out_specs, check_vma=False)
```

```python
import functools

import jax
import jax.numpy as jnp
from jax import lax
from jax.experimental import pallas as pl
from jax.experimental.pallas import tpu as pltpu
from jax.sharding import PartitionSpec as P

BW = 256
CONV = 4
HALO = 8
BF = jnp.bfloat16
F32 = jnp.float32
LANES = 128
ROWS16 = 16
MESH = pl.DeviceIdType.MESH


def dot(left, right):
    return jnp.dot(left, right, preferred_element_type=F32)


def contract_last(left, right):
    return lax.dot_general(left, right, (((1,), (1,)), ((), ())), preferred_element_type=F32)


def contract_rows(left, right):
    return lax.dot_general(left, right, (((0,), (0,)), ((), ())), preferred_element_type=F32)


def swap(values, mask):
    return lax.ppermute(values, "seq", [(i, i ^ mask) for i in range(lax.axis_size("seq"))])


def inverse_rms(values):
    return lax.rsqrt(jnp.mean(values * values, axis=-1, keepdims=True) + 1e-06)


def rms_norm(values, gain):
    return values * inverse_rms(values) * gain


def sigmoid(values):
    return 0.5 * jnp.tanh(0.5 * values) + 0.5


def gelu_parts(values):
    c = 0.7978845608028654
    sq = values * values
    t = jnp.tanh(c * values * (1.0 + 0.044715 * sq))
    half = 0.5 * (1.0 + t)
    return values * half, half + 0.5 * values * (1.0 - t * t) * (c * (1.0 + 3.0 * 0.044715 * sq))


def drop_of(rate_log):
    u = 2.0 * rate_log
    series = 1.0 + u * (1.0 / 8.0)
    for n in (7, 6, 5, 4, 3, 2):
        series = 1.0 + u * series * (1.0 / n)
    return jnp.where(u > -0.4, -u * series, 1.0 - jnp.exp(u))


def scan_rows(rate, drive, reverse):
    rows, lanes = rate.shape
    count = rows // 8
    rate = rate.reshape(count, 8, lanes)
    drive = drive.reshape(count, 8, lanes)
    row = lax.broadcasted_iota(jnp.int32, (count, 8, lanes), 1)
    for step in (1, 2, 4):
        shift = 8 - step if reverse else step
        keep = row < 8 - step if reverse else row >= step
        drive = drive + rate * jnp.where(keep, pltpu.roll(drive, shift, 1), 0.0)
        rate = rate * jnp.where(keep, pltpu.roll(rate, shift, 1), 1.0)
    state, reach = jnp.zeros((1, lanes), F32), jnp.ones((1, lanes), F32)
    states, reaches = [None] * count, [None] * count
    last = 0 if reverse else 7
    for i in reversed(range(count)) if reverse else range(count):
        states[i] = drive[i] + rate[i] * state
        reaches[i] = rate[i] * reach
        state = states[i][last : last + 1]
        reach = reaches[i][last : last + 1]
    return jnp.concatenate(states, axis=0), jnp.concatenate(reaches, axis=0)


def forward_kernel(
    off_ref, x_ref, edge_ref, gates_ref, chan_ref,
    forget_out, admit_out, conv_out_ref, rate_out, local_out, reach_out, ends_out,
    logits,
):
    q = pl.program_id(0)
    tokens = x_ref.shape[0]
    share = chan_ref.shape[1]
    blocks = x_ref.shape[1] // BW
    off = pl.multiple_of(off_ref[0], LANES)
    for b in range(blocks):
        cols = slice(b * BW, (b + 1) * BW)
        mixed = jnp.dot(x_ref[:, cols], gates_ref[cols, :], preferred_element_type=F32)
        logits[0, :, cols] = mixed[:, :BW]
        logits[1, :, cols] = mixed[:, BW:]
    for j in range(share // LANES):
        lanes = slice(j * LANES, (j + 1) * LANES)
        here = pl.ds(pl.multiple_of(off + j * LANES, LANES), LANES)
        chan = [chan_ref[i : i + 1, lanes] for i in range(8)]
        forget = (logits[0, :, here] + chan[0]).astype(BF)
        admit = (logits[1, :, here] + chan[1]).astype(BF)
        forget_out[:, lanes] = forget
        admit_out[:, lanes] = admit
        edge = edge_ref[pl.ds(pl.multiple_of(q * HALO, HALO), HALO), here]
        padded = jnp.concatenate([edge, x_ref[:, here].astype(F32)], axis=0)
        conv = chan[3] + chan[4] * padded[HALO:]
        for k in range(1, CONV):
            conv = conv + chan[4 + k] * pltpu.roll(padded, k, 0)[HALO:]
        conv_out_ref[:, lanes] = conv
        rate_log = -8.0 * chan[2] * (0.1 + 0.9 * sigmoid(forget.astype(F32)))
        rate = jnp.exp(rate_log)
        drive = jnp.sqrt(drop_of(rate_log)) * sigmoid(admit.astype(F32)) * conv
        state, reach = scan_rows(rate, drive, False)
        rate_out[:, lanes] = rate
        local_out[:, lanes] = state
        reach_out[:, lanes] = reach
        ends_out[0, 0, :, lanes] = reach[tokens - 1 :]
        ends_out[0, 1, :, lanes] = state[tokens - 1 :]


def whole(shape):
    return pl.BlockSpec(shape, lambda q: (0,) * len(shape))


def per_seq(width):
    return pl.BlockSpec((1, 1, width), lambda q: (q, 0, 0))


def temporal_forward(off, x_win, edge, gates, chan, tokens):
    total, window = x_win.shape
    share = chan.shape[1]
    seqs = total // tokens
    part = lambda width: pl.BlockSpec((tokens, width), lambda q: (q, 0))
    return pl.pallas_call(
        forward_kernel,
        grid=(seqs,),
        in_specs=[
            pl.BlockSpec(memory_space=pltpu.SMEM),
            part(window),
            whole(edge.shape),
            whole(gates.shape),
            whole(chan.shape),
        ],
        out_specs=[
            part(share), part(share), part(share), part(share), part(share), part(share),
            pl.BlockSpec((1, 2, 1, share), lambda q: (q, 0, 0, 0)),
        ],
        out_shape=[
            jax.ShapeDtypeStruct((total, share), BF),
            jax.ShapeDtypeStruct((total, share), BF),
            jax.ShapeDtypeStruct((total, share), F32),
            jax.ShapeDtypeStruct((total, share), F32),
            jax.ShapeDtypeStruct((total, share), F32),
            jax.ShapeDtypeStruct((total, share), F32),
            jax.ShapeDtypeStruct((seqs, 2, 1, share), F32),
        ],
        scratch_shapes=[
            pltpu.VMEM((2, tokens, window), F32),
        ],
        compiler_params=pltpu.CompilerParams(vmem_limit_bytes=60 * 1024 * 1024),
        cost_estimate=pl.CostEstimate(flops=1000, bytes_accessed=1000, transcendentals=0),
        name="temporal_forward",
    )(off, x_win, edge, gates, chan)


def partner(mask):
    s = lax.axis_index("seq")
    if mask == 1:
        other = s + 1 - 2 * (s % 2)
    else:
        other = (s + 2) % 4
    return {"seq": other}


def greet():
    barrier = pltpu.get_barrier_semaphore()
    for mask in (1, 2):
        pl.semaphore_signal(barrier, inc=1, device_id=partner(mask), device_id_type=MESH)
    pl.semaphore_wait(barrier, 2)


def sender(sends, recvs):
    def send(slot, source, target, mask):
        copy = pltpu.make_async_remote_copy(
            src_ref=source,
            dst_ref=target,
            send_sem=sends.at[slot],
            recv_sem=recvs.at[slot],
            device_id=partner(mask),
            device_id_type=MESH,
        )
        copy.start()
        return copy

    return send


def over_chunks(rows, run):
    def step(i, carry):
        run(pl.ds(pl.multiple_of(i * ROWS16, ROWS16), ROWS16))
        return carry

    lax.fori_loop(0, rows // ROWS16, step, 0)


def reduce_phase(product, send, first_slot, acc, sent, got):
    rows = acc.shape[1]
    half = rows // 2
    low, high = pl.ds(0, half), pl.ds(half, half)
    product(3, lambda cols, value: sent.__setitem__((0, slice(None), cols), value.astype(BF)))
    far_near = send(first_slot, sent.at[0, low], got.at[0, low], 1)
    far_side = send(first_slot + 1, sent.at[0, high], got.at[0, high], 2)
    product(1, lambda cols, value: acc.__setitem__((1, slice(None), cols), value))
    over_chunks(half, lambda r: sent.__setitem__((1, r), acc[1, r].astype(BF)))
    near_low = send(first_slot + 2, sent.at[1, low], got.at[1, low], 1)
    product(2, lambda cols, value: acc.__setitem__((2, slice(None), cols), value))

    def tail(k):
        def run(r):
            r = pl.ds(pl.multiple_of(r.start + half, ROWS16), ROWS16)
            sent[k, r] = acc[k, r].astype(BF)

        return run

    over_chunks(half, tail(2))
    side_high = send(first_slot + 3, sent.at[2, high], got.at[2, high], 2)
    far_side.wait_recv()

    def add_high(r):
        r = pl.ds(pl.multiple_of(r.start + half, ROWS16), ROWS16)
        sent[1, r] = (acc[1, r] + got[0, r].astype(F32)).astype(BF)

    over_chunks(half, add_high)
    near_high = send(first_slot + 4, sent.at[1, high], got.at[1, high], 1)
    far_near.wait_recv()

    def add_low(r):
        sent[2, r] = (acc[2, r] + got[0, r].astype(F32)).astype(BF)

    over_chunks(half, add_low)
    side_low = send(first_slot + 5, sent.at[2, low], got.at[2, low], 2)
    product(0, lambda cols, value: acc.__setitem__((0, slice(None), cols), value))
    arriving = [near_low, side_high, near_high, side_low]
    for copy in arriving:
        copy.wait_recv()
    return [far_near, far_side] + arriving


def both_ways(send, slot, source, out):
    half = source.shape[0] // 2
    low, high = pl.ds(0, half), pl.ds(half, half)
    return [
        send(slot, source.at[low], out.at[1, low], 1),
        send(slot + 1, source.at[high], out.at[2, high], 2),
        send(slot + 2, source.at[high], out.at[1, high], 1),
        send(slot + 3, source.at[low], out.at[2, low], 2),
    ]


def pass_on(send, slot, out, copies):
    half = out.shape[1] // 2
    low, high = pl.ds(0, half), pl.ds(half, half)
    copies[0].wait_recv()
    far_low = send(slot + 4, out.at[1, low], out.at[3, low], 2)
    copies[1].wait_recv()
    far_high = send(slot + 5, out.at[2, high], out.at[3, high], 1)
    return copies + [far_low, far_high]


def settle(copies):
    for copy in copies[2:]:
        copy.wait_recv()
    for copy in copies:
        copy.wait_send()


def at_seq(k):
    s = lax.axis_index("seq")
    return s if k == 0 else 3 - s if k == 3 else partner(k)["seq"]


def product_of(left, right, contract, rows, tile, ready=None):
    def product(k, store):
        def step(c, carry):
            cols = pl.ds(pl.multiple_of(c * tile, tile), tile)
            if ready is not None and k == 3:
                ready(c)
            total = None
            for a, b in zip(left, right):
                part = b[cols, :] if contract else b[:, cols]
                value = lax.dot_general(
                    a[k * rows : (k + 1) * rows, :],
                    part,
                    (((1,), (1 if contract else 0,)), ((), ())),
                    preferred_element_type=F32,
                )
                total = value if total is None else total + value
            store(cols, total)
            return carry

        width = right[0].shape[0 if contract else 1]
        lax.fori_loop(0, width // tile, step, 0)

    return product


def rms_parts(values):
    return lax.rsqrt(jnp.mean(values * values, axis=-1, keepdims=True) + 1e-06)


def stream_kernel(
    mixed_ref, weight_ref, flat_ref, gain_ref, own_ref,
    near_low_ref, near_high_ref, side_low_ref, side_high_ref, far_low_ref, far_high_ref,
    stream_out, temporal_out, normed_out, joined_out,
    acc, sent, got, sends, recvs,
):
    rows = flat_ref.shape[0]
    greet()
    send = sender(sends, recvs)
    copies = reduce_phase(
        product_of([mixed_ref], [weight_ref], False, rows, 512), send, 0, acc, sent, got
    )

    def finish(r):
        temporal = acc[0, r] + got[1, r].astype(F32) + got[2, r].astype(F32)
        temporal_out[r] = temporal
        stream = flat_ref[r].astype(F32) + temporal
        stream_out[r] = stream
        normed_out[0, r] = (stream * rms_parts(stream) * gain_ref[...]).astype(BF)

    over_chunks(rows, finish)
    gathered = both_ways(send, 6, normed_out.at[0], normed_out)
    joined_out[0] = own_ref[...]
    halves = (near_low_ref, near_high_ref, side_low_ref, side_high_ref, far_low_ref, far_high_ref)
    half = rows // 2
    for i, part in enumerate(halves):
        joined_out[1 + i // 2, (i % 2) * half : (i % 2 + 1) * half, :] = part[...]
    gathered = pass_on(send, 6, normed_out, gathered)
    settle(gathered)
    for copy in copies:
        copy.wait_send()


def exchange_scratch(rows, width, copies):
    return [
        pltpu.VMEM((3, rows, width), F32),
        pltpu.VMEM((3, rows, width), BF),
        pltpu.VMEM((3, rows, width), BF),
        pltpu.SemaphoreType.DMA((copies,)),
        pltpu.SemaphoreType.DMA((copies,)),
    ]


def remote_call(kernel, name, ident, outs, operands, scratch, far=0):
    return pl.pallas_call(
        kernel,
        in_specs=[pl.BlockSpec(memory_space=pltpu.VMEM)] * (len(operands) - far)
        + [pl.BlockSpec(memory_space=pl.ANY)] * far,
        out_specs=[pl.BlockSpec(memory_space=pltpu.VMEM)] * len(outs),
        out_shape=[jax.ShapeDtypeStruct(shape, kind) for shape, kind in outs],
        scratch_shapes=scratch,
        compiler_params=pltpu.CompilerParams(
            collective_id=ident, has_side_effects=True, vmem_limit_bytes=60 * 1024 * 1024
        ),
        cost_estimate=pl.CostEstimate(flops=1000, bytes_accessed=1000, transcendentals=0),
        name=name,
    )(*operands)


def stream_and_norm(mixed, weight, flat, gain, parts):
    rows, width = flat.shape
    groups = mixed.shape[0] // rows
    return remote_call(
        stream_kernel,
        "stream_and_norm",
        1,
        [
            ((rows, width), F32),
            ((rows, width), F32),
            ((groups, rows, width), BF),
            ((groups, rows, width), BF),
        ],
        (mixed, weight, flat, gain, *parts),
        exchange_scratch(rows, width, 12),
    )


def rows_kernel(upstream_ref, down_ref, gate_ref, up_ref, rows_out):
    tile = gate_ref.shape[1]
    hidden = rows_out.shape[1] // 2
    grad = lax.dot_general(
        upstream_ref[...], down_ref[...], (((1,), (1,)), ((), ())), preferred_element_type=F32
    )
    value, slope = gelu_parts(gate_ref[...])
    at = pl.multiple_of(pl.program_id(0) * tile, tile)
    rows_out[:, pl.ds(at, tile)] = (grad * up_ref[...] * slope).astype(BF)
    rows_out[:, pl.ds(hidden + at, tile)] = (grad * value).astype(BF)


def mlp_rows(upstream, down, gate_up):
    total, width = upstream.shape
    hidden = down.shape[0]
    tile = BW
    half = hidden // tile
    return pl.pallas_call(
        rows_kernel,
        grid=(half,),
        in_specs=[
            whole(upstream.shape),
            pl.BlockSpec((tile, width), lambda j: (j, 0)),
            pl.BlockSpec((total, tile), lambda j: (0, j)),
            pl.BlockSpec((total, tile), lambda j: (0, half + j)),
        ],
        out_specs=whole((total, 2 * hidden)),
        out_shape=jax.ShapeDtypeStruct((total, 2 * hidden), BF),
        compiler_params=pltpu.CompilerParams(vmem_limit_bytes=60 * 1024 * 1024),
        cost_estimate=pl.CostEstimate(flops=1000, bytes_accessed=1000, transcendentals=0),
        name="mlp_rows",
    )(upstream, down, gate_up, gate_up)


def stream_back_kernel(
    rows_ref, stream_ref, gain_ref, upstream_ref, weight_far, hidden_far, down_far, out_far,
    grad_out, low_out, gain_out, feed_out, mixed_out,
    weight_ref, hidden_ref, down_ref, out_ref, fetches,
    acc, sent, got, sends, recvs,
):
    rows, width = stream_ref.shape
    tile = 512

    def fetch(c):
        part = pl.ds(pl.multiple_of(c * tile, tile), tile)
        return pltpu.make_async_copy(weight_far.at[part], weight_ref.at[part], fetches.at[c])

    count = width // tile
    for c in range(count):
        fetch(c).start()
    late = [
        pltpu.make_async_copy(hidden_far, hidden_ref, fetches.at[count]),
        pltpu.make_async_copy(down_far, down_ref, fetches.at[count + 1]),
        pltpu.make_async_copy(out_far, out_ref, fetches.at[count + 2]),
    ]
    for copy in late:
        copy.start()
    greet()
    send = sender(sends, recvs)
    product = product_of(
        [rows_ref], [weight_ref], True, rows, tile, ready=lambda c: fetch(c).wait()
    )
    copies = reduce_phase(product, send, 0, acc, sent, got)
    gain_out[...] = jnp.zeros_like(gain_out)

    def finish(r):
        grad = acc[0, r] + got[1, r].astype(F32) + got[2, r].astype(F32)
        stream = stream_ref[r]
        inv = rms_parts(stream)
        scaled = grad * gain_ref[...]
        inner = jnp.mean(stream * scaled, axis=-1, keepdims=True)
        total = upstream_ref[r].astype(F32) + inv * scaled - stream * (inv * inv * inv * inner)
        grad_out[r] = total
        low_out[0, r] = total.astype(BF)
        gained = grad * stream * inv
        gain_out[...] += gained[:8] + gained[8:]

    over_chunks(rows, finish)
    gathered = both_ways(send, 6, low_out.at[0], low_out)
    for copy in late:
        copy.wait()
    feed = product_of([hidden_ref], [down_ref], False, rows, tile)

    def feed_block(k):
        feed(k, lambda cols, value: feed_out.__setitem__((k, slice(None), cols), value.astype(BF)))

    def mixed_block(k):
        mixed_out[k] = lax.dot_general(
            low_out[k], out_ref[...], (((1,), (1,)), ((), ())), preferred_element_type=F32
        )

    feed_block(3)
    gathered = pass_on(send, 6, low_out, gathered)
    feed_block(0)
    mixed_block(0)
    feed_block(1)
    feed_block(2)
    near_low, side_high, near_high, side_low, far_low, far_high = gathered
    near_high.wait_recv()
    mixed_block(1)
    side_low.wait_recv()
    mixed_block(2)
    far_low.wait_recv()
    far_high.wait_recv()
    mixed_block(3)
    for copy in gathered:
        copy.wait_send()
    for copy in copies:
        copy.wait_send()


def stream_back(rows_all, weight, stream, gain, upstream, hidden, down, out_rows):
    rows, width = stream.shape
    groups = rows_all.shape[0] // rows
    return remote_call(
        stream_back_kernel,
        "stream_back",
        2,
        [
            ((rows, width), F32),
            ((groups, rows, width), BF),
            ((8, width), F32),
            ((groups, rows, width), BF),
            ((groups, rows, out_rows.shape[0]), F32),
        ],
        (rows_all, stream, gain, upstream, weight, hidden, down, out_rows),
        [
            pltpu.VMEM(weight.shape, BF),
            pltpu.VMEM(hidden.shape, BF),
            pltpu.VMEM(down.shape, BF),
            pltpu.VMEM(out_rows.shape, BF),
            pltpu.SemaphoreType.DMA((width // 512 + 3,)),
        ]
        + exchange_scratch(rows, width, 12),
        far=4,
    )


def inputs_back_kernel(
    branch_ref, y_ref, flat_ref, gain_ref, weight_far, mixed_far, low_far,
    grad_out, gain_out, columns_out,
    weight_ref, mixed_ref, low_ref, fetches, columns_ref, acc, sent, got, sends, recvs,
):
    rows = flat_ref.shape[0]
    tile = 512
    parts = weight_ref.shape[0] // tile

    def fetch(c):
        part = pl.ds(pl.multiple_of(c * tile, tile), tile)
        return pltpu.make_async_copy(
            weight_far.at[part, : weight_ref.shape[1]], weight_ref.at[part], fetches.at[c]
        )

    for c in range(parts):
        fetch(c).start()
    late = [
        pltpu.make_async_copy(mixed_far, mixed_ref, fetches.at[parts]),
        pltpu.make_async_copy(low_far, low_ref, fetches.at[parts + 1]),
    ]
    for copy in late:
        copy.start()
    s = lax.axis_index("seq")
    count, columns = columns_ref.shape[0], columns_out.shape[1]
    barrier = pltpu.get_barrier_semaphore()
    for k in (1, 2, 3):
        pl.semaphore_signal(barrier, inc=1, device_id={"seq": at_seq(k)}, device_id_type=MESH)
    pl.semaphore_wait(barrier, 3)
    send = sender(sends, recvs)
    here = pl.ds(pl.multiple_of(s * count, ROWS16), count)

    def columns_of(k):
        return columns_ref.at[:, pl.ds(pl.multiple_of(at_seq(k) * columns, LANES), columns)]

    moved = []
    for k in (3, 1, 2):
        copy = pltpu.make_async_remote_copy(
            src_ref=columns_of(k),
            dst_ref=columns_out.at[here],
            send_sem=sends.at[5 + k],
            recv_sem=recvs.at[5 + k],
            device_id={"seq": at_seq(k)},
            device_id_type=MESH,
        )
        moved.append(copy)
    window = branch_ref.shape[1]
    weights = [weight_ref.at[:, :window], weight_ref.at[:, window:]]
    product = product_of(
        [branch_ref, y_ref], weights, True, rows, tile, ready=lambda c: fetch(c).wait()
    )

    def product_and_move(k, store):
        if k == 0:
            for copy in late:
                copy.wait()
            left = mixed_ref[...].T
            for c in range(columns_ref.shape[1] // tile):
                cols = slice(c * tile, (c + 1) * tile)
                columns_ref[:, cols] = jnp.dot(
                    left, low_ref[:, cols], preferred_element_type=F32
                ).astype(BF)
            for copy in moved:
                copy.start()
        product(k, store)

    copies = reduce_phase(product_and_move, send, 0, acc, sent, got)
    columns_out[here] = columns_of(0)[...]
    gain_out[...] = jnp.zeros_like(gain_out)

    def finish(r):
        grad = acc[0, r] + got[1, r].astype(F32) + got[2, r].astype(F32)
        values = flat_ref[r].astype(F32)
        inv = rms_parts(values)
        scaled = grad * gain_ref[...]
        inner = jnp.mean(values * scaled, axis=-1, keepdims=True)
        grad_out[r] = inv * scaled - values * (inv * inv * inv * inner)
        gained = grad * values * inv
        gain_out[...] += gained[:8] + gained[8:]

    over_chunks(rows, finish)
    for copy in moved:
        copy.wait_recv()
    for copy in copies + moved:
        copy.wait_send()


def inputs_back(branch_rows, y_rows, weight, flat, gain, mixed, low):
    rows, width = flat.shape
    count, columns = mixed.shape[1], low.shape[1]
    return remote_call(
        inputs_back_kernel,
        "inputs_back",
        3,
        [((rows, width), F32), ((8, width), F32), ((4 * count, columns // 4), BF)],
        (branch_rows, y_rows, flat, gain, weight, mixed, low),
        [
            pltpu.VMEM((width, branch_rows.shape[1] + y_rows.shape[1]), BF),
            pltpu.VMEM(mixed.shape, BF),
            pltpu.VMEM(low.shape, BF),
            pltpu.SemaphoreType.DMA((width // 512 + 2,)),
            pltpu.VMEM((count, columns), BF),
        ]
        + exchange_scratch(rows, width, 9),
        far=3,
    )


def start_kernel(inputs_ref, inputs_out, edge_out, sends, recvs):
    seqs = edge_out.shape[1] // ROWS16
    tokens = inputs_ref.shape[0] // seqs
    w = lax.axis_index("wide")
    wide = lax.axis_size("wide")
    after, before = lax.rem(w + 1, wide), lax.rem(w + wide - 1, wide)
    barrier = pltpu.get_barrier_semaphore()
    for mask in (1, 2):
        pl.semaphore_signal(barrier, inc=1, device_id=partner(mask), device_id_type=MESH)
    pl.semaphore_signal(barrier, inc=1, device_id={"wide": before}, device_id_type=MESH)
    pl.semaphore_wait(barrier, 3)
    send = sender(sends, recvs)
    edges = []
    for q in range(seqs):
        copy = pltpu.make_async_remote_copy(
            src_ref=inputs_ref.at[pl.ds((q + 1) * tokens - ROWS16, ROWS16)],
            dst_ref=edge_out.at[0, pl.ds(q * ROWS16, ROWS16)],
            send_sem=sends.at[12 + q],
            recv_sem=recvs.at[12 + q],
            device_id={"wide": after},
            device_id_type=MESH,
        )
        copy.start()
        edges.append(copy)
    blocks = both_ways(send, 0, inputs_ref, inputs_out)
    inputs_out[0] = inputs_ref[...]
    for copy in edges:
        copy.wait_recv()
        copy.wait_send()
    edges = both_ways(send, 6, edge_out.at[0], edge_out)
    blocks = pass_on(send, 0, inputs_out, blocks)
    edges = pass_on(send, 6, edge_out, edges)
    settle(blocks)
    settle(edges)


def start(inputs, groups, seqs):
    rows, width = inputs.shape
    copies = 12 + seqs
    return remote_call(
        start_kernel,
        "start",
        6,
        [((groups, rows, width), BF), ((groups, seqs * ROWS16, width), BF)],
        (inputs,),
        [pltpu.SemaphoreType.DMA((copies,)), pltpu.SemaphoreType.DMA((copies,))],
    )


def middle_kernel(
    grad_ref, y_ref, local_ref, reach_ref, carry_ref, rate_ref, chan_ref, ends_ref,
    edge_ref, gates_ref, valid_ref, feed_ref,
    conv_far, forget_far, admit_far, x_far, stream_far, temporal_far,
    y_rows_out, branch_out, forget_out, admit_out, sums_out, result_out, squares_out,
    adjoint, later, heads, packet, packet_in, tails, after, conv_rows,
    conv_ref, forget_ref, admit_ref, x_ref, stream_ref, temporal_ref,
    sent, got, fetches, sends, recvs, head_sends, head_recvs,
):
    wide, seqs, share = ends_ref.shape
    tokens = grad_ref.shape[0] // seqs
    window = x_ref.shape[1]
    rows, width = stream_ref.shape
    half = rows // 2
    low, high = pl.ds(0, half), pl.ds(half, half)
    w = lax.axis_index("wide")
    first_channel = lax.axis_index("seq") * share
    base = jnp.minimum(first_channel // BW * BW, lax.axis_size("seq") * share - window)
    off = pl.multiple_of(first_channel - base, LANES)
    fetched = []
    for i, (far, near) in enumerate(
        (
            (conv_far, conv_ref),
            (forget_far, forget_ref),
            (admit_far, admit_ref),
            (x_far, x_ref),
            (stream_far, stream_ref),
            (temporal_far, temporal_ref),
        )
    ):
        copy = pltpu.make_async_copy(far, near, fetches.at[i])
        copy.start()
        fetched.append(copy)

    barrier = pltpu.get_barrier_semaphore()
    for mask in (1, 2):
        pl.semaphore_signal(barrier, inc=1, device_id=partner(mask), device_id_type=MESH)

    def tell(i, carry):
        other = lax.rem(w + i, wide)
        pl.semaphore_signal(barrier, inc=1, device_id={"wide": other}, device_id_type=MESH)
        return carry

    lax.fori_loop(1, wide, tell, 0)
    pl.semaphore_wait(barrier, wide + 1)
    send = sender(sends, recvs)
    far_near = send(0, feed_ref.at[3, low], got.at[0, low], 1)
    far_side = send(1, feed_ref.at[3, high], got.at[0, high], 2)
    near_low = send(2, feed_ref.at[1, low], got.at[1, low], 1)
    side_high = send(3, feed_ref.at[2, high], got.at[2, high], 2)

    row = lax.broadcasted_iota(jnp.int32, (tokens, LANES), 0)
    fetched[1].wait()
    fetched[2].wait()

    def scan_step(q, carry):
        r = pl.ds(pl.multiple_of(q * tokens, tokens), tokens)
        head_rows = pl.ds(pl.multiple_of(q * tokens, tokens), ROWS16)
        for j in range(share // LANES):
            lanes = slice(j * LANES, (j + 1) * LANES)
            grad = grad_ref[r, lanes]
            value, slope = gelu_parts(y_ref[r, lanes])
            state = (local_ref[r, lanes] + reach_ref[r, lanes] * carry_ref[q, :, lanes]).astype(BF)
            y_rows_out[r, lanes] = (grad * state.astype(F32) * slope).astype(BF)
            state_grad = (grad * value).astype(BF).astype(F32)
            rate = rate_ref[r, lanes]
            ahead = jnp.where(row == tokens - 1, 1.0, pltpu.roll(rate, tokens - 1, 0))
            adjoints, laters = scan_rows(ahead, state_grad, True)
            adjoint[r, lanes] = adjoints
            later[r, lanes] = laters
            tails[q, :, lanes] = rate[:1] * adjoints[:1]
            forget_sig = sigmoid(forget_ref[head_rows, lanes].astype(F32)[:HALO])
            admit_sig = sigmoid(admit_ref[head_rows, lanes].astype(F32)[:HALO])
            rate_log = -8.0 * chan_ref[2:3, lanes] * (0.1 + 0.9 * forget_sig)
            gain = jnp.sqrt(drop_of(rate_log)) * admit_sig
            for i, values in enumerate((adjoints[:HALO] * gain, laters[:HALO] * gain)):
                for t in range(CONV - 1):
                    packet[i, t, q, :, lanes] = values[t : t + 1]
        return carry

    lax.fori_loop(0, seqs, scan_step, 0)
    for q in range(seqs):
        heads[0, q : q + 1, :] = tails[q]

    def head_copy(i):
        return pltpu.make_async_remote_copy(
            src_ref=heads.at[0],
            dst_ref=heads.at[i],
            send_sem=head_sends.at[i],
            recv_sem=head_recvs.at[i],
            device_id={"wide": lax.rem(w + i, wide)},
            device_id_type=MESH,
        )

    def head_start(i, carry):
        head_copy(i).start()
        return carry

    def head_wait(i, carry):
        copy = head_copy(i)
        copy.wait_recv()
        copy.wait_send()
        return carry

    lax.fori_loop(1, wide, head_start, 0)
    packets = pltpu.make_async_remote_copy(
        src_ref=packet,
        dst_ref=packet_in,
        send_sem=sends.at[6],
        recv_sem=recvs.at[6],
        device_id={"wide": lax.rem(w + wide - 1, wide)},
        device_id_type=MESH,
    )
    packets.start()

    far_side.wait_recv()
    sent[0] = (feed_ref[1, high].astype(F32) + got[0, high].astype(F32)).astype(BF)
    near_high = send(4, sent.at[0], got.at[1, high], 1)
    far_near.wait_recv()
    sent[1] = (feed_ref[2, low].astype(F32) + got[0, low].astype(F32)).astype(BF)
    side_low = send(5, sent.at[1], got.at[2, low], 2)

    lax.fori_loop(1, wide, head_wait, 0)
    packets.wait_recv()
    packets.wait_send()

    def tail_step(i, carry):
        tail, next_tail = carry
        j = wide - i
        stepped = ends_ref[j] * tail + heads[lax.rem(w + i, wide)]
        return jnp.where(j > w, stepped, tail), jnp.where(j > w + 1, stepped, next_tail)

    zero = jnp.zeros((seqs, share), F32)
    tail, next_tail = lax.fori_loop(1, wide, tail_step, (zero, zero))
    next_tail = jnp.where(w == wide - 1, 0.0, next_tail)
    inside = jnp.where(w == wide - 1, 0.0, 1.0)
    after[...] = jnp.zeros_like(after)
    for q in range(seqs):
        tails[q] = tail[q : q + 1]
        for t in range(CONV - 1):
            after[q * HALO + t : q * HALO + t + 1, :] = (
                inside * packet_in[0, t, q] + packet_in[1, t, q] * next_tail[q : q + 1]
            )

    forget_out[...] = jnp.zeros_like(forget_out)
    admit_out[...] = jnp.zeros_like(admit_out)
    conv_rows[...] = jnp.zeros_like(conv_rows)
    sums_out[...] = jnp.zeros_like(sums_out)
    fetched[0].wait()
    fetched[3].wait()

    def rows_step(q, carry):
        r = pl.ds(pl.multiple_of(q * tokens, tokens), tokens)
        pack = pl.ds(pl.multiple_of(q * HALO, HALO), HALO)
        for j in range(share // LANES):
            lanes = slice(j * LANES, (j + 1) * LANES)
            here = pl.ds(pl.multiple_of(off + j * LANES, LANES), LANES)
            chan = [chan_ref[i : i + 1, lanes] for i in range(8)]
            start = carry_ref[q, :, lanes]
            carried = local_ref[r, lanes] + reach_ref[r, lanes] * start
            before = jnp.where(row == 0, start, pltpu.roll(carried, 1, 0))
            full = adjoint[r, lanes] + later[r, lanes] * tails[q, :, lanes]
            forget_sig = sigmoid(forget_ref[r, lanes].astype(F32))
            admit_sig = sigmoid(admit_ref[r, lanes].astype(F32))
            span = 0.1 + 0.9 * forget_sig
            rate = rate_ref[r, lanes]
            scale = jnp.sqrt(drop_of(-8.0 * chan[2] * span))
            gated = admit_sig * conv_ref[r, lanes]
            log_grad = full * (rate * before - rate * rate / scale * gated)
            conv_grad = full * scale * admit_sig
            forget_rows = (
                log_grad * (-7.2) * chan[2] * forget_sig * (1.0 - forget_sig)
            ).astype(BF)
            admit_rows = (full * scale * gated * (1.0 - admit_sig)).astype(BF)
            forget_out[r, here] = forget_rows
            admit_out[r, here] = admit_rows
            ahead = jnp.concatenate([conv_grad, after[pack, lanes]], axis=0)
            back = chan[4] * conv_grad
            for k in range(1, CONV):
                back = back + chan[4 + k] * pltpu.roll(ahead, tokens + HALO - k, 0)[:tokens]
            conv_rows[:, here] = back.astype(BF).astype(F32)
            padded = jnp.concatenate(
                [edge_ref[pack, here], x_ref[r, here].astype(F32)], axis=0
            )
            sums = [
                forget_rows.astype(F32),
                admit_rows.astype(F32),
                log_grad * (-8.0) * span,
                conv_grad,
                conv_grad * padded[HALO:],
            ] + [conv_grad * pltpu.roll(padded, k, 0)[HALO:] for k in range(1, CONV)]
            sums_out[:, lanes] += jnp.concatenate(
                [jnp.sum(v, axis=0, keepdims=True) for v in sums], axis=0
            )
        for b in range(window // BW):
            cols = slice(b * BW, (b + 1) * BW)
            back = conv_rows[:, cols]
            for source, at in ((forget_out, 0), (admit_out, BW)):
                back = back + lax.dot_general(
                    source[r, cols],
                    gates_ref[cols, at : at + BW],
                    (((1,), (1,)), ((), ())),
                    preferred_element_type=F32,
                )
            branch_out[r, cols] = back.astype(BF)
        return carry

    lax.fori_loop(0, seqs, rows_step, 0)
    fetched[4].wait()
    fetched[5].wait()
    for copy in (near_low, side_high, near_high, side_low):
        copy.wait_recv()
    squares_out[...] = jnp.zeros_like(squares_out)

    def finish(r):
        feed = feed_ref[0, r].astype(F32) + got[1, r].astype(F32) + got[2, r].astype(F32)
        result = stream_ref[r] + feed
        result_out[r] = result
        valid = valid_ref[r]
        for i, values in enumerate((result, temporal_ref[r], feed)):
            square = valid * values * values
            squares_out[i] += square[:8] + square[8:]

    over_chunks(rows, finish)
    for copy in (far_near, far_side, near_low, side_high, near_high, side_low):
        copy.wait_send()


def middle(
    grad, y, local, reach, carry, rate, chan, ends, edge, gates, valid, feed,
    conv, forget, admit, x_win, stream, temporal,
):
    total, share = grad.shape
    window = x_win.shape[1]
    rows, width = stream.shape
    wide, seqs = ends.shape[:2]
    tokens = total // seqs
    vmem = pl.BlockSpec(memory_space=pltpu.VMEM)
    anywhere = pl.BlockSpec(memory_space=pl.ANY)
    outs = [
        ((total, share), BF),
        ((total, window), BF),
        ((total, window), BF),
        ((total, window), BF),
        ((8, share), F32),
        ((rows, width), F32),
        ((3, 8, width), F32),
    ]
    return pl.pallas_call(
        middle_kernel,
        in_specs=[vmem] * 12 + [anywhere] * 6,
        out_specs=[vmem] * len(outs),
        out_shape=[jax.ShapeDtypeStruct(shape, kind) for shape, kind in outs],
        scratch_shapes=[
            pltpu.VMEM((total, share), F32),
            pltpu.VMEM((total, share), F32),
            pltpu.VMEM((wide, seqs, share), F32),
            pltpu.VMEM((2, CONV - 1, seqs, 1, share), F32),
            pltpu.VMEM((2, CONV - 1, seqs, 1, share), F32),
            pltpu.VMEM((seqs, 1, share), F32),
            pltpu.VMEM((seqs * HALO, share), F32),
            pltpu.VMEM((tokens, window), F32),
            pltpu.VMEM((total, share), F32),
            pltpu.VMEM((total, share), BF),
            pltpu.VMEM((total, share), BF),
            pltpu.VMEM((total, window), BF),
            pltpu.VMEM((rows, width), F32),
            pltpu.VMEM((rows, width), F32),
            pltpu.VMEM((2, rows // 2, width), BF),
            pltpu.VMEM((3, rows, width), BF),
            pltpu.SemaphoreType.DMA((6,)),
            pltpu.SemaphoreType.DMA((7,)),
            pltpu.SemaphoreType.DMA((7,)),
            pltpu.SemaphoreType.DMA((wide,)),
            pltpu.SemaphoreType.DMA((wide,)),
        ],
        compiler_params=pltpu.CompilerParams(
            collective_id=7, has_side_effects=True, vmem_limit_bytes=60 * 1024 * 1024
        ),
        cost_estimate=pl.CostEstimate(flops=1000, bytes_accessed=1000, transcendentals=0),
        name="middle",
    )(
        grad, y, local, reach, carry[:, None, :], rate, chan, ends, edge, gates, valid, feed,
        conv, forget, admit, x_win, stream, temporal,
    )


def grads_kernel(
    bases, normed_ref, y_ref, branch_ref, x_ref, forget_ref, admit_ref,
    stacked_out,
    gates, blocks, gate_total, sends, recvs,
):
    step = pl.program_id(0)
    wide, stacked_rows, quarter = stacked_out.shape
    window = x_ref.shape[1]
    tiles = (window + y_ref.shape[1]) // LANES
    group = wide // pl.num_programs(0)
    part = normed_ref.shape[1] // group
    room = stacked_rows - tiles * part
    share = gate_total.shape[0] // wide

    def quarter_of(k):
        return pl.ds(pl.multiple_of(at_seq(k) * quarter, LANES), quarter)

    def exchange(k):
        return pltpu.make_async_remote_copy(
            src_ref=gates.at[:, quarter_of(k)],
            dst_ref=blocks.at[k],
            send_sem=sends.at[k],
            recv_sem=recvs.at[k],
            device_id={"seq": at_seq(k)},
            device_id_type=MESH,
        )

    @pl.when(step == 0)
    def _():
        barrier = pltpu.get_barrier_semaphore()
        for k in (1, 2, 3):
            pl.semaphore_signal(barrier, inc=1, device_id={"seq": at_seq(k)}, device_id_type=MESH)
        for b in range(window // BW):
            cols = slice(b * BW, (b + 1) * BW)
            block = x_ref[:, cols].T
            for source, at in ((forget_ref, 0), (admit_ref, BW)):
                gates[cols, at : at + BW] = jnp.dot(
                    block, source[:, cols], preferred_element_type=F32
                ).astype(BF)
        pl.semaphore_wait(barrier, 3)
        for k in (3, 1, 2):
            exchange(k).start()

    left = normed_ref[...].T
    first = 0
    for right in (branch_ref, y_ref):
        sums = jnp.dot(left, right[...], preferred_element_type=F32).astype(BF)
        count = right.shape[1] // LANES
        for g in range(group):
            for i in range(count):
                at = (first + i) * part
                stacked_out[step * group + g, at : at + part, :] = sums[
                    g * part : (g + 1) * part, i * LANES : (i + 1) * LANES
                ]
        first += count

    @pl.when(step == pl.num_programs(0) - 1)
    def _():
        gate_total[...] = jnp.zeros_like(gate_total)
        for k in range(4):
            if k:
                exchange(k).wait_recv()
            other = at_seq(k)
            base = other * 0
            for j, start_row in enumerate(bases):
                base = jnp.where(other == j, start_row, base)
            at = pl.ds(pl.multiple_of(base, 8), window)
            value = blocks[k] if k else gates[:, quarter_of(0)]
            gate_total[at, :] += value.astype(F32)
        for g in range(wide):
            value = gate_total[g * share : (g + 1) * share, :]
            if room > share:
                value = jnp.concatenate([value, jnp.zeros((room - share, quarter), F32)], axis=0)
            stacked_out[g, tiles * part :, :] = value.astype(BF)
        for k in (1, 2, 3):
            exchange(k).wait_send()


def temporal_grads(normed, y_rows, branch_rows, x_win, forget_win, admit_win, wide, bases, stacked_rows):
    total, width = normed.shape
    share, window = y_rows.shape[1], x_win.shape[1]
    quarter = 2 * BW // 4
    return pl.pallas_call(
        functools.partial(grads_kernel, bases),
        grid=(width // BW,),
        in_specs=[pl.BlockSpec((total, BW), lambda i: (0, i))]
        + [whole(v.shape) for v in (y_rows, branch_rows, x_win, forget_win, admit_win)],
        out_specs=whole((wide, stacked_rows, quarter)),
        out_shape=jax.ShapeDtypeStruct((wide, stacked_rows, quarter), BF),
        scratch_shapes=[
            pltpu.VMEM((window, 2 * BW), BF),
            pltpu.VMEM((4, window, quarter), BF),
            pltpu.VMEM((4 * share, quarter), F32),
            pltpu.SemaphoreType.DMA((4,)),
            pltpu.SemaphoreType.DMA((4,)),
        ],
        compiler_params=pltpu.CompilerParams(
            collective_id=9, has_side_effects=True, vmem_limit_bytes=60 * 1024 * 1024
        ),
        cost_estimate=pl.CostEstimate(flops=1000, bytes_accessed=1000, transcendentals=0),
        name="temporal_grads",
    )(normed, y_rows, branch_rows, x_win, forget_win, admit_win)


def place(k, block, buffer, plan, outs):
    buffer[...] = block[...].astype(F32)
    other = at_seq(k)
    for (first, count, tiles, starts), out in zip(plan, outs):
        base = other * 0
        for j, start_col in enumerate(starts):
            base = jnp.where(other == j, start_col, base)
        for i in range(tiles):
            cols = pl.ds(pl.multiple_of(base + i * LANES, LANES), LANES)
            out[:, cols] += buffer[first + i * count : first + (i + 1) * count, :]


def spread_kernel(plan, parts_ref, early_ref, late_ref, *refs):
    outs, refs = refs[: len(plan)], refs[len(plan) :]
    sums_out, blocks, buffer, *refs = refs
    wholes, refs = refs[: len(plan)], refs[len(plan) :]
    total, sums_ref, got_sums, sends, recvs, sum_sends, sum_recvs = refs
    wide = sums_ref.shape[0]
    early = early_ref.shape[1]
    sums_ref[:, :early] = early_ref[...]
    sums_ref[:, early:] = late_ref[...]
    w = lax.axis_index("wide")
    barrier = pltpu.get_barrier_semaphore()
    for mask in (1, 2):
        pl.semaphore_signal(barrier, inc=1, device_id=partner(mask), device_id_type=MESH)

    def tell(i, carry):
        other = lax.rem(w + i, wide)
        pl.semaphore_signal(barrier, inc=1, device_id={"wide": other}, device_id_type=MESH)
        return carry

    lax.fori_loop(1, wide, tell, 0)
    pl.semaphore_wait(barrier, wide + 1)
    send = sender(sends, recvs)

    def chunk(i):
        other = lax.rem(w + i, wide)
        return pltpu.make_async_remote_copy(
            src_ref=sums_ref.at[other],
            dst_ref=got_sums.at[i],
            send_sem=sum_sends.at[i],
            recv_sem=sum_recvs.at[i],
            device_id={"wide": other},
            device_id_type=MESH,
        )

    def begin(i, carry):
        chunk(i).start()
        return carry

    def finish(i, carry):
        copy = chunk(i)
        copy.wait_recv()
        copy.wait_send()
        return carry + got_sums[i]

    lax.fori_loop(1, wide, begin, 0)
    copies = both_ways(send, 0, parts_ref, blocks)
    for out in wholes:
        out[...] = jnp.zeros_like(out)
    place(0, parts_ref, buffer, plan, wholes)
    total[0] = lax.fori_loop(1, wide, finish, sums_ref[w])
    to_near = send(6, total.at[0], total.at[1], 1)
    copies = pass_on(send, 0, blocks, copies)
    to_near.wait_recv()
    total[2] = total[0] + total[1]
    to_side = send(7, total.at[2], total.at[3], 2)
    to_side.wait_recv()
    sums_out[...] = total[2] + total[3]
    settle(copies)
    for k in (1, 2, 3):
        place(k, blocks.at[k], buffer, plan, wholes)
    for out, values in zip(outs, wholes):
        out[...] = values[...].astype(BF)
    to_near.wait_send()
    to_side.wait_send()


def spread(parts, early, late, plan, shapes):
    wide = early.shape[0]
    count = early.shape[1] + late.shape[1]
    return remote_call(
        functools.partial(spread_kernel, plan),
        "spread",
        8,
        [(shape, BF) for shape in shapes] + [((count, LANES), F32)],
        (parts, early, late),
        [pltpu.VMEM((4,) + parts.shape, BF), pltpu.VMEM(parts.shape, F32)]
        + [pltpu.VMEM(shape, F32) for shape in shapes]
        + [
            pltpu.VMEM((4, count, LANES), F32),
            pltpu.VMEM((wide, count, LANES), F32),
            pltpu.VMEM((wide, count, LANES), F32),
            pltpu.SemaphoreType.DMA((8,)),
            pltpu.SemaphoreType.DMA((8,)),
            pltpu.SemaphoreType.DMA((wide,)),
            pltpu.SemaphoreType.DMA((wide,)),
        ],
    )


def finish_kernel(
    mlp_ref, down_ref, stream_ref, first_ref, result_ref, gelu_ref, branch_ref,
    gate_out, up_out, down_out, inputs_out, result_out, gelu_out, branch_out,
):
    hidden = gate_out.shape[1]
    gate_out[...] = mlp_ref[:, :hidden].astype(F32)
    up_out[...] = mlp_ref[:, hidden:].astype(F32)
    down_out[...] = down_ref[...].astype(F32)
    inputs_out[...] = stream_ref[...] + first_ref[...]
    result_out[...] = result_ref[...].astype(BF)
    gelu_out[...] = gelu_ref[...].astype(F32)
    branch_out[...] = branch_ref[...].astype(F32)


def finish(mlp, down, stream_grad, first_back, result, gelu, branch):
    steps = max(1, min(8, mlp.shape[0] // 16))
    half = (mlp.shape[0], mlp.shape[1] // 2)
    operands = (mlp, down, stream_grad, first_back, result, gelu, branch)
    outs = [
        (half, F32), (half, F32), (down.shape, F32), (stream_grad.shape, F32),
        (result.shape, BF), (gelu.shape, F32), (branch.shape, F32),
    ]

    def part(shape):
        return pl.BlockSpec((shape[0] // steps, shape[1]), lambda i: (i, 0))

    return pl.pallas_call(
        finish_kernel,
        grid=(steps,),
        in_specs=[part(v.shape) for v in operands],
        out_specs=[part(shape) for shape, _unused in outs],
        out_shape=[jax.ShapeDtypeStruct(shape, kind) for shape, kind in outs],
        compiler_params=pltpu.CompilerParams(vmem_limit_bytes=60 * 1024 * 1024),
        cost_estimate=pl.CostEstimate(
            flops=8 * result.size, bytes_accessed=24 * 1024 * 1024, transcendentals=0
        ),
        name="finish",
    )(*operands)


def body(
    inputs,
    lengths,
    norm_gain,
    gelu_weight,
    branch_weight,
    forget_gates,
    admit_gates,
    forget_bias,
    admit_bias,
    decay_rate,
    conv_weight,
    conv_bias,
    out_weight,
    mlp_gain,
    gate_weight,
    up_weight,
    down_weight,
    cotangent,
):
    groups = lax.axis_size("seq")
    wide = lax.axis_size("wide")
    s = lax.axis_index("seq")
    w = lax.axis_index("wide")
    seqs, tokens, width = inputs.shape
    rows = seqs * tokens
    total = groups * rows
    all_seqs = groups * seqs
    channels = gelu_weight.shape[1]
    share = channels // groups
    window = (share + BW - 1) // BW * BW
    blocks = window // BW

    def base_of(index):
        return jnp.minimum(index * share // BW * BW, channels - window)

    base = base_of(s)
    off = s * share - base
    quarter = width // groups
    gate_cols = 2 * BW // groups

    flat_low = inputs.reshape(rows, width)
    upstream = cotangent.reshape(rows, width)
    all_low, edge_low = start(flat_low, groups, seqs)
    all_low = all_low.reshape(total, width)
    edge_low = jnp.where(w == 0, 0.0, edge_low.reshape(all_seqs * ROWS16, width).astype(F32))

    dw, rw = width // wide, channels // wide
    out_part = lax.dynamic_slice_in_dim(out_weight, s * quarter, quarter, 1)
    rest = rw - dw
    rest_part = out_part[dw:]
    temporal_cols = lax.all_gather(
        jnp.concatenate(
            [
                lax.dynamic_slice_in_dim(branch_weight, base, window, 1),
                lax.dynamic_slice_in_dim(gelu_weight, s * share, share, 1),
                out_part[:dw],
                jnp.concatenate(
                    [rest_part[:, i : i + LANES] for i in range(0, quarter, LANES)], axis=0
                ),
            ],
            axis=1,
        ),
        "wide",
        axis=0,
        tiled=True,
    )
    out_body = temporal_cols[:, window + share : window + share + quarter]
    out_rest = temporal_cols[:, window + share + quarter :]
    out_rest = out_rest.reshape(wide, quarter // LANES, rest, LANES).transpose(0, 2, 1, 3)
    out_quarter = jnp.concatenate(
        [out_body.reshape(wide, dw, quarter), out_rest.reshape(wide, rest, quarter)], axis=1
    ).reshape(channels, quarter)
    small = jnp.concatenate(
        [norm_gain, mlp_gain, forget_bias, admit_bias, decay_rate, conv_bias, conv_weight.reshape(-1)]
    ).reshape(-1, gate_cols)
    gates_quarter = jnp.concatenate([forget_gates, admit_gates], axis=1)
    small = jnp.concatenate(
        [lax.dynamic_slice_in_dim(gates_quarter, s * gate_cols, gate_cols, 1), small], axis=0
    )
    small, edge_low, later_upstream = lax.optimization_barrier((small, edge_low, upstream))
    half = rows // 2
    upstream_near = [swap(later_upstream[:half], 1), swap(later_upstream[half:], 1)]
    upstream_side = [swap(later_upstream[:half], 2), swap(later_upstream[half:], 2)]
    small = lax.all_gather(small, "wide")
    gates_quarter = small[:, :rw].reshape(channels, gate_cols)
    small = small[:, rw:].reshape(wide, -1).astype(F32)
    gain_one = small[:, :dw].reshape(1, width)
    gain_two = small[:, dw : 2 * dw].reshape(1, width)
    per_channel = small[:, 2 * dw :].reshape(wide, 8, rw).transpose(1, 0, 2).reshape(8, channels)
    per_channel = lax.dynamic_slice_in_dim(per_channel, s * share, share, 1)

    mlp_full = lax.all_gather(
        jnp.concatenate([gate_weight, up_weight], axis=1), "wide", axis=0, tiled=True
    )
    down_full = lax.all_gather(down_weight, "wide", axis=1, tiled=True)
    hidden_units = gate_weight.shape[1]

    def in_order(parts):
        near = [jnp.where(s % 2 == 1, parts[k ^ 1], parts[k]) for k in range(groups)]
        return [jnp.where(s // 2 == 1, near[k ^ 2], near[k]) for k in range(groups)]

    def swapped(part_of):
        return [swap(part_of(s ^ k), k) if k else part_of(s) for k in range(groups)]

    gates = jnp.concatenate(
        in_order(
            swapped(lambda j: lax.dynamic_slice_in_dim(gates_quarter, base_of(j), window, 0))
        ),
        axis=1,
    )
    normed_all = rms_norm(all_low.astype(F32), gain_one).astype(BF)
    normed_edge = rms_norm(edge_low, gain_one).astype(BF)

    x_y = dot(normed_all, temporal_cols[:, : window + share])
    x_win = x_y[:, :window].astype(BF)
    branch_y = x_y[:, window:]
    x_win, out_quarter, *upstream_parts = lax.optimization_barrier(
        (x_win, out_quarter, *upstream_near, *upstream_side)
    )
    upstream_parts += [swap(upstream_parts[0], 2), swap(upstream_parts[3], 1)]
    out_rows = jnp.concatenate(
        in_order(swapped(lambda j: lax.dynamic_slice_in_dim(out_quarter, j * share, share, 0))),
        axis=1,
    )
    edge_win = dot(normed_edge, temporal_cols[:, :window]).astype(BF).astype(F32)
    edge_win = edge_win.reshape(all_seqs, ROWS16, window)[:, ROWS16 - HALO :]
    edge_win = edge_win.reshape(all_seqs * HALO, window)
    offset = off.reshape(1)
    forget, admit, conv_out, rate, local, reach, ends = temporal_forward(
        offset, x_win, edge_win, gates, per_channel, tokens
    )
    ends = lax.all_gather(ends, "wide")[:, :, :, 0]
    ends, *upstream_parts = lax.optimization_barrier((ends, *upstream_parts))
    carry = jnp.zeros((all_seqs, share), F32)
    for j in range(wide - 1):
        carry = jnp.where(j < w, ends[j, :, 0] * carry + ends[j, :, 1], carry)
    carried = local.reshape(all_seqs, tokens, share) + reach.reshape(
        all_seqs, tokens, share
    ) * carry[:, None, :]
    state = carried.astype(BF).astype(F32).reshape(total, share)

    gelu_y = jax.nn.gelu(branch_y)
    mixed_low = (state * gelu_y).astype(BF)
    stream, temporal, normed_two_all, upstream_all = stream_and_norm(
        mixed_low, out_rows, flat_low, gain_two, [upstream, *upstream_parts]
    )
    upstream_all = upstream_all.reshape(total, width)
    normed_two_all = normed_two_all.reshape(total, width)

    gate_up = dot(normed_two_all, mlp_full)
    gate, up_values = gate_up[:, :hidden_units], gate_up[:, hidden_units:]
    gelu_gate = jax.nn.gelu(gate)
    hidden_low = (gelu_gate * up_values).astype(BF)
    down_part = contract_rows(hidden_low, upstream_all).astype(BF)
    hidden_low, down_part, upstream_low = lax.optimization_barrier(
        (hidden_low, down_part, upstream_all)
    )
    down_grad = lax.psum_scatter(down_part, "wide", scatter_dimension=1, tiled=True)
    rows_all = mlp_rows(upstream_low, down_full, gate_up)
    mlp_part = contract_rows(normed_two_all, rows_all).astype(BF)
    rows_all, mlp_part = lax.optimization_barrier((rows_all, mlp_part))
    mlp_grad = lax.psum_scatter(mlp_part, "wide", scatter_dimension=0, tiled=True)
    stream_grad, stream_low_all, gain_two_grad, feed_parts, mixed_grad = stream_back(
        rows_all, mlp_full, stream, gain_two, upstream, hidden_low, down_full, out_rows
    )
    mixed_grad = mixed_grad.reshape(total, share)
    gain_two_grad = jnp.sum(gain_two_grad, axis=0)
    stream_low_all = stream_low_all.reshape(total, width)
    mixed_grad, down_grad = lax.optimization_barrier((mixed_grad, down_grad))
    position = w * tokens + jnp.arange(tokens, dtype=jnp.int32)
    valid = (position[None, :] < lengths[:, None]).astype(F32).reshape(rows, 1)
    y_rows, branch_rows, forget_win, admit_win, channel_grads, result, squares = middle(
        mixed_grad, branch_y, local, reach, carry, rate, per_channel, ends[:, :, 0],
        edge_win, gates, valid, feed_parts, conv_out, forget, admit, x_win, stream, temporal,
    )
    partial_sums = jnp.concatenate([jnp.sum(squares, axis=(1, 2)), jnp.sum(valid).reshape(1)])

    bases = tuple(min(j * share // BW * BW, channels - window) for j in range(groups))
    branch_size = dw * window // LANES
    gates_at = branch_size + dw * share // LANES
    stacked_rows = (gates_at + rw + 31) // 32 * 32
    stacked = temporal_grads(
        normed_all, y_rows, branch_rows, x_win, forget_win, admit_win, wide, bases, stacked_rows
    )

    def sum_over_wide(values):
        return lax.psum_scatter(values, "wide", scatter_dimension=0, tiled=True)

    stacked, mlp_grad = lax.optimization_barrier((stacked, mlp_grad))
    channel_all = lax.dynamic_update_slice_in_dim(
        jnp.zeros((8, channels), F32), channel_grads, s * share, 1
    )
    early_sums = jnp.concatenate(
        [
            channel_all.reshape(8, wide, rw).transpose(1, 0, 2).reshape(wide, 8 * rw),
            gain_two_grad.reshape(wide, dw),
            jnp.tile(partial_sums[None, :], (wide, 1)),
        ],
        axis=1,
    )
    early_sums = jnp.pad(early_sums, ((0, 0), (0, -early_sums.shape[1] % (8 * LANES))))
    early_sums = early_sums.reshape(wide, -1, LANES)
    branch_late, early_sums, stacked = lax.optimization_barrier((branch_rows, early_sums, stacked))
    temporal_sum = sum_over_wide(stacked)
    first_back, gain_one_grad, out_cols = inputs_back(
        branch_late, y_rows, temporal_cols, flat_low, gain_one, mixed_low, stream_low_all
    )
    out_sum = sum_over_wide(out_cols)
    late_sums = jnp.sum(gain_one_grad, axis=0).reshape(wide, dw)
    late_sums = jnp.pad(late_sums, ((0, 0), (0, -dw % (8 * LANES)))).reshape(wide, -1, LANES)
    temporal_sum, late_sums = lax.optimization_barrier((temporal_sum, late_sums))

    plan = (
        (0, dw, window // LANES, bases),
        (branch_size, dw, share // LANES, tuple(j * share for j in range(groups))),
        (gates_at, rw, gate_cols // LANES, tuple(j * gate_cols for j in range(groups))),
    )
    branch_whole, gelu_whole, gates_whole, sums = spread(
        temporal_sum[0],
        early_sums,
        late_sums,
        plan,
        ((dw, channels), (dw, channels), (rw, 2 * BW)),
    )
    late_at = early_sums.shape[1]
    gain_one_sum = sums[late_at:].reshape(-1)[:dw]
    sums = sums[:late_at].reshape(-1)
    channel_sums = sums[: 8 * rw].reshape(8, rw)
    gain_two_sum = sums[8 * rw : 8 * rw + dw]
    totals = sums[8 * rw + dw : 8 * rw + dw + 4]
    statistics = jnp.sqrt(totals[0:3] / (totals[3] * width))
    out_sum, gelu_whole = lax.optimization_barrier((out_sum, gelu_whole))
    result, *vectors = lax.optimization_barrier(
        (
            result,
            gain_one_sum,
            gates_whole[:, :BW].astype(F32),
            gates_whole[:, BW:].astype(F32),
            channel_sums[0],
            channel_sums[1],
            channel_sums[2],
            channel_sums[4:8],
            channel_sums[3],
            gain_two_sum,
            statistics,
        )
    )
    gain_one_sum, forget_whole, admit_whole, *channel_out, gain_two_sum, statistics = vectors
    out_whole = jnp.concatenate(in_order(swapped(lambda j: out_sum)), axis=1).astype(F32)
    gate_grad, up_grad, down_grad, inputs_grad, output, gelu_whole, branch_whole = finish(
        mlp_grad, down_grad, stream_grad, first_back, result, gelu_whole, branch_whole
    )
    return (
        output.reshape(seqs, tokens, width),
        inputs_grad.reshape(seqs, tokens, width),
        gain_one_sum,
        gelu_whole,
        branch_whole,
        forget_whole,
        admit_whole,
        *channel_out,
        out_whole,
        gain_two_sum,
        gate_grad,
        up_grad,
        down_grad,
        statistics,
    )


def solution(mesh):
    in_specs = (
        P("seq", "wide", None),
        P("seq"),
        P("wide"),
        P("wide", None),
        P("wide", None),
        P("wide", None),
        P("wide", None),
        P("wide"),
        P("wide"),
        P("wide"),
        P(None, "wide"),
        P("wide"),
        P("wide", None),
        P("wide"),
        P("wide", "seq"),
        P("wide", "seq"),
        P("seq", "wide"),
        P("seq", "wide", None),
    )
    out_specs = (
        P("seq", "wide", None),
        P("seq", "wide", None),
        P("wide"),
        P("wide", None),
        P("wide", None),
        P("wide", None),
        P("wide", None),
        P("wide"),
        P("wide"),
        P("wide"),
        P(None, "wide"),
        P("wide"),
        P("wide", None),
        P("wide"),
        P("wide", "seq"),
        P("wide", "seq"),
        P("seq", "wide"),
        P(),
    )
    return jax.shard_map(body, mesh=mesh, in_specs=in_specs, out_specs=out_specs, check_vma=False)
```
